128 devices in a mesh: row: 16 (over z, y), col: 8 (over x, core).
Axes of the slice: x: 4, y: 4, z: 4, core: 2. Of those that a mesh axis runs over, the one named last changes fastest.
Arguments:
- forcing: float32 [2, 512, 16384], P(None, 'col', 'row'), may hold values from -170 to 170
- medium_index: int32 [512, 16384], P('col', 'row'), may hold values from 0 to 7
- absorbing_mask: int32 [512, 16384], P('col', 'row'), may hold values 0 or 1
- source_rows: int32 [16], replicated, may hold values from 0 to 511
- source_cols: int32 [16], replicated, may hold values from 0 to 16383
- refraction: float32 [8], replicated, may hold values from 0.6 to 1.8
- lift_weight: float32 [4, 64], replicated, may hold values from -3 to 3
- lift_bias: float32 [64], replicated, may hold values from -3 to 3
- spectral_weight: bfloat16 [2, 256, 64, 64], replicated, may hold values from -1.5 to 1.5
- point_weight: bfloat16 [64, 64], replicated, may hold values from -0.75 to 0.75
- layer_bias: float32 [64], replicated, may hold values from -3 to 3
- project_weight: bfloat16 [64, 2], replicated, may hold values from -0.75 to 0.75
Outputs:
- solution: float32 [2, 512, 16384], P(None, 'col', 'row')
- residual: float32 [2, 512, 16384], P(None, 'col', 'row')
The draws below stay inside these ranges and needn't reach their ends.
All inputs are finite; a program needn't handle non-finite values. No bound on the sum of `absorbing_mask` on one device may be relied on, other than what follows from the above.
Results may differ from the reference program's by a relative error of at most 0.015.
Values sent between devices are 32-bit elements; how exact they have to be, the bound alone decides.
A program may use at most 192 MiB of HBM per device.

```python
import math
import jax
import jax.numpy as jnp
from jax import lax

NY = 16384
K = 256
C = 64
LEVELS = 8
NSRC = 16
NX = 512


def draw_forcing(key, part):
    key = jax.random.fold_in(key, 11)
    base_key = jax.random.fold_in(key, 0)
    line_pos = jnp.arange(NX, dtype=jnp.float32) / NX
    column_pos = jnp.arange(NY, dtype=jnp.float32) / NY
    envelope = jnp.exp(math.log(3.0) * line_pos)[:, None] * jnp.exp(math.log(3.0) * column_pos)[None, :]
    base = jax.random.truncated_normal(base_key, -4.0, 4.0, (2, NX, NY), jnp.float32)
    return base * envelope[None]


def plant(drawn, own_key, low, largest):
    longest = drawn.shape.index(max(drawn.shape))
    spots = []
    for shift in (0, 1):
        where = [jax.random.randint(jax.random.fold_in(own_key, axis), (), 0, length) for axis, length in enumerate(drawn.shape)]
        where[longest] = (where[longest] + shift) % drawn.shape[longest]
        spots.append(tuple(where))
    return drawn.at[spots[0]].set(low).at[spots[1]].set(largest)


def bell_draw(key, extent, deviation, reach, kind=jnp.bfloat16):
    return jnp.clip(deviation * jax.random.normal(key, extent, jnp.float32), -reach, reach).astype(kind)


def setup_inputs(seed: int = 0) -> dict:
    streams_of = jax.random.split(jax.random.key(seed), 13)
    return {
        "forcing": draw_forcing(jax.random.fold_in(streams_of[12], 71), 0),
        "medium_index": plant(jax.random.randint(streams_of[1], (NX, NY), 0, LEVELS), jax.random.fold_in(streams_of[1], 1), 0, LEVELS - 1).astype(jnp.int32),
        "absorbing_mask": plant((jax.random.randint(streams_of[2], (NX, NY), 0, 4) < 1).astype(jnp.int32), jax.random.fold_in(streams_of[2], 1), 0, 1),
        "source_rows": plant(jax.random.randint(streams_of[3], (NSRC,), 0, NX), jax.random.fold_in(streams_of[3], 1), 0, NX - 1).astype(jnp.int32),
        "source_cols": plant(jax.random.randint(streams_of[4], (NSRC,), 0, NY), jax.random.fold_in(streams_of[4], 1), 0, NY - 1).astype(jnp.int32),
        "refraction": jnp.clip(jnp.exp(jax.random.uniform(streams_of[5], (LEVELS,), jnp.float32, math.log(0.6), math.log(1.8))), 0.6, 1.8),
        "lift_weight": bell_draw(streams_of[6], (4, C), 4 ** -0.5, 3.0, jnp.float32),
        "lift_bias": bell_draw(streams_of[7], (C,), 0.5, 3.0, jnp.float32),
        "spectral_weight": bell_draw(streams_of[8], (2, K, C, C), (C // 4) ** -0.5, 1.5),
        "point_weight": bell_draw(streams_of[9], (C, C), C ** -0.5, 0.75),
        "layer_bias": bell_draw(streams_of[10], (C,), 0.5, 3.0, jnp.float32),
        "project_weight": bell_draw(streams_of[11], (C, 2), C ** -0.5, 0.75),
    }


wave_base = 0.23
source_gain = 8.0
norm_eps = 1e-06

def forward_table(first_row, row_count, kept_modes, grid_length):
    positions = first_row + jnp.arange(row_count, dtype=jnp.int32)
    mode_index = jnp.arange(kept_modes, dtype=jnp.int32)
    phases = positions[:, None] * mode_index[None, :] % grid_length
    angles = phases.astype(jnp.float32) * jnp.float32(2.0 * math.pi / grid_length)
    factor = jnp.float32(1.0 / math.sqrt(grid_length))
    return jnp.concatenate([jnp.cos(angles) * factor, -jnp.sin(angles) * factor], axis=1)

def inverse_table(first_row, row_count, kept_modes, grid_length):
    positions = first_row + jnp.arange(row_count, dtype=jnp.int32)
    mode_index = jnp.arange(kept_modes, dtype=jnp.int32)
    phases = mode_index[:, None] * positions[None, :] % grid_length
    angles = phases.astype(jnp.float32) * jnp.float32(2.0 * math.pi / grid_length)
    factor = jnp.where(mode_index == 0, 1.0, 2.0).astype(jnp.float32) * jnp.float32(1.0 / math.sqrt(grid_length))
    return jnp.concatenate([jnp.cos(angles) * factor[:, None], -jnp.sin(angles) * factor[:, None]], axis=0).astype(jnp.bfloat16)

def transform(fields, table):
    line_count = fields.shape[1]
    result = jnp.dot(fields.reshape(2 * line_count, fields.shape[2]), table, precision=lax.Precision.HIGHEST)
    return result.reshape(2, line_count, table.shape[1]).transpose(1, 0, 2)

def lift_modes(all_modes, lift_weight, lift_bias, grid_length):
    line_count = all_modes.shape[0]
    kept_modes = all_modes.shape[2] // 2
    channels = all_modes.reshape(line_count, 4, 2, kept_modes).transpose(0, 3, 2, 1)
    lifted = channels[..., 0:1] * lift_weight[0] + channels[..., 1:2] * lift_weight[1] + channels[..., 2:3] * lift_weight[2] + channels[..., 3:4] * lift_weight[3]
    mode_index = jnp.arange(kept_modes, dtype=jnp.int32)[:, None, None]
    plane_index = jnp.arange(2, dtype=jnp.int32)[None, :, None]
    at_anchor = ((mode_index == 0) & (plane_index == 0)).astype(lifted.dtype)
    lifted = lifted + at_anchor * (lift_bias * jnp.float32(math.sqrt(grid_length)))
    return lifted.reshape(line_count, kept_modes, 2 * lift_bias.shape[0]).astype(jnp.bfloat16)

def mode_weights(spectral_weight):
    real_part = spectral_weight[0]
    imag_part = spectral_weight[1]
    upper = jnp.concatenate([real_part, imag_part], axis=2)
    lower_half = jnp.concatenate([-imag_part, real_part], axis=2)
    return jnp.concatenate([upper, lower_half], axis=1)

def layer_block(fields, mode_mix, back_table, weights):
    lift_weight, lift_bias, point_weight, layer_bias, project_weight = weights
    line_count, kept_modes, double_width = mode_mix.shape
    channel_width = double_width // 2
    spectra = mode_mix.reshape(line_count, kept_modes, 2, channel_width).transpose(0, 3, 2, 1)
    spectra = spectra.reshape(line_count, channel_width, 2 * kept_modes)
    spectral = jnp.einsum('lcm,my->lcy', spectra.astype(jnp.float32), back_table.astype(jnp.float32), precision=lax.Precision.HIGHEST)
    lifted_field = (lift_weight[0][None, :, None] * fields[0][:, None, :] + lift_weight[1][None, :, None] * fields[1][:, None, :] + lift_weight[2][None, :, None] * fields[2][:, None, :] + lift_weight[3][None, :, None] * fields[3][:, None, :] + lift_bias[None, :, None]).astype(jnp.bfloat16)
    pointwise = jnp.einsum('cd,lcy->ldy', point_weight.astype(jnp.float32), lifted_field.astype(jnp.float32), precision=lax.Precision.HIGHEST)
    activation = jax.nn.gelu(pointwise + spectral + layer_bias[None, :, None], approximate=False).astype(jnp.bfloat16)
    return jnp.einsum('cg,lcy->gly', project_weight.astype(jnp.float32), activation.astype(jnp.float32), precision=lax.Precision.HIGHEST)

def run_layer(fields, mode_mix, back_table, weights):
    line_count = fields.shape[1]
    grid_length = fields.shape[2]
    channel_width = mode_mix.shape[2] // 2
    block_size = math.gcd(line_count, max(1, 2 ** 21 // (channel_width * grid_length)))
    block_count = line_count // block_size
    stacked_fields = fields.reshape(4, block_count, block_size, grid_length).transpose(1, 0, 2, 3)
    stacked_modes = mode_mix.reshape(block_count, block_size, mode_mix.shape[1], mode_mix.shape[2])

    def one_block(inputs):
        return layer_block(inputs[0], inputs[1], back_table, weights)
    result = lax.map(one_block, (stacked_fields, stacked_modes))
    return result.transpose(1, 0, 2, 3).reshape(2, line_count, grid_length)

def apply_operator(padded, grid_field, wave_factor, damping):
    edge_sum = padded[:, 2:, 1:-1] + padded[:, :-2, 1:-1] + padded[:, 1:-1, 2:] + padded[:, 1:-1, :-2]
    corner = padded[:, 2:, 2:] + padded[:, 2:, :-2] + padded[:, :-2, 2:] + padded[:, :-2, :-2]
    laplace = (4.0 * edge_sum + corner - 20.0 * grid_field) / 6.0
    real_plane = -laplace[0] - wave_factor * (grid_field[0] + damping * grid_field[1])
    imag_plane = -laplace[1] - wave_factor * (grid_field[1] - damping * grid_field[0])
    return jnp.stack([real_plane, imag_plane])

def inner_pair(first_field, second_field):
    real_sum = jnp.sum(first_field[0] * second_field[0] + first_field[1] * second_field[1])
    imag_sum = jnp.sum(first_field[0] * second_field[1] - first_field[1] * second_field[0])
    return (real_sum, imag_sum)

def complex_scale(real_part, imag_part, grid_field):
    return jnp.stack([real_part * grid_field[0] - imag_part * grid_field[1], real_part * grid_field[1] + imag_part * grid_field[0]])

def small_solve(initial_norm, top_left, lower_left, top_right, middle_right, lower_right):
    a_re, a_im = top_left
    b_re, b_im = top_right
    d_re, d_im = middle_right
    c_val = lower_left
    e_val = lower_right
    gram_first = a_re * a_re + a_im * a_im + c_val * c_val
    gram_second = b_re * b_re + b_im * b_im + d_re * d_re + d_im * d_im + e_val * e_val
    cross_re = a_re * b_re + a_im * b_im + c_val * d_re
    cross_im = a_re * b_im - a_im * b_re + c_val * d_im
    minor_re = a_re * d_re - a_im * d_im - b_re * c_val
    minor_im = a_re * d_im + a_im * d_re - b_im * c_val
    determinant = minor_re * minor_re + minor_im * minor_im + (a_re * a_re + a_im * a_im) * e_val * e_val + c_val * c_val * e_val * e_val
    first_re = initial_norm * a_re
    first_im = -initial_norm * a_im
    second_re = initial_norm * b_re
    second_im = -initial_norm * b_im
    coef0_re = (gram_second * first_re - (cross_re * second_re - cross_im * second_im)) / determinant
    coef0_im = (gram_second * first_im - (cross_re * second_im + cross_im * second_re)) / determinant
    coef1_re = (gram_first * second_re - (cross_re * first_re + cross_im * first_im)) / determinant
    coef1_im = (gram_first * second_im - (cross_re * first_im - cross_im * first_re)) / determinant
    rest0_re = initial_norm - (a_re * coef0_re - a_im * coef0_im + b_re * coef1_re - b_im * coef1_im)
    rest0_im = -(a_re * coef0_im + a_im * coef0_re + b_re * coef1_im + b_im * coef1_re)
    rest1_re = -(c_val * coef0_re + d_re * coef1_re - d_im * coef1_im)
    rest1_im = -(c_val * coef0_im + d_re * coef1_im + d_im * coef1_re)
    rest2_re = -e_val * coef1_re
    rest2_im = -e_val * coef1_im
    return ((coef0_re, coef0_im), (coef1_re, coef1_im), (rest0_re, rest0_im), (rest1_re, rest1_im), (rest2_re, rest2_im))

def reference(forcing, medium_index, absorbing_mask, source_rows, source_cols, refraction, lift_weight, lift_bias, spectral_weight, point_weight, layer_bias, project_weight):
    source_count = jnp.zeros((NX, NY), jnp.float32).at[source_rows, source_cols].add(1.0)
    right_side = jnp.stack([forcing[0] + source_gain * source_count, forcing[1]])
    refractive = refraction[medium_index]
    damping = 0.1 + absorbing_mask.astype(jnp.float32)
    wave_factor = wave_base * refractive * (wave_base * refractive)
    features = jnp.stack([refractive, damping])
    forward = forward_table(0, NY, K, NY)
    back_table = inverse_table(0, NY, K, NY)
    feature_modes = transform(features, forward)
    big_weights = mode_weights(spectral_weight)
    grid_scale = jnp.float32(math.sqrt(NX * NY))
    weights = (lift_weight, lift_bias, point_weight, layer_bias, project_weight)

    def precondition(vector):
        scaled = vector * grid_scale
        all_modes = jnp.concatenate([transform(scaled, forward), feature_modes], axis=1)
        lifted = lift_modes(all_modes, lift_weight, lift_bias, NY)
        mode_mix = jnp.einsum('lkc,kcd->lkd', lifted.astype(jnp.float32), big_weights.astype(jnp.float32), precision=lax.Precision.HIGHEST).astype(jnp.bfloat16)
        return run_layer(jnp.concatenate([scaled, features], axis=0), mode_mix, back_table, weights)

    def operate(grid_field):
        padded = jnp.pad(grid_field, ((0, 0), (1, 1), (1, 1)))
        return apply_operator(padded, grid_field, wave_factor, damping)
    initial_norm = jnp.sqrt(jnp.sum(right_side * right_side) + norm_eps)
    krylov_basis = [right_side / initial_norm]
    corrections = []
    products_all = []
    subdiagonals = []
    for column in range(2):
        correction = precondition(krylov_basis[column])
        corrections.append(correction)
        applied = operate(correction)
        products = [inner_pair(krylov_basis[earlier], applied) for earlier in range(column + 1)]
        for earlier in range(column + 1):
            applied = applied - complex_scale(products[earlier][0], products[earlier][1], krylov_basis[earlier])
        subdiagonal = jnp.sqrt(jnp.sum(applied * applied) + norm_eps)
        krylov_basis.append(applied / subdiagonal)
        products_all.append(products)
        subdiagonals.append(subdiagonal)
    coef0, coef1, rest0, rest1, rest2 = small_solve(initial_norm, products_all[0][0], subdiagonals[0], products_all[1][0], products_all[1][1], subdiagonals[1])
    solution = complex_scale(coef0[0], coef0[1], corrections[0]) + complex_scale(coef1[0], coef1[1], corrections[1])
    residual = complex_scale(rest0[0], rest0[1], krylov_basis[0]) + complex_scale(rest1[0], rest1[1], krylov_basis[1]) + complex_scale(rest2[0], rest2[1], krylov_basis[2])
    return (solution, residual)
```

```python
import functools
import math

import jax
import jax.numpy as jnp
import numpy as np
import ml_dtypes
from jax import lax
from jax.experimental import pallas as pl
from jax.experimental.pallas import tpu as pltpu
from jax.sharding import PartitionSpec as P

K = 256

wave_base = 0.23
source_gain = 8.0
norm_eps = 1e-06

MESH = pl.DeviceIdType.MESH
F32 = jnp.float32
BF16 = jnp.bfloat16
LINES = 16
SLABS = 16
PIECE = 256


def base_tables(tile_cols, kept_modes, grid_cols):
    positions = np.arange(tile_cols, dtype=np.int64)
    mode_index = np.arange(kept_modes, dtype=np.int64)
    angles = (positions[:, None] * mode_index[None, :] % grid_cols) * (2.0 * math.pi / grid_cols)
    scale = 1.0 / math.sqrt(grid_cols)
    table = np.concatenate([np.cos(angles), -np.sin(angles)], axis=1) * scale
    high = table.astype(np.float32).astype(ml_dtypes.bfloat16)
    low = (table - high.astype(np.float64)).astype(np.float32).astype(ml_dtypes.bfloat16)
    return high, low, np.ascontiguousarray(high.T)


def phase_table(row_count, kept_modes):
    tile = np.arange(row_count, dtype=np.int64)
    mode_index = np.arange(kept_modes, dtype=np.int64)
    angles = (tile[:, None] * mode_index[None, :] % row_count) * (2.0 * math.pi / row_count)
    table = np.concatenate([np.cos(angles), np.sin(angles)], axis=1).astype(np.float32)
    return np.ascontiguousarray(np.broadcast_to(table[:, None, :], (row_count, 8, 2 * kept_modes)))


def split(x):
    high = x.astype(BF16)
    return high, (x - high.astype(F32)).astype(BF16)


def gelu(x):
    return 0.5 * x * (1.0 + lax.erf(x * math.sqrt(0.5)))


def cmul(a, b):
    return a[0] * b[0] - a[1] * b[1], a[0] * b[1] + a[1] * b[0]


def conj_cmul(a, b):
    return a[0] * b[0] + a[1] * b[1], a[0] * b[1] - a[1] * b[0]


def small_solve(beta, a, b, c, d, e):
    gram_first = a[0] * a[0] + a[1] * a[1] + c * c
    gram_second = b[0] * b[0] + b[1] * b[1] + d[0] * d[0] + d[1] * d[1] + e * e
    cross = conj_cmul(a, b)
    cross = (cross[0] + c * d[0], cross[1] + c * d[1])
    ad = cmul(a, d)
    minor = (ad[0] - b[0] * c, ad[1] - b[1] * c)
    determinant = (
        minor[0] * minor[0]
        + minor[1] * minor[1]
        + (a[0] * a[0] + a[1] * a[1]) * e * e
        + c * c * e * e
    )
    first = (beta * a[0], -beta * a[1])
    second = (beta * b[0], -beta * b[1])
    t = cmul(cross, second)
    y0 = ((gram_second * first[0] - t[0]) / determinant, (gram_second * first[1] - t[1]) / determinant)
    t = conj_cmul(cross, first)
    y1 = ((gram_first * second[0] - t[0]) / determinant, (gram_first * second[1] - t[1]) / determinant)
    return y0, y1


def kernel(
    row_count,
    col_count,
    kept,
    forcing,
    medium,
    mask,
    source_rows,
    source_cols,
    refraction,
    mode_map,
    point_map,
    project_map,
    table_high,
    table_low,
    table_back,
    phases,
    solution_ref,
    residual_ref,
    fwd_high,
    fwd_low,
    phase,
    wave_ref,
    damp_ref,
    right_ref,
    rhs_cols,
    mixed,
    fixed,
    modes,
    high,
    low,
    send_feat,
    got_feat,
    all_feat,
    send_wave,
    got_wave,
    all_wave,
    got_scal,
    col_scal,
    ext,
    applied,
    basis,
    table_sems,
    halo_send,
    halo_recv,
    send_sems,
    recv_sems,
):
    lines, columns = mask.shape
    channels = mode_map.shape[2]
    groups = lines // LINES
    double = 2 * kept
    row = lax.axis_index("row")
    col = lax.axis_index("col")
    grid_scale = math.sqrt(lines * col_count * columns * row_count)

    table_copies = [
        pltpu.make_async_copy(table_high, fwd_high, table_sems.at[0]),
        pltpu.make_async_copy(table_low, fwd_low, table_sems.at[1]),
        pltpu.make_async_copy(phases.at[row], phase, table_sems.at[2]),
    ]
    back_copies = [
        pltpu.make_async_copy(table_back, rhs_cols.at[g, pl.ds(0, double)], table_sems.at[3 + g])
        for g in range(groups)
    ]
    for copy in table_copies + back_copies:
        copy.start()

    barrier = pltpu.get_barrier_semaphore()
    greeted = 0
    for d in range(1, row_count):
        pl.semaphore_signal(
            barrier, inc=1, device_id={"row": lax.rem(row + d, row_count)}, device_id_type=MESH
        )
        greeted += 1
    for d in range(1, col_count):
        pl.semaphore_signal(
            barrier, inc=1, device_id={"col": lax.rem(col + d, col_count)}, device_id_type=MESH
        )
        greeted += 1
    for dr in (1, row_count - 1):
        for dc in (1, col_count - 1):
            pl.semaphore_signal(
                barrier,
                inc=1,
                device_id={
                    "row": lax.rem(row + dr, row_count),
                    "col": lax.rem(col + dc, col_count),
                },
                device_id_type=MESH,
            )
            greeted += 1

    def spread(source, target, index, axis, me, count):
        for d in range(1, count):
            there = lax.rem(me + d, count)
            pltpu.make_async_remote_copy(
                src_ref=source(there),
                dst_ref=target.at[me],
                send_sem=send_sems.at[index],
                recv_sem=recv_sems.at[index],
                device_id={axis: there},
                device_id_type=MESH,
            ).start()

    def arrived(target, index, count, sems):
        whole = target.at[pl.ds(0, count - 1)]
        pltpu.make_async_copy(whole, whole, sems.at[index]).wait()

    def forward(out):
        spectrum = (
            jnp.dot(high[...], fwd_high[...], preferred_element_type=F32)
            + jnp.dot(high[...], fwd_low[...], preferred_element_type=F32)
            + jnp.dot(low[...], fwd_high[...], preferred_element_type=F32)
        )
        cosine, sine = phase[0:1, :kept], phase[0:1, kept:]
        re, im = spectrum[:, :kept], spectrum[:, kept:]
        out[:, :, 0:kept] = (re * cosine + im * sine).reshape(row_count, 8, kept)
        out[:, :, kept:double] = (im * cosine - re * sine).reshape(row_count, 8, kept)

    def unrotated(both):
        cosine, sine = phase[0:1, :kept], phase[0:1, kept:]
        re, im = both[:, :kept], both[:, kept:]
        return re * cosine - im * sine, im * cosine + re * sine

    def slab(g, j, value):
        rhs_cols[g, double + LINES * j : double + LINES * (j + 1), :] = value

    def field_slabs(g, j, value):
        top, rest = split(value)
        slab(g, j, top)
        slab(g, j + 1, rest)
        slab(g, j + 2, top)
        return top, rest

    def rows_of(g):
        return slice(LINES * g, LINES * (g + 1))

    def folded(x):
        total = jnp.zeros((8, 128), F32)
        for i in range(x.shape[0] // 8):
            for j in range(x.shape[1] // 128):
                total = total + x[8 * i : 8 * i + 8, 128 * j : 128 * j + 128]
        return total

    def scalar_tile(parts):
        place = lax.broadcasted_iota(jnp.int32, (8, 128), 0)
        tile = jnp.zeros((8, 128), F32)
        for i, part in enumerate(parts):
            tile = jnp.where(place == i, jnp.sum(part, axis=0, keepdims=True), tile)
        return tile

    for g in range(groups):
        lines_of = rows_of(g)
        kind = medium[lines_of, :]
        refractive = jnp.zeros((LINES, columns), F32)
        for level in range(refraction.shape[0]):
            refractive = jnp.where(kind == level, refraction[level], refractive)
        damping = 0.1 + mask[lines_of, :].astype(F32)
        damp_ref[lines_of, :] = damping
        scaled = wave_base * refractive
        wave_ref[lines_of, :] = scaled * scaled
        top, rest = field_slabs(g, 6, refractive)
        high[lines_of, :] = top
        low[lines_of, :] = rest
        top, rest = field_slabs(g, 9, damping)
        high[lines + LINES * g : lines + LINES * (g + 1), :] = top
        low[lines + LINES * g : lines + LINES * (g + 1), :] = rest
        ones = jnp.ones((LINES, columns), BF16)
        slab(g, 12, ones)
        slab(g, 13, ones)
        slab(g, 14, jnp.zeros_like(ones))
        slab(g, 15, jnp.zeros_like(ones))
    for copy in table_copies:
        copy.wait()
    forward(send_feat)
    pl.semaphore_wait(barrier, greeted)
    spread(lambda there: send_feat.at[there], got_feat, 0, "row", row, row_count)

    col_hits = (
        source_cols[...]
        == columns * row + lax.broadcasted_iota(jnp.int32, (source_cols.shape[0], columns), 1)
    ).astype(F32).astype(BF16)
    line_hits = (
        source_rows[...]
        == lines * col + lax.broadcasted_iota(jnp.int32, (lines, source_rows.shape[1]), 0)
    ).astype(F32).astype(BF16)
    source_count = jnp.dot(line_hits, col_hits, preferred_element_type=F32)
    square = jnp.zeros((8, 128), F32)
    for g in range(groups):
        lines_of = rows_of(g)
        for p in range(2):
            field = forcing[p, lines_of, :]
            if p == 0:
                field = field + source_gain * source_count[lines_of, :]
            right_ref[p, lines_of, :] = field
            square = square + folded(field * field)
            top, rest = split(field)
            high[p * lines + LINES * g : p * lines + LINES * (g + 1), :] = top
            low[p * lines + LINES * g : p * lines + LINES * (g + 1), :] = rest
    def send_modes(step, tile):
        forward(send_wave.at[step])
        for r in range(row_count):
            send_wave[step, r, :, double:] = tile
        spread(
            lambda there: send_wave.at[step, there], got_wave.at[step], 2 + 3 * step, "row", row, row_count
        )

    send_modes(0, scalar_tile([square]))

    for line in range(lines):
        i = line % LINES
        mixed[line, :, double:] = point_map[channels * i : channels * (i + 1), :]

    def reduced(got, source):
        got[row] = source[row]
        total = got[0]
        for r in range(1, row_count):
            total = total + got[r]
        return total

    arrived(got_feat, 0, row_count, recv_sems)
    all_feat[row] = reduced(got_feat, send_feat)
    spread(lambda there: all_feat.at[row], all_feat, 1, "row", row, row_count)

    def wave_reduce(step):
        index = 2 + 3 * step
        arrived(got_wave.at[step], index, row_count, recv_sems)
        total = reduced(got_wave.at[step], send_wave.at[step])
        all_wave[step, row] = total[:, :double]
        spread(
            lambda there: all_wave.at[step, row], all_wave.at[step], index + 1, "row", row, row_count
        )
        col_scal[step, col] = total[:, double:]
        spread(
            lambda there: col_scal.at[step, col], col_scal.at[step], index + 2, "col", col, col_count
        )

    def col_total(step):
        arrived(col_scal.at[step], 4 + 3 * step, col_count, recv_sems)
        total = col_scal[step, 0]
        for r in range(1, col_count):
            total = total + col_scal[step, r]
        return jnp.sum(total, axis=1, keepdims=True)

    def mix(channels_in, bias, source, store):
        for kc in range(kept // 128):
            low_k, high_k = pl.ds(128 * kc, 128), pl.ds(kept + 128 * kc, 128)
            for ob in range(channels // 16):
                outs = pl.ds(16 * ob, 16)
                maps = [
                    (mode_map[0, g, outs, low_k], mode_map[1, g, outs, low_k]) for g in channels_in
                ]
                start = (mode_map[0, 4, outs, low_k], mode_map[1, 4, outs, low_k]) if bias else None

                def eight_lines(block, carry):
                    first = pl.multiple_of(8 * block, 8)
                    parts = [
                        (modes[g, pl.ds(first, 8), low_k], modes[g, pl.ds(first, 8), high_k])
                        for g in channels_in
                    ]
                    for i in range(8):
                        line = first + i
                        if bias:
                            re, im = start
                        else:
                            re, im = source[line, outs, low_k], source[line, outs, high_k]
                        for (mode_re, mode_im), (map_re, map_im) in zip(parts, maps):
                            one_re, one_im = mode_re[i : i + 1], mode_im[i : i + 1]
                            re = re + (map_re * one_re - map_im * one_im)
                            im = im + (map_re * one_im + map_im * one_re)
                        store[line, outs, low_k] = re.astype(store.dtype)
                        store[line, outs, high_k] = im.astype(store.dtype)
                    return carry

                lax.fori_loop(0, lines // 8, eight_lines, 0)

    def layer(step):
        def one_group(g, carry):
            left = mixed[pl.ds(LINES * g, LINES)].reshape(LINES * channels, double + SLABS * LINES)
            first = pl.multiple_of(8 + LINES * g, 8)
            for n in range(columns // PIECE):
                piece = slice(PIECE * n, PIECE * (n + 1))
                x = jnp.dot(left, rhs_cols[g, :, piece], preferred_element_type=F32)
                active = gelu(x).astype(BF16)
                out = jnp.dot(project_map[...], active, preferred_element_type=F32)
                place = slice(128 + PIECE * n, 128 + PIECE * (n + 1))
                ext[step, 0, pl.ds(first, LINES), place] = out[:LINES]
                ext[step, 1, pl.ds(first, LINES), place] = out[LINES:]
            return carry

        lax.fori_loop(0, groups, one_group, 0)

    def halos(step):
        tall, wide = pl.ds(8, lines), pl.ds(128, columns)
        line_ends = {1: (pl.ds(lines, 8), pl.ds(0, 8)), -1: (pl.ds(8, 8), pl.ds(8 + lines, 8)), 0: (tall, tall)}
        col_ends = {
            1: (pl.ds(columns, 128), pl.ds(0, 128)),
            -1: (pl.ds(128, 128), pl.ds(128 + columns, 128)),
            0: (wide, wide),
        }
        copies = []
        for i, (dr, dc) in enumerate(
            [(1, 0), (-1, 0), (0, 1), (0, -1), (1, 1), (1, -1), (-1, 1), (-1, -1)]
        ):
            here_l, there_l = line_ends[dc]
            here_c, there_c = col_ends[dr]
            copies.append(
                pltpu.make_async_remote_copy(
                    src_ref=ext.at[step, :, here_l, here_c],
                    dst_ref=ext.at[step, :, there_l, there_c],
                    send_sem=halo_send.at[step, i],
                    recv_sem=halo_recv.at[step, i],
                    device_id={
                        "row": lax.rem(row + dr + row_count, row_count),
                        "col": lax.rem(col + dc + col_count, col_count),
                    },
                    device_id_type=MESH,
                )
            )
        for copy in copies:
            copy.start()
        for copy in copies:
            copy.wait()
        view = ext.at[step]

        @pl.when(row == 0)
        def _():
            view[:, :, 0:128] = jnp.zeros((2, lines + 16, 128), F32)

        @pl.when(row == row_count - 1)
        def _():
            view[:, :, 128 + columns :] = jnp.zeros((2, lines + 16, 128), F32)

        @pl.when(col == 0)
        def _():
            view[:, 0:8, :] = jnp.zeros((2, 8, columns + 256), F32)

        @pl.when(col == col_count - 1)
        def _():
            view[:, 8 + lines :, :] = jnp.zeros((2, 8, columns + 256), F32)

    def operate(step, g):
        laps, fields = [], []
        for p in range(2):
            first = 8 + LINES * g
            beside = (
                ext[step, p, first - 1 : first - 1 + LINES, :]
                + ext[step, p, first + 1 : first + 1 + LINES, :]
            )
            centre = ext[step, p, first : first + LINES, :]
            both = 4.0 * centre + beside
            width = columns + 256
            around = pltpu.roll(both, 1, 1) + pltpu.roll(both, width - 1, 1)
            total = (4.0 * beside - 20.0 * centre + around) * (1.0 / 6.0)
            laps.append(total[:, 128 : 128 + columns])
            fields.append(centre[:, 128 : 128 + columns])
        wave, damping = wave_ref[rows_of(g), :], damp_ref[rows_of(g), :]
        real = -laps[0] - wave * (fields[0] + damping * fields[1])
        imag = -laps[1] - wave * (fields[1] - damping * fields[0])
        return real, imag

    def pair(first, second):
        return (
            folded(first[0] * second[0] + first[1] * second[1]),
            folded(first[0] * second[1] - first[1] * second[0]),
        )

    def add(a, b):
        return [x + y for x, y in zip(a, b)]

    wave_reduce(0)
    arrived(all_feat, 1, row_count, recv_sems)
    re, im = unrotated(all_feat[...].reshape(2 * lines, double))
    for g in range(2):
        modes[2 + g, :, :kept] = re[g * lines : (g + 1) * lines]
        modes[2 + g, :, kept:] = im[g * lines : (g + 1) * lines]
    mix((2, 3), True, None, fixed)
    for copy in back_copies:
        copy.wait()

    arrived(all_wave.at[0], 3, row_count, recv_sems)
    total_square = col_total(0)[0:1, :]
    beta = jnp.sqrt(total_square + norm_eps)
    inverse_beta = 1.0 / beta
    re, im = unrotated(all_wave[0].reshape(2 * lines, double))
    for p in range(2):
        modes[p, :, :kept] = re[p * lines : (p + 1) * lines] * (grid_scale * inverse_beta)
        modes[p, :, kept:] = im[p * lines : (p + 1) * lines] * (grid_scale * inverse_beta)
    for g in range(groups):
        for p in range(2):
            field_slabs(g, 3 * p, right_ref[p, rows_of(g), :] * (grid_scale * inverse_beta))
    mix((0, 1), False, fixed, mixed)
    layer(0)
    halos(0)
    sums = [jnp.zeros((8, 128), F32)] * 3
    for g in range(groups):
        lines_of = rows_of(g)
        result = operate(0, g)
        for p in range(2):
            applied[0, p, lines_of, :] = result[p]
            top, rest = split(result[p])
            high[p * lines + LINES * g : p * lines + LINES * (g + 1), :] = top
            low[p * lines + LINES * g : p * lines + LINES * (g + 1), :] = rest
        start = (right_ref[0, lines_of, :], right_ref[1, lines_of, :])
        square = folded(result[0] * result[0] + result[1] * result[1])
        sums = add(sums, (*pair(start, result), square))
    send_modes(1, scalar_tile(sums))
    wave_reduce(1)
    arrived(all_wave.at[1], 6, row_count, recv_sems)
    totals = col_total(1)
    unit_square = total_square * inverse_beta * inverse_beta
    a = (totals[0:1, :] * inverse_beta, totals[1:2, :] * inverse_beta)
    a_square = a[0] * a[0] + a[1] * a[1]
    rest_square = jnp.maximum(totals[2:3, :] - a_square * (2.0 - unit_square), 0.0)
    c = jnp.sqrt(rest_square + norm_eps)
    inverse_c = 1.0 / c
    a_over = (a[0] * inverse_beta, a[1] * inverse_beta)

    def next_vector(w, v):
        scaled = cmul(a_over, v)
        return (w[0] - scaled[0]) * inverse_c, (w[1] - scaled[1]) * inverse_c

    old, new = (all_wave[i].reshape(2 * lines, double) for i in range(2))
    planes = next_vector((new[:lines], new[lines:]), (old[:lines], old[lines:]))
    for p in range(2):
        re, im = unrotated(planes[p])
        modes[p, :, :kept] = re * grid_scale
        modes[p, :, kept:] = im * grid_scale
    for g in range(groups):
        lines_of = rows_of(g)
        vector = next_vector(
            (applied[0, 0, lines_of, :], applied[0, 1, lines_of, :]),
            (right_ref[0, lines_of, :], right_ref[1, lines_of, :]),
        )
        for p in range(2):
            basis[p, lines_of, :] = vector[p]
            field_slabs(g, 3 * p, vector[p] * grid_scale)
    mix((0, 1), False, fixed, mixed)
    layer(1)
    halos(1)
    sums = [jnp.zeros((8, 128), F32)] * 5
    for g in range(groups):
        lines_of = rows_of(g)
        result = operate(1, g)
        for p in range(2):
            applied[1, p, lines_of, :] = result[p]
        start = (right_ref[0, lines_of, :], right_ref[1, lines_of, :])
        vector = (basis[0, lines_of, :], basis[1, lines_of, :])
        square = folded(result[0] * result[0] + result[1] * result[1])
        sums = add(sums, (*pair(start, result), *pair(vector, result), square))
    got_scal[row] = scalar_tile(sums)
    spread(lambda there: got_scal.at[row], got_scal, 8, "row", row, row_count)
    arrived(got_scal, 8, row_count, recv_sems)
    total = got_scal[0]
    for r in range(1, row_count):
        total = total + got_scal[r]
    col_scal[2, col] = total
    spread(lambda there: col_scal.at[2, col], col_scal.at[2], 9, "col", col, col_count)
    arrived(col_scal.at[2], 9, col_count, recv_sems)
    total = col_scal[2, 0]
    for r in range(1, col_count):
        total = total + col_scal[2, r]
    totals = jnp.sum(total, axis=1, keepdims=True)
    b = (totals[0:1, :] * inverse_beta, totals[1:2, :] * inverse_beta)
    d = (totals[2:3, :], totals[3:4, :])
    b_square = b[0] * b[0] + b[1] * b[1]
    d_square = d[0] * d[0] + d[1] * d[1]
    second_square = rest_square * inverse_c * inverse_c
    overlap = (norm_eps * inverse_beta * inverse_beta) * inverse_c
    between = conj_cmul(b, d)
    between = between[0] * a[0] - between[1] * a[1]
    last_square = (
        totals[4:5, :]
        - b_square * (2.0 - unit_square)
        - d_square * (2.0 - second_square)
        + 2.0 * overlap * between
    )
    e = jnp.sqrt(jnp.maximum(last_square, 0.0) + norm_eps)
    y0, y1 = small_solve(beta, a, b, c, d, e)
    for g in range(groups):
        lines_of = rows_of(g)
        inner = slice(8 + LINES * g, 8 + LINES * (g + 1))
        z0, z1, w0, w1 = (
            [ext[0, p, inner, 128 : 128 + columns] for p in range(2)],
            [ext[1, p, inner, 128 : 128 + columns] for p in range(2)],
            [applied[0, p, lines_of, :] for p in range(2)],
            [applied[1, p, lines_of, :] for p in range(2)],
        )
        z0, z1, w0, w1 = cmul(y0, z0), cmul(y1, z1), cmul(y0, w0), cmul(y1, w1)
        for p in range(2):
            solution_ref[p, lines_of, :] = z0[p] + z1[p]
            residual_ref[p, lines_of, :] = right_ref[p, lines_of, :] - w0[p] - w1[p]

    arrived(got_feat, 0, row_count, send_sems)
    arrived(all_feat, 1, row_count, send_sems)
    for step in range(2):
        arrived(got_wave.at[step], 2 + 3 * step, row_count, send_sems)
        arrived(all_wave.at[step], 3 + 3 * step, row_count, send_sems)
        arrived(col_scal.at[step], 4 + 3 * step, col_count, send_sems)
    arrived(got_scal, 8, row_count, send_sems)
    arrived(col_scal.at[2], 9, col_count, send_sems)


def rounded(x):
    return lax.reduce_precision(x, 8, 7)


def shards(
    row_count,
    col_count,
    kept,
    forcing,
    medium_index,
    absorbing_mask,
    source_rows,
    source_cols,
    refraction,
    lift_weight,
    lift_bias,
    spectral_weight,
    point_weight,
    layer_bias,
    project_weight,
):
    _, lines, columns = forcing.shape
    channels = point_weight.shape[0]
    grid_cols = columns * row_count
    groups = lines // LINES
    double = 2 * kept
    assert row_count * 8 == 2 * lines

    table_high, table_low, table_back = base_tables(columns, kept, grid_cols)
    phases = phase_table(row_count, kept)

    highest = lax.Precision.HIGHEST
    lift = jnp.concatenate([lift_weight, lift_bias[None]], axis=0)
    mode_map = jnp.einsum("gc,pkco->pgok", lift, spectral_weight.astype(F32), precision=highest)
    twice = np.where(np.arange(kept) == 0, 1.0, 2.0).astype(np.float32)
    anchor = np.where(np.arange(kept) == 0, math.sqrt(grid_cols), 0.0).astype(np.float32)
    mode_map = mode_map * jnp.stack([twice] * 4 + [anchor])[None, :, None, :]

    point = jnp.einsum("co,gc->og", point_weight.astype(F32), lift, precision=highest)
    point = point + jnp.where(jnp.arange(5) == 4, layer_bias[:, None], 0.0)
    top = rounded(point)
    rest = rounded(point - top)
    order = []
    for g in range(4):
        order += [top[:, g], top[:, g], rest[:, g]]
    order += [top[:, 4], rest[:, 4], jnp.zeros_like(top[:, 4]), jnp.zeros_like(top[:, 4])]
    one_line = jnp.stack(order, axis=1)
    eye = jnp.eye(LINES, dtype=F32)
    point_map = (one_line[None, :, :, None] * eye[:, None, None, :]).reshape(
        LINES * channels, SLABS * LINES
    ).astype(BF16)
    project_map = (
        project_weight.astype(F32).T[:, None, None, :] * eye[None, :, :, None]
    ).reshape(2 * LINES, LINES * channels).astype(BF16)

    field = jax.ShapeDtypeStruct((2, lines, columns), F32)
    vmem = pl.BlockSpec(memory_space=pltpu.VMEM)
    smem = pl.BlockSpec(memory_space=pltpu.SMEM)
    hbm = pl.BlockSpec(memory_space=pl.ANY)
    dma = pltpu.SemaphoreType.DMA
    return pl.pallas_call(
        functools.partial(kernel, row_count, col_count, kept),
        out_shape=(field, field),
        in_specs=[vmem] * 5 + [smem] + [vmem] * 3 + [hbm] * 4,
        out_specs=(vmem, vmem),
        scratch_shapes=[
            pltpu.VMEM((columns, double), BF16),
            pltpu.VMEM((columns, double), BF16),
            pltpu.VMEM((8, double), F32),
            pltpu.VMEM((lines, columns), F32),
            pltpu.VMEM((lines, columns), F32),
            pltpu.VMEM((2, lines, columns), F32),
            pltpu.VMEM((groups, double + SLABS * LINES, columns), BF16),
            pltpu.VMEM((lines, channels, double + SLABS * LINES), BF16),
            pltpu.VMEM((lines, channels, double), F32),
            pltpu.VMEM((4, lines, double), F32),
            pltpu.VMEM((2 * lines, columns), BF16),
            pltpu.VMEM((2 * lines, columns), BF16),
            pltpu.VMEM((row_count, 8, double), F32),
            pltpu.VMEM((row_count, 8, double), F32),
            pltpu.VMEM((row_count, 8, double), F32),
            pltpu.VMEM((2, row_count, 8, double + 128), F32),
            pltpu.VMEM((2, row_count, 8, double + 128), F32),
            pltpu.VMEM((2, row_count, 8, double), F32),
            pltpu.VMEM((row_count, 8, 128), F32),
            pltpu.VMEM((3, col_count, 8, 128), F32),
            pltpu.VMEM((2, 2, lines + 16, columns + 256), F32),
            pltpu.VMEM((2, 2, lines, columns), F32),
            pltpu.VMEM((2, lines, columns), F32),
            dma((3 + groups,)),
            dma((2, 8)),
            dma((2, 8)),
            dma((10,)),
            dma((10,)),
        ],
        compiler_params=pltpu.CompilerParams(
            collective_id=0, has_side_effects=True, vmem_limit_bytes=56 * 2**20
        ),
        name="krylov",
    )(
        forcing,
        medium_index,
        absorbing_mask,
        source_rows.reshape(1, -1),
        source_cols.reshape(-1, 1),
        refraction,
        mode_map,
        point_map,
        project_map,
        table_high,
        table_low,
        table_back,
        phases,
    )


def solution(mesh):
    return jax.shard_map(
        functools.partial(shards, mesh.shape["row"], mesh.shape["col"], K),
        mesh=mesh,
        in_specs=(
            P(None, "col", "row"),
            P("col", "row"),
            P("col", "row"),
            P(),
            P(),
            P(),
            P(),
            P(),
            P(),
            P(),
            P(),
            P(),
        ),
        out_specs=(P(None, "col", "row"), P(None, "col", "row")),
        check_vma=False,
    )
```

```python
import functools
import math

import jax
import jax.numpy as jnp
import numpy as np
import ml_dtypes
from jax import lax
from jax.experimental import pallas as pl
from jax.experimental.pallas import tpu as pltpu
from jax.sharding import PartitionSpec as P

K = 256

wave_base = 0.23
source_gain = 8.0
norm_eps = 1e-06

MESH = pl.DeviceIdType.MESH
F32 = jnp.float32
BF16 = jnp.bfloat16
LINES = 16
SLABS = 16
PIECE = 256


def base_tables(tile_cols, kept_modes, grid_cols):
    positions = np.arange(tile_cols, dtype=np.int64)
    mode_index = np.arange(kept_modes, dtype=np.int64)
    angles = (positions[:, None] * mode_index[None, :] % grid_cols) * (2.0 * math.pi / grid_cols)
    scale = 1.0 / math.sqrt(grid_cols)
    table = np.concatenate([np.cos(angles), -np.sin(angles)], axis=1) * scale
    high = table.astype(np.float32).astype(ml_dtypes.bfloat16)
    low = (table - high.astype(np.float64)).astype(np.float32).astype(ml_dtypes.bfloat16)
    return high, low, np.ascontiguousarray(high.T)


def phase_table(row_count, kept_modes):
    tile = np.arange(row_count, dtype=np.int64)
    mode_index = np.arange(kept_modes, dtype=np.int64)
    angles = (tile[:, None] * mode_index[None, :] % row_count) * (2.0 * math.pi / row_count)
    table = np.concatenate([np.cos(angles), np.sin(angles)], axis=1).astype(np.float32)
    return np.ascontiguousarray(np.broadcast_to(table[:, None, :], (row_count, 8, 2 * kept_modes)))


def split(x):
    high = x.astype(BF16)
    return high, (x - high.astype(F32)).astype(BF16)


def three_way(x):
    high, low = split(x)
    return high, low, (x - high.astype(F32) - low.astype(F32)).astype(BF16)


def gelu(x):
    return 0.5 * x * (1.0 + lax.erf(x * math.sqrt(0.5)))


def cmul(a, b):
    return a[0] * b[0] - a[1] * b[1], a[0] * b[1] + a[1] * b[0]


def conj_cmul(a, b):
    return a[0] * b[0] + a[1] * b[1], a[0] * b[1] - a[1] * b[0]


def small_solve(beta, a, b, c, d, e):
    gram_first = a[0] * a[0] + a[1] * a[1] + c * c
    gram_second = b[0] * b[0] + b[1] * b[1] + d[0] * d[0] + d[1] * d[1] + e * e
    cross = conj_cmul(a, b)
    cross = (cross[0] + c * d[0], cross[1] + c * d[1])
    ad = cmul(a, d)
    minor = (ad[0] - b[0] * c, ad[1] - b[1] * c)
    determinant = (
        minor[0] * minor[0]
        + minor[1] * minor[1]
        + (a[0] * a[0] + a[1] * a[1]) * e * e
        + c * c * e * e
    )
    first = (beta * a[0], -beta * a[1])
    second = (beta * b[0], -beta * b[1])
    t = cmul(cross, second)
    y0 = ((gram_second * first[0] - t[0]) / determinant, (gram_second * first[1] - t[1]) / determinant)
    t = conj_cmul(cross, first)
    y1 = ((gram_first * second[0] - t[0]) / determinant, (gram_first * second[1] - t[1]) / determinant)
    return y0, y1


def kernel(
    row_count,
    col_count,
    kept,
    forcing,
    medium,
    mask,
    source_rows,
    source_cols,
    refraction,
    lift_weight,
    lift_bias,
    spectral_weight,
    point_weight,
    layer_bias,
    project_weight,
    table_high,
    table_low,
    table_back,
    phases,
    solution_ref,
    residual_ref,
    fwd_high,
    fwd_low,
    phase,
    weights,
    by_mode,
    mode_map,
    project_map,
    wave_ref,
    damp_ref,
    right_ref,
    rhs_cols,
    mixed,
    fixed,
    modes,
    high,
    low,
    send_feat,
    got_feat,
    all_feat,
    send_wave,
    got_wave,
    all_wave,
    got_scal,
    col_scal,
    before,
    ext,
    applied,
    basis,
    table_sems,
    halo_send,
    halo_recv,
    send_sems,
    recv_sems,
):
    lines, columns = mask.shape
    channels = point_weight.shape[0]
    groups = lines // LINES
    double = 2 * kept
    row = lax.axis_index("row")
    col = lax.axis_index("col")
    grid_scale = math.sqrt(lines * col_count * columns * row_count)

    table_copies = [
        pltpu.make_async_copy(table_high, fwd_high, table_sems.at[0]),
        pltpu.make_async_copy(table_low, fwd_low, table_sems.at[1]),
        pltpu.make_async_copy(phases.at[row], phase, table_sems.at[2]),
    ]
    back_copies = [
        pltpu.make_async_copy(table_back, rhs_cols.at[g, pl.ds(0, double)], table_sems.at[3 + g])
        for g in range(groups)
    ]
    weight_copy = pltpu.make_async_copy(spectral_weight, weights, table_sems.at[3 + groups])
    for copy in [*table_copies, weight_copy, *back_copies]:
        copy.start()

    barrier = pltpu.get_barrier_semaphore()
    greeted = 0
    for d in range(1, row_count):
        pl.semaphore_signal(
            barrier, inc=1, device_id={"row": lax.rem(row + d, row_count)}, device_id_type=MESH
        )
        greeted += 1
    for d in range(1, col_count):
        pl.semaphore_signal(
            barrier, inc=1, device_id={"col": lax.rem(col + d, col_count)}, device_id_type=MESH
        )
        greeted += 1
    for dr in (1, row_count - 1):
        for dc in (1, col_count - 1):
            pl.semaphore_signal(
                barrier,
                inc=1,
                device_id={
                    "row": lax.rem(row + dr, row_count),
                    "col": lax.rem(col + dc, col_count),
                },
                device_id_type=MESH,
            )
            greeted += 1

    def spread(source, target, index, axis, me, count):
        for d in range(1, count):
            there = lax.rem(me + d, count)
            pltpu.make_async_remote_copy(
                src_ref=source(there),
                dst_ref=target.at[me],
                send_sem=send_sems.at[index],
                recv_sem=recv_sems.at[index],
                device_id={axis: there},
                device_id_type=MESH,
            ).start()

    def arrived(target, index, count, sems):
        whole = target.at[pl.ds(0, count - 1)]
        pltpu.make_async_copy(whole, whole, sems.at[index]).wait()

    def forward(out):
        spectrum = (
            jnp.dot(high[...], fwd_high[...], preferred_element_type=F32)
            + jnp.dot(high[...], fwd_low[...], preferred_element_type=F32)
            + jnp.dot(low[...], fwd_high[...], preferred_element_type=F32)
        )
        cosine, sine = phase[0:1, :kept], phase[0:1, kept:]
        re, im = spectrum[:, :kept], spectrum[:, kept:]
        out[:, :, 0:kept] = (re * cosine + im * sine).reshape(row_count, 8, kept)
        out[:, :, kept:double] = (im * cosine - re * sine).reshape(row_count, 8, kept)

    def unrotated(both):
        cosine, sine = phase[0:1, :kept], phase[0:1, kept:]
        re, im = both[:, :kept], both[:, kept:]
        return re * cosine - im * sine, im * cosine + re * sine

    def slab(g, j, value):
        rhs_cols[g, double + LINES * j : double + LINES * (j + 1), :] = value

    def field_slabs(g, j, value):
        top, rest = split(value)
        slab(g, j, top)
        slab(g, j + 1, rest)
        slab(g, j + 2, top)
        return top, rest

    def rows_of(g):
        return slice(LINES * g, LINES * (g + 1))

    def folded(x):
        total = jnp.zeros((8, 128), F32)
        for i in range(x.shape[0] // 8):
            for j in range(x.shape[1] // 128):
                total = total + x[8 * i : 8 * i + 8, 128 * j : 128 * j + 128]
        return total

    def scalar_tile(parts):
        place = lax.broadcasted_iota(jnp.int32, (8, 128), 0)
        tile = jnp.zeros((8, 128), F32)
        for i, part in enumerate(parts):
            tile = jnp.where(place == i, jnp.sum(part, axis=0, keepdims=True), tile)
        return tile

    for g in range(groups):
        lines_of = rows_of(g)
        kind = medium[lines_of, :]
        refractive = jnp.zeros((LINES, columns), F32)
        for level in range(refraction.shape[0]):
            refractive = jnp.where(kind == level, refraction[level], refractive)
        damping = 0.1 + mask[lines_of, :].astype(F32)
        damp_ref[lines_of, :] = damping
        scaled = wave_base * refractive
        wave_ref[lines_of, :] = scaled * scaled
        top, rest = field_slabs(g, 6, refractive)
        high[lines_of, :] = top
        low[lines_of, :] = rest
        top, rest = field_slabs(g, 9, damping)
        high[lines + LINES * g : lines + LINES * (g + 1), :] = top
        low[lines + LINES * g : lines + LINES * (g + 1), :] = rest
        ones = jnp.ones((LINES, columns), BF16)
        slab(g, 12, ones)
        slab(g, 13, ones)
        slab(g, 14, jnp.zeros_like(ones))
        slab(g, 15, jnp.zeros_like(ones))
    for copy in table_copies:
        copy.wait()
    forward(send_feat)
    pl.semaphore_wait(barrier, greeted)
    spread(lambda there: send_feat.at[there], got_feat, 0, "row", row, row_count)

    sources = source_rows.shape[0]
    place = lax.broadcasted_iota(jnp.int32, (sources, 128), 0)
    col_of = jnp.zeros((sources, 128), jnp.int32)
    for i in range(sources):
        col_of = jnp.where(place == i, source_cols[i] - columns * row, col_of)
    lane = lax.broadcasted_iota(jnp.int32, (sources, 128), 1)
    col_hits = jnp.concatenate(
        [jnp.where(col_of == lane + 128 * j, 1.0, 0.0) for j in range(columns // 128)], axis=1
    ).astype(BF16)
    place = lax.broadcasted_iota(jnp.int32, (lines, sources), 1)
    row_of = jnp.zeros((lines, sources), jnp.int32)
    for i in range(sources):
        row_of = jnp.where(place == i, source_rows[i] - lines * col, row_of)
    line_hits = jnp.where(
        row_of == lax.broadcasted_iota(jnp.int32, (lines, sources), 0), 1.0, 0.0
    ).astype(BF16)
    source_count = jnp.dot(line_hits, col_hits, preferred_element_type=F32)
    square = jnp.zeros((8, 128), F32)
    for g in range(groups):
        lines_of = rows_of(g)
        for p in range(2):
            field = forcing[p, lines_of, :]
            if p == 0:
                field = field + source_gain * source_count[lines_of, :]
            right_ref[p, lines_of, :] = field
            square = square + folded(field * field)
            top, rest = split(field)
            high[p * lines + LINES * g : p * lines + LINES * (g + 1), :] = top
            low[p * lines + LINES * g : p * lines + LINES * (g + 1), :] = rest
    def send_modes(step, tile):
        forward(send_wave.at[step])
        for r in range(row_count):
            send_wave[step, r, :, double:] = tile
        spread(
            lambda there: send_wave.at[step, there], got_wave.at[step], 2 + 3 * step, "row", row, row_count
        )

    send_modes(0, scalar_tile([square]))

    lift = jnp.concatenate(
        [lift_weight[...], lift_bias[...], jnp.zeros((3, channels), F32)], axis=0
    )
    lift_parts = three_way(lift)
    point = jnp.zeros((8, channels), F32)
    for part in lift_parts:
        point = point + jnp.dot(part, point_weight[...], preferred_element_type=F32)
    channel_row = lax.broadcasted_iota(jnp.int32, (8, channels), 0)
    point = point + jnp.where(channel_row == 4, layer_bias[...], 0.0)
    top, rest = split(point)
    wide = SLABS * LINES
    from_row = lax.broadcasted_iota(jnp.int32, (8, wide), 0)
    slab_of = lax.broadcasted_iota(jnp.int32, (8, wide), 1) // LINES
    first_slab = 3 * from_row
    pick_top = ((slab_of == first_slab) | ((slab_of == first_slab + 1) & (from_row < 4))) & (from_row < 5)
    pick_rest = ((slab_of == first_slab + 2) & (from_row < 4)) | ((slab_of == 13) & (from_row == 4))
    over_rows = (((0,), (0,)), ((), ()))
    spread_out = lax.dot_general(
        top.astype(F32), jnp.where(pick_top, 1.0, 0.0), over_rows, preferred_element_type=F32
    ) + lax.dot_general(
        rest.astype(F32), jnp.where(pick_rest, 1.0, 0.0), over_rows, preferred_element_type=F32
    )
    line_of = lax.broadcasted_iota(jnp.int32, (channels, wide), 1) % LINES
    for i in range(LINES):
        masked = jnp.where(line_of == i, spread_out, 0.0).astype(BF16)
        for g in range(groups):
            mixed[LINES * g + i, :, double:] = masked
    all_rows = LINES * channels
    tiles = jnp.where(
        lax.broadcasted_iota(jnp.int32, (channels, all_rows), 0)
        == lax.broadcasted_iota(jnp.int32, (channels, all_rows), 1) % channels,
        1.0,
        0.0,
    )
    across = lax.dot_general(
        project_weight[...].astype(F32), tiles, over_rows, preferred_element_type=F32
    )
    own_line = (
        lax.broadcasted_iota(jnp.int32, (LINES, all_rows), 0)
        == lax.broadcasted_iota(jnp.int32, (LINES, all_rows), 1) // channels
    )
    for p in range(2):
        project_map[LINES * p : LINES * (p + 1), :] = jnp.where(
            own_line, across[p : p + 1, :], 0.0
        ).astype(BF16)

    own_mode = (
        lax.broadcasted_iota(jnp.int32, (8, 8 * channels), 0)
        == lax.broadcasted_iota(jnp.int32, (8, 8 * channels), 1) // channels
    )
    stacked = []
    for part in lift_parts[:2]:
        along = jnp.concatenate([part.astype(F32)] * 8, axis=1)
        stacked += [jnp.where(own_mode, along[g : g + 1, :], 0.0) for g in range(5)]
    stacked = jnp.concatenate(stacked, axis=0).astype(BF16)
    weight_copy.wait()

    def eight_modes(block, carry):
        first = pl.multiple_of(8 * block, 8)
        for part in range(2):
            some = weights[part, pl.ds(first, 8)].reshape(8 * channels, channels)
            both = jnp.dot(stacked, some, preferred_element_type=F32)
            both = both[:40] + both[40:]
            for g in range(5):
                by_mode[part, g, pl.ds(first, 8), 0:channels] = both[8 * g : 8 * g + 8]
        return carry

    lax.fori_loop(0, kept // 8, eight_modes, 0)
    mode_of = lax.broadcasted_iota(jnp.int32, (1, kept), 1)
    twice = jnp.where(mode_of == 0, 1.0, 2.0)
    anchor = jnp.where(mode_of == 0, math.sqrt(columns * row_count), 0.0)
    for part in range(2):
        for g in range(5):
            turned = jnp.transpose(by_mode[part, g])[:channels]
            mode_map[part, g] = turned * (twice if g < 4 else anchor)

    def reduced(got, source):
        got[row] = source[row]
        total = got[0]
        for r in range(1, row_count):
            total = total + got[r]
        return total

    arrived(got_feat, 0, row_count, recv_sems)
    all_feat[row] = reduced(got_feat, send_feat)
    spread(lambda there: all_feat.at[row], all_feat, 1, "row", row, row_count)

    def wave_reduce(step):
        index = 2 + 3 * step
        arrived(got_wave.at[step], index, row_count, recv_sems)
        total = reduced(got_wave.at[step], send_wave.at[step])
        all_wave[step, row] = total[:, :double]
        spread(
            lambda there: all_wave.at[step, row], all_wave.at[step], index + 1, "row", row, row_count
        )
        col_scal[step, col] = total[:, double:]
        spread(
            lambda there: col_scal.at[step, col], col_scal.at[step], index + 2, "col", col, col_count
        )

    def col_total(step):
        arrived(col_scal.at[step], 4 + 3 * step, col_count, recv_sems)
        total = col_scal[step, 0]
        for r in range(1, col_count):
            total = total + col_scal[step, r]
        return jnp.sum(total, axis=1, keepdims=True)

    def mix_lines(first, count, kc, ob, channels_in, bias, source, store):
        low_k, high_k = pl.ds(128 * kc, 128), pl.ds(kept + 128 * kc, 128)
        outs = pl.ds(16 * ob, 16)
        maps = [(mode_map[0, g, outs, low_k], mode_map[1, g, outs, low_k]) for g in channels_in]
        start = (mode_map[0, 4, outs, low_k], mode_map[1, 4, outs, low_k]) if bias else None
        for block in range(count // 8):
            top = first + 8 * block
            parts = [
                (modes[g, pl.ds(top, 8), low_k], modes[g, pl.ds(top, 8), high_k]) for g in channels_in
            ]
            for i in range(8):
                line = top + i
                if bias:
                    re, im = start
                else:
                    re, im = source[line, outs, low_k], source[line, outs, high_k]
                for (mode_re, mode_im), (map_re, map_im) in zip(parts, maps):
                    one_re, one_im = mode_re[i : i + 1], mode_im[i : i + 1]
                    re = re + (map_re * one_re - map_im * one_im)
                    im = im + (map_re * one_im + map_im * one_re)
                store[line, outs, low_k] = re.astype(store.dtype)
                store[line, outs, high_k] = im.astype(store.dtype)

    def mix_fixed():
        for kc in range(kept // 128):
            for ob in range(channels // 16):

                def eight_lines(block, carry):
                    first = pl.multiple_of(8 * block, 8)
                    mix_lines(first, 8, kc, ob, (2, 3), True, None, fixed)
                    return carry

                lax.fori_loop(0, lines // 8, eight_lines, 0)

    def mix_group(g):
        for kc in range(kept // 128):
            for ob in range(channels // 16):
                mix_lines(LINES * g, LINES, kc, ob, (0, 1), False, fixed, mixed)

    def layer(step):
        last = columns // PIECE - 1
        edges = [(g, n) for g in range(groups) for n in sorted({0, last})]
        ends = [(g, n) for g in sorted({0, groups - 1}) for n in range(1, last)]
        inside = [(g, n) for g in range(1, groups - 1) for n in range(1, last)]
        order = edges + ends + inside
        copies = halo_copies(step)

        def multiply(g, n, slot):
            left = mixed[LINES * g : LINES * (g + 1)].reshape(LINES * channels, double + SLABS * LINES)
            before[slot] = jnp.dot(
                left, rhs_cols[g, :, PIECE * n : PIECE * (n + 1)], preferred_element_type=F32
            )

        def finish(g, n, slot):
            active = gelu(before[slot]).astype(BF16)
            out = jnp.dot(project_map[...], active, preferred_element_type=F32)
            first = 8 + LINES * g
            place = slice(128 + PIECE * n, 128 + PIECE * (n + 1))
            ext[step, 0, first : first + LINES, place] = out[:LINES]
            ext[step, 1, first : first + LINES, place] = out[LINES:]

        mix_group(0)
        for t in range(len(order) + 1):
            if t < len(order):
                g, n = order[t]
                multiply(g, n, t % 2)
                if t < len(edges) and n == 0 and g + 1 < groups:
                    mix_group(g + 1)
            if t > 0:
                finish(*order[t - 1], (t - 1) % 2)
            if t == len(edges):
                for i in (0, 1, 4, 5, 6, 7):
                    copies[i].start()
            if t == len(edges) + len(ends):
                for i in (2, 3):
                    copies[i].start()

    def halo_copies(step):
        tall, across_all = pl.ds(8, lines), pl.ds(128, columns)
        line_ends = {
            1: (pl.ds(lines, 8), pl.ds(0, 8)),
            -1: (pl.ds(8, 8), pl.ds(8 + lines, 8)),
            0: (tall, tall),
        }
        col_ends = {
            1: (pl.ds(columns, 128), pl.ds(0, 128)),
            -1: (pl.ds(128, 128), pl.ds(128 + columns, 128)),
            0: (across_all, across_all),
        }
        copies = []
        for i, (dr, dc) in enumerate(
            [(1, 0), (-1, 0), (0, 1), (0, -1), (1, 1), (1, -1), (-1, 1), (-1, -1)]
        ):
            here_l, there_l = line_ends[dc]
            here_c, there_c = col_ends[dr]
            copies.append(
                pltpu.make_async_remote_copy(
                    src_ref=ext.at[step, :, here_l, here_c],
                    dst_ref=ext.at[step, :, there_l, there_c],
                    send_sem=halo_send.at[step, i],
                    recv_sem=halo_recv.at[step, i],
                    device_id={
                        "row": lax.rem(row + dr + row_count, row_count),
                        "col": lax.rem(col + dc + col_count, col_count),
                    },
                    device_id_type=MESH,
                )
            )
        return copies

    def halos(step):
        for copy in halo_copies(step):
            copy.wait()
        view = ext.at[step]

        @pl.when(row == 0)
        def _():
            view[:, :, 0:128] = jnp.zeros((2, lines + 16, 128), F32)

        @pl.when(row == row_count - 1)
        def _():
            view[:, :, 128 + columns :] = jnp.zeros((2, lines + 16, 128), F32)

        @pl.when(col == 0)
        def _():
            view[:, 0:8, :] = jnp.zeros((2, 8, columns + 256), F32)

        @pl.when(col == col_count - 1)
        def _():
            view[:, 8 + lines :, :] = jnp.zeros((2, 8, columns + 256), F32)

    def operate(step, g):
        laps, fields = [], []
        for p in range(2):
            first = 8 + LINES * g
            beside = (
                ext[step, p, first - 1 : first - 1 + LINES, :]
                + ext[step, p, first + 1 : first + 1 + LINES, :]
            )
            centre = ext[step, p, first : first + LINES, :]
            both = 4.0 * centre + beside
            width = columns + 256
            around = pltpu.roll(both, 1, 1) + pltpu.roll(both, width - 1, 1)
            total = (4.0 * beside - 20.0 * centre + around) * (1.0 / 6.0)
            laps.append(total[:, 128 : 128 + columns])
            fields.append(centre[:, 128 : 128 + columns])
        wave, damping = wave_ref[rows_of(g), :], damp_ref[rows_of(g), :]
        real = -laps[0] - wave * (fields[0] + damping * fields[1])
        imag = -laps[1] - wave * (fields[1] - damping * fields[0])
        return real, imag

    def pair(first, second):
        return (
            folded(first[0] * second[0] + first[1] * second[1]),
            folded(first[0] * second[1] - first[1] * second[0]),
        )

    def add(a, b):
        return [x + y for x, y in zip(a, b)]

    wave_reduce(0)
    arrived(all_feat, 1, row_count, recv_sems)
    re, im = unrotated(all_feat[...].reshape(2 * lines, double))
    for g in range(2):
        modes[2 + g, :, :kept] = re[g * lines : (g + 1) * lines]
        modes[2 + g, :, kept:] = im[g * lines : (g + 1) * lines]
    mix_fixed()
    for copy in back_copies:
        copy.wait()

    arrived(all_wave.at[0], 3, row_count, recv_sems)
    total_square = col_total(0)[0:1, :]
    beta = jnp.sqrt(total_square + norm_eps)
    inverse_beta = 1.0 / beta
    re, im = unrotated(all_wave[0].reshape(2 * lines, double))
    for p in range(2):
        modes[p, :, :kept] = re[p * lines : (p + 1) * lines] * (grid_scale * inverse_beta)
        modes[p, :, kept:] = im[p * lines : (p + 1) * lines] * (grid_scale * inverse_beta)
    for g in range(groups):
        for p in range(2):
            field_slabs(g, 3 * p, right_ref[p, rows_of(g), :] * (grid_scale * inverse_beta))
    layer(0)
    halos(0)
    sums = [jnp.zeros((8, 128), F32)] * 3
    for g in range(groups):
        lines_of = rows_of(g)
        result = operate(0, g)
        for p in range(2):
            applied[0, p, lines_of, :] = result[p]
            top, rest = split(result[p])
            high[p * lines + LINES * g : p * lines + LINES * (g + 1), :] = top
            low[p * lines + LINES * g : p * lines + LINES * (g + 1), :] = rest
        start = (right_ref[0, lines_of, :], right_ref[1, lines_of, :])
        square = folded(result[0] * result[0] + result[1] * result[1])
        sums = add(sums, (*pair(start, result), square))
    send_modes(1, scalar_tile(sums))
    wave_reduce(1)
    arrived(all_wave.at[1], 6, row_count, recv_sems)
    totals = col_total(1)
    unit_square = total_square * inverse_beta * inverse_beta
    a = (totals[0:1, :] * inverse_beta, totals[1:2, :] * inverse_beta)
    a_square = a[0] * a[0] + a[1] * a[1]
    rest_square = jnp.maximum(totals[2:3, :] - a_square * (2.0 - unit_square), 0.0)
    c = jnp.sqrt(rest_square + norm_eps)
    inverse_c = 1.0 / c
    a_over = (a[0] * inverse_beta, a[1] * inverse_beta)

    def next_vector(w, v):
        scaled = cmul(a_over, v)
        return (w[0] - scaled[0]) * inverse_c, (w[1] - scaled[1]) * inverse_c

    old, new = (all_wave[i].reshape(2 * lines, double) for i in range(2))
    planes = next_vector((new[:lines], new[lines:]), (old[:lines], old[lines:]))
    for p in range(2):
        re, im = unrotated(planes[p])
        modes[p, :, :kept] = re * grid_scale
        modes[p, :, kept:] = im * grid_scale
    for g in range(groups):
        lines_of = rows_of(g)
        vector = next_vector(
            (applied[0, 0, lines_of, :], applied[0, 1, lines_of, :]),
            (right_ref[0, lines_of, :], right_ref[1, lines_of, :]),
        )
        for p in range(2):
            basis[p, lines_of, :] = vector[p]
            field_slabs(g, 3 * p, vector[p] * grid_scale)
    layer(1)
    halos(1)
    sums = [jnp.zeros((8, 128), F32)] * 5
    for g in range(groups):
        lines_of = rows_of(g)
        result = operate(1, g)
        for p in range(2):
            applied[1, p, lines_of, :] = result[p]
        start = (right_ref[0, lines_of, :], right_ref[1, lines_of, :])
        vector = (basis[0, lines_of, :], basis[1, lines_of, :])
        square = folded(result[0] * result[0] + result[1] * result[1])
        sums = add(sums, (*pair(start, result), *pair(vector, result), square))
    got_scal[row] = scalar_tile(sums)
    spread(lambda there: got_scal.at[row], got_scal, 8, "row", row, row_count)
    arrived(got_scal, 8, row_count, recv_sems)
    total = got_scal[0]
    for r in range(1, row_count):
        total = total + got_scal[r]
    col_scal[2, col] = total
    spread(lambda there: col_scal.at[2, col], col_scal.at[2], 9, "col", col, col_count)
    arrived(col_scal.at[2], 9, col_count, recv_sems)
    total = col_scal[2, 0]
    for r in range(1, col_count):
        total = total + col_scal[2, r]
    totals = jnp.sum(total, axis=1, keepdims=True)
    b = (totals[0:1, :] * inverse_beta, totals[1:2, :] * inverse_beta)
    d = (totals[2:3, :], totals[3:4, :])
    b_square = b[0] * b[0] + b[1] * b[1]
    d_square = d[0] * d[0] + d[1] * d[1]
    second_square = rest_square * inverse_c * inverse_c
    overlap = (norm_eps * inverse_beta * inverse_beta) * inverse_c
    between = conj_cmul(b, d)
    between = between[0] * a[0] - between[1] * a[1]
    last_square = (
        totals[4:5, :]
        - b_square * (2.0 - unit_square)
        - d_square * (2.0 - second_square)
        + 2.0 * overlap * between
    )
    e = jnp.sqrt(jnp.maximum(last_square, 0.0) + norm_eps)
    y0, y1 = small_solve(beta, a, b, c, d, e)
    for g in range(groups):
        lines_of = rows_of(g)
        inner = slice(8 + LINES * g, 8 + LINES * (g + 1))
        z0, z1, w0, w1 = (
            [ext[0, p, inner, 128 : 128 + columns] for p in range(2)],
            [ext[1, p, inner, 128 : 128 + columns] for p in range(2)],
            [applied[0, p, lines_of, :] for p in range(2)],
            [applied[1, p, lines_of, :] for p in range(2)],
        )
        z0, z1, w0, w1 = cmul(y0, z0), cmul(y1, z1), cmul(y0, w0), cmul(y1, w1)
        for p in range(2):
            solution_ref[p, lines_of, :] = z0[p] + z1[p]
            residual_ref[p, lines_of, :] = right_ref[p, lines_of, :] - w0[p] - w1[p]

    arrived(got_feat, 0, row_count, send_sems)
    arrived(all_feat, 1, row_count, send_sems)
    for step in range(2):
        arrived(got_wave.at[step], 2 + 3 * step, row_count, send_sems)
        arrived(all_wave.at[step], 3 + 3 * step, row_count, send_sems)
        arrived(col_scal.at[step], 4 + 3 * step, col_count, send_sems)
    arrived(got_scal, 8, row_count, send_sems)
    arrived(col_scal.at[2], 9, col_count, send_sems)


def shards(
    row_count,
    col_count,
    kept,
    forcing,
    medium_index,
    absorbing_mask,
    source_rows,
    source_cols,
    refraction,
    lift_weight,
    lift_bias,
    spectral_weight,
    point_weight,
    layer_bias,
    project_weight,
):
    _, lines, columns = forcing.shape
    channels = point_weight.shape[0]
    grid_cols = columns * row_count
    groups = lines // LINES
    double = 2 * kept
    assert row_count * 8 == 2 * lines

    table_high, table_low, table_back = base_tables(columns, kept, grid_cols)
    phases = phase_table(row_count, kept)

    field = jax.ShapeDtypeStruct((2, lines, columns), F32)
    vmem = pl.BlockSpec(memory_space=pltpu.VMEM)
    smem = pl.BlockSpec(memory_space=pltpu.SMEM)
    hbm = pl.BlockSpec(memory_space=pl.ANY)
    dma = pltpu.SemaphoreType.DMA
    return pl.pallas_call(
        functools.partial(kernel, row_count, col_count, kept),
        out_shape=(field, field),
        in_specs=[vmem] * 3 + [smem] * 3 + [vmem] * 2 + [hbm] + [vmem] * 3 + [hbm] * 4,
        out_specs=(vmem, vmem),
        scratch_shapes=[
            pltpu.VMEM((columns, double), BF16),
            pltpu.VMEM((columns, double), BF16),
            pltpu.VMEM((8, double), F32),
            pltpu.VMEM((2, kept, channels, channels), BF16),
            pltpu.VMEM((2, 5, kept, 128), F32),
            pltpu.VMEM((2, 5, channels, kept), F32),
            pltpu.VMEM((2 * LINES, LINES * channels), BF16),
            pltpu.VMEM((lines, columns), F32),
            pltpu.VMEM((lines, columns), F32),
            pltpu.VMEM((2, lines, columns), F32),
            pltpu.VMEM((groups, double + SLABS * LINES, columns), BF16),
            pltpu.VMEM((lines, channels, double + SLABS * LINES), BF16),
            pltpu.VMEM((lines, channels, double), F32),
            pltpu.VMEM((4, lines, double), F32),
            pltpu.VMEM((2 * lines, columns), BF16),
            pltpu.VMEM((2 * lines, columns), BF16),
            pltpu.VMEM((row_count, 8, double), F32),
            pltpu.VMEM((row_count, 8, double), F32),
            pltpu.VMEM((row_count, 8, double), F32),
            pltpu.VMEM((2, row_count, 8, double + 128), F32),
            pltpu.VMEM((2, row_count, 8, double + 128), F32),
            pltpu.VMEM((2, row_count, 8, double), F32),
            pltpu.VMEM((row_count, 8, 128), F32),
            pltpu.VMEM((3, col_count, 8, 128), F32),
            pltpu.VMEM((2, LINES * channels, PIECE), F32),
            pltpu.VMEM((2, 2, lines + 16, columns + 256), F32),
            pltpu.VMEM((2, 2, lines, columns), F32),
            pltpu.VMEM((2, lines, columns), F32),
            dma((4 + groups,)),
            dma((2, 8)),
            dma((2, 8)),
            dma((10,)),
            dma((10,)),
        ],
        compiler_params=pltpu.CompilerParams(
            collective_id=0, has_side_effects=True, vmem_limit_bytes=56 * 2**20
        ),
        name="krylov",
    )(
        forcing,
        medium_index,
        absorbing_mask,
        source_rows,
        source_cols,
        refraction,
        lift_weight,
        lift_bias.reshape(1, -1),
        spectral_weight,
        point_weight,
        layer_bias.reshape(1, -1),
        project_weight,
        table_high,
        table_low,
        table_back,
        phases,
    )


def solution(mesh):
    return jax.shard_map(
        functools.partial(shards, mesh.shape["row"], mesh.shape["col"], K),
        mesh=mesh,
        in_specs=(
            P(None, "col", "row"),
            P("col", "row"),
            P("col", "row"),
            P(),
            P(),
            P(),
            P(),
            P(),
            P(),
            P(),
            P(),
            P(),
        ),
        out_specs=(P(None, "col", "row"), P(None, "col", "row")),
        check_vma=False,
    )
```

```python
import functools
import math

import jax
import jax.numpy as jnp
import numpy as np
import ml_dtypes
from jax import lax
from jax.experimental import pallas as pl
from jax.experimental.pallas import tpu as pltpu
from jax.sharding import PartitionSpec as P

K = 256

wave_base = 0.23
source_gain = 8.0
norm_eps = 1e-06

MESH = pl.DeviceIdType.MESH
F32 = jnp.float32
BF16 = jnp.bfloat16
LINES = 16
SLABS = 16
PIECE = 256


def base_tables(tile_cols, kept_modes, grid_cols):
    positions = np.arange(tile_cols, dtype=np.int64)
    mode_index = np.arange(kept_modes, dtype=np.int64)
    angles = (positions[:, None] * mode_index[None, :] % grid_cols) * (2.0 * math.pi / grid_cols)
    scale = 1.0 / math.sqrt(grid_cols)
    table = np.concatenate([np.cos(angles), -np.sin(angles)], axis=1) * scale
    high = table.astype(np.float32).astype(ml_dtypes.bfloat16)
    low = (table - high.astype(np.float64)).astype(np.float32).astype(ml_dtypes.bfloat16)
    return high, low, np.ascontiguousarray(high.T)


def phase_table(row_count, kept_modes):
    tile = np.arange(row_count, dtype=np.int64)
    mode_index = np.arange(kept_modes, dtype=np.int64)
    angles = (tile[:, None] * mode_index[None, :] % row_count) * (2.0 * math.pi / row_count)
    table = np.concatenate([np.cos(angles), np.sin(angles)], axis=1).astype(np.float32)
    return np.ascontiguousarray(np.broadcast_to(table[:, None, :], (row_count, 8, 2 * kept_modes)))


def split(x):
    high = x.astype(BF16)
    return high, (x - high.astype(F32)).astype(BF16)


def three_way(x):
    high, low = split(x)
    return high, low, (x - high.astype(F32) - low.astype(F32)).astype(BF16)


def gelu(x):
    return 0.5 * x * (1.0 + lax.erf(x * math.sqrt(0.5)))


def cmul(a, b):
    return a[0] * b[0] - a[1] * b[1], a[0] * b[1] + a[1] * b[0]


def conj_cmul(a, b):
    return a[0] * b[0] + a[1] * b[1], a[0] * b[1] - a[1] * b[0]


def small_solve(beta, a, b, c, d, e):
    gram_first = a[0] * a[0] + a[1] * a[1] + c * c
    gram_second = b[0] * b[0] + b[1] * b[1] + d[0] * d[0] + d[1] * d[1] + e * e
    cross = conj_cmul(a, b)
    cross = (cross[0] + c * d[0], cross[1] + c * d[1])
    ad = cmul(a, d)
    minor = (ad[0] - b[0] * c, ad[1] - b[1] * c)
    determinant = (
        minor[0] * minor[0]
        + minor[1] * minor[1]
        + (a[0] * a[0] + a[1] * a[1]) * e * e
        + c * c * e * e
    )
    first = (beta * a[0], -beta * a[1])
    second = (beta * b[0], -beta * b[1])
    t = cmul(cross, second)
    y0 = ((gram_second * first[0] - t[0]) / determinant, (gram_second * first[1] - t[1]) / determinant)
    t = conj_cmul(cross, first)
    y1 = ((gram_first * second[0] - t[0]) / determinant, (gram_first * second[1] - t[1]) / determinant)
    return y0, y1


def kernel(
    row_count,
    col_count,
    kept,
    forcing,
    medium,
    mask,
    source_rows,
    source_cols,
    refraction,
    lift_scalars,
    bias_scalars,
    lift_weight,
    lift_bias,
    spectral_weight,
    point_weight,
    layer_bias,
    project_weight,
    table_high,
    table_low,
    table_back,
    phases,
    solution_ref,
    residual_ref,
    fwd_high,
    fwd_low,
    phase,
    weights,
    mode_map,
    project_map,
    wave_ref,
    damp_ref,
    right_ref,
    rhs_cols,
    mixed,
    fixed,
    modes,
    high,
    low,
    send_feat,
    got_feat,
    all_feat,
    send_wave,
    got_wave,
    all_wave,
    got_scal,
    col_scal,
    before,
    ext,
    applied,
    basis,
    table_sems,
    halo_send,
    halo_recv,
    send_sems,
    recv_sems,
):
    lines, columns = mask.shape
    channels = point_weight.shape[0]
    groups = lines // LINES
    double = 2 * kept
    row = lax.axis_index("row")
    col = lax.axis_index("col")
    grid_scale = math.sqrt(lines * col_count * columns * row_count)

    table_copies = [
        pltpu.make_async_copy(table_high, fwd_high, table_sems.at[0]),
        pltpu.make_async_copy(table_low, fwd_low, table_sems.at[1]),
        pltpu.make_async_copy(phases.at[row], phase, table_sems.at[2]),
    ]
    back_copies = [
        pltpu.make_async_copy(table_back, rhs_cols.at[g, pl.ds(0, double)], table_sems.at[3 + g])
        for g in range(groups)
    ]
    weight_copy = pltpu.make_async_copy(spectral_weight, weights, table_sems.at[3 + groups])
    for copy in [*table_copies, weight_copy, *back_copies]:
        copy.start()

    barrier = pltpu.get_barrier_semaphore()
    greeted = 0
    for d in range(1, row_count):
        pl.semaphore_signal(
            barrier, inc=1, device_id={"row": lax.rem(row + d, row_count)}, device_id_type=MESH
        )
        greeted += 1
    for d in range(1, col_count):
        pl.semaphore_signal(
            barrier, inc=1, device_id={"col": lax.rem(col + d, col_count)}, device_id_type=MESH
        )
        greeted += 1
    for dr in (1, row_count - 1):
        for dc in (1, col_count - 1):
            pl.semaphore_signal(
                barrier,
                inc=1,
                device_id={
                    "row": lax.rem(row + dr, row_count),
                    "col": lax.rem(col + dc, col_count),
                },
                device_id_type=MESH,
            )
            greeted += 1

    def spread(source, target, index, axis, me, count):
        for d in range(1, count):
            there = lax.rem(me + d, count)
            pltpu.make_async_remote_copy(
                src_ref=source(there),
                dst_ref=target.at[me],
                send_sem=send_sems.at[index],
                recv_sem=recv_sems.at[index],
                device_id={axis: there},
                device_id_type=MESH,
            ).start()

    def arrived(target, index, count, sems):
        whole = target.at[pl.ds(0, count - 1)]
        pltpu.make_async_copy(whole, whole, sems.at[index]).wait()

    def forward(out):
        spectrum = (
            jnp.dot(high[...], fwd_high[...], preferred_element_type=F32)
            + jnp.dot(high[...], fwd_low[...], preferred_element_type=F32)
            + jnp.dot(low[...], fwd_high[...], preferred_element_type=F32)
        )
        cosine, sine = phase[0:1, :kept], phase[0:1, kept:]
        re, im = spectrum[:, :kept], spectrum[:, kept:]
        out[:, :, 0:kept] = (re * cosine + im * sine).reshape(row_count, 8, kept)
        out[:, :, kept:double] = (im * cosine - re * sine).reshape(row_count, 8, kept)

    def unrotated(both):
        cosine, sine = phase[0:1, :kept], phase[0:1, kept:]
        re, im = both[:, :kept], both[:, kept:]
        return re * cosine - im * sine, im * cosine + re * sine

    def slab(g, j, value):
        rhs_cols[g, double + LINES * j : double + LINES * (j + 1), :] = value

    def field_slabs(g, j, value):
        top, rest = split(value)
        slab(g, j, top)
        slab(g, j + 1, rest)
        slab(g, j + 2, top)
        return top, rest

    def rows_of(g):
        return slice(LINES * g, LINES * (g + 1))

    def folded(x):
        total = jnp.zeros((8, 128), F32)
        for i in range(x.shape[0] // 8):
            for j in range(x.shape[1] // 128):
                total = total + x[8 * i : 8 * i + 8, 128 * j : 128 * j + 128]
        return total

    def scalar_tile(parts):
        place = lax.broadcasted_iota(jnp.int32, (8, 128), 0)
        tile = jnp.zeros((8, 128), F32)
        for i, part in enumerate(parts):
            tile = jnp.where(place == i, jnp.sum(part, axis=0, keepdims=True), tile)
        return tile

    for g in range(groups):
        lines_of = rows_of(g)
        kind = medium[lines_of, :]
        refractive = jnp.zeros((LINES, columns), F32)
        for level in range(refraction.shape[0]):
            refractive = jnp.where(kind == level, refraction[level], refractive)
        damping = 0.1 + mask[lines_of, :].astype(F32)
        damp_ref[lines_of, :] = damping
        scaled = wave_base * refractive
        wave_ref[lines_of, :] = scaled * scaled
        top, rest = field_slabs(g, 6, refractive)
        high[lines_of, :] = top
        low[lines_of, :] = rest
        top, rest = field_slabs(g, 9, damping)
        high[lines + LINES * g : lines + LINES * (g + 1), :] = top
        low[lines + LINES * g : lines + LINES * (g + 1), :] = rest
        ones = jnp.ones((LINES, columns), BF16)
        slab(g, 12, ones)
        slab(g, 13, ones)
        slab(g, 14, jnp.zeros_like(ones))
        slab(g, 15, jnp.zeros_like(ones))
    for copy in table_copies:
        copy.wait()
    forward(send_feat)
    pl.semaphore_wait(barrier, greeted)
    spread(lambda there: send_feat.at[there], got_feat, 0, "row", row, row_count)

    sources = source_rows.shape[0]
    place = lax.broadcasted_iota(jnp.int32, (sources, 128), 0)
    col_of = jnp.zeros((sources, 128), jnp.int32)
    for i in range(sources):
        col_of = jnp.where(place == i, source_cols[i] - columns * row, col_of)
    lane = lax.broadcasted_iota(jnp.int32, (sources, 128), 1)
    col_hits = jnp.concatenate(
        [jnp.where(col_of == lane + 128 * j, 1.0, 0.0) for j in range(columns // 128)], axis=1
    ).astype(BF16)
    place = lax.broadcasted_iota(jnp.int32, (lines, sources), 1)
    row_of = jnp.zeros((lines, sources), jnp.int32)
    for i in range(sources):
        row_of = jnp.where(place == i, source_rows[i] - lines * col, row_of)
    line_hits = jnp.where(
        row_of == lax.broadcasted_iota(jnp.int32, (lines, sources), 0), 1.0, 0.0
    ).astype(BF16)
    source_count = jnp.dot(line_hits, col_hits, preferred_element_type=F32)
    square = jnp.zeros((8, 128), F32)
    for g in range(groups):
        lines_of = rows_of(g)
        for p in range(2):
            field = forcing[p, lines_of, :]
            if p == 0:
                field = field + source_gain * source_count[lines_of, :]
            right_ref[p, lines_of, :] = field
            square = square + folded(field * field)
            top, rest = split(field)
            high[p * lines + LINES * g : p * lines + LINES * (g + 1), :] = top
            low[p * lines + LINES * g : p * lines + LINES * (g + 1), :] = rest
    def send_modes(step, tile):
        forward(send_wave.at[step])
        for r in range(row_count):
            send_wave[step, r, :, double:] = tile
        spread(
            lambda there: send_wave.at[step, there], got_wave.at[step], 2 + 3 * step, "row", row, row_count
        )

    send_modes(0, scalar_tile([square]))

    lift = jnp.concatenate(
        [lift_weight[...], lift_bias[...], jnp.zeros((3, channels), F32)], axis=0
    )
    lift_parts = three_way(lift)
    point = jnp.zeros((8, channels), F32)
    for part in lift_parts:
        point = point + jnp.dot(part, point_weight[...], preferred_element_type=F32)
    channel_row = lax.broadcasted_iota(jnp.int32, (8, channels), 0)
    point = point + jnp.where(channel_row == 4, layer_bias[...], 0.0)
    top, rest = split(point)
    wide = SLABS * LINES
    from_row = lax.broadcasted_iota(jnp.int32, (8, wide), 0)
    slab_of = lax.broadcasted_iota(jnp.int32, (8, wide), 1) // LINES
    first_slab = 3 * from_row
    pick_top = ((slab_of == first_slab) | ((slab_of == first_slab + 1) & (from_row < 4))) & (from_row < 5)
    pick_rest = ((slab_of == first_slab + 2) & (from_row < 4)) | ((slab_of == 13) & (from_row == 4))
    over_rows = (((0,), (0,)), ((), ()))
    spread_out = lax.dot_general(
        top.astype(F32), jnp.where(pick_top, 1.0, 0.0), over_rows, preferred_element_type=F32
    ) + lax.dot_general(
        rest.astype(F32), jnp.where(pick_rest, 1.0, 0.0), over_rows, preferred_element_type=F32
    )
    line_of = lax.broadcasted_iota(jnp.int32, (channels, wide), 1) % LINES
    for i in range(LINES):
        masked = jnp.where(line_of == i, spread_out, 0.0).astype(BF16)
        for g in range(groups):
            mixed[LINES * g + i, :, double:] = masked
    all_rows = LINES * channels
    tiles = jnp.where(
        lax.broadcasted_iota(jnp.int32, (channels, all_rows), 0)
        == lax.broadcasted_iota(jnp.int32, (channels, all_rows), 1) % channels,
        1.0,
        0.0,
    )
    across = lax.dot_general(
        project_weight[...].astype(F32), tiles, (((1,), (0,)), ((), ())), preferred_element_type=F32
    )
    own_line = (
        lax.broadcasted_iota(jnp.int32, (LINES, all_rows), 0)
        == lax.broadcasted_iota(jnp.int32, (LINES, all_rows), 1) // channels
    )
    for p in range(2):
        project_map[LINES * p : LINES * (p + 1), :] = jnp.where(
            own_line, across[p : p + 1, :], 0.0
        ).astype(BF16)

    mode_of = lax.broadcasted_iota(jnp.int32, (1, 128), 1)
    weight_copy.wait()
    for part in range(2):
        for ob in range(channels // 16):
            outs = pl.ds(16 * ob, 16)
            for kc in range(kept // 128):
                some = pl.ds(128 * kc, 128)
                used = 5 if kc == 0 else 4

                def one_channel(c, sums):
                    weight = weights[part, c, outs, some].astype(F32)
                    factors = [lift_scalars[g, c] for g in range(4)] + [bias_scalars[c]]
                    return tuple(x + f * weight for x, f in zip(sums, factors))

                sums = lax.fori_loop(
                    0, channels, one_channel, (jnp.zeros((16, 128), F32),) * used, unroll=8
                )
                twice = jnp.where(mode_of == 0, 1.0, 2.0) if kc == 0 else 2.0
                for g in range(4):
                    mode_map[part, g, outs, some] = sums[g] * twice
                anchor = jnp.where(mode_of == 0, math.sqrt(columns * row_count), 0.0)
                mode_map[part, 4, outs, some] = (
                    sums[4] * anchor if kc == 0 else jnp.zeros((16, 128), F32)
                )

    def reduced(got, source):
        got[row] = source[row]
        total = got[0]
        for r in range(1, row_count):
            total = total + got[r]
        return total

    arrived(got_feat, 0, row_count, recv_sems)
    all_feat[row] = reduced(got_feat, send_feat)
    spread(lambda there: all_feat.at[row], all_feat, 1, "row", row, row_count)

    def wave_reduce(step):
        index = 2 + 3 * step
        arrived(got_wave.at[step], index, row_count, recv_sems)
        total = reduced(got_wave.at[step], send_wave.at[step])
        all_wave[step, row] = total[:, :double]
        spread(
            lambda there: all_wave.at[step, row], all_wave.at[step], index + 1, "row", row, row_count
        )
        col_scal[step, col] = total[:, double:]
        spread(
            lambda there: col_scal.at[step, col], col_scal.at[step], index + 2, "col", col, col_count
        )

    def col_total(step):
        arrived(col_scal.at[step], 4 + 3 * step, col_count, recv_sems)
        total = col_scal[step, 0]
        for r in range(1, col_count):
            total = total + col_scal[step, r]
        return jnp.sum(total, axis=1, keepdims=True)

    def mix_lines(first, count, kc, ob, channels_in, bias, source, store):
        low_k, high_k = pl.ds(128 * kc, 128), pl.ds(kept + 128 * kc, 128)
        outs = pl.ds(16 * ob, 16)
        maps = [(mode_map[0, g, outs, low_k], mode_map[1, g, outs, low_k]) for g in channels_in]
        start = (mode_map[0, 4, outs, low_k], mode_map[1, 4, outs, low_k]) if bias else None
        for block in range(count // 8):
            top = first + 8 * block
            parts = [
                (modes[g, pl.ds(top, 8), low_k], modes[g, pl.ds(top, 8), high_k]) for g in channels_in
            ]
            for i in range(8):
                line = top + i
                if bias:
                    re, im = start
                else:
                    re, im = source[line, outs, low_k], source[line, outs, high_k]
                for (mode_re, mode_im), (map_re, map_im) in zip(parts, maps):
                    one_re, one_im = mode_re[i : i + 1], mode_im[i : i + 1]
                    re = re + (map_re * one_re - map_im * one_im)
                    im = im + (map_re * one_im + map_im * one_re)
                store[line, outs, low_k] = re.astype(store.dtype)
                store[line, outs, high_k] = im.astype(store.dtype)

    def mix_fixed():
        for kc in range(kept // 128):
            for ob in range(channels // 16):

                def eight_lines(block, carry):
                    first = pl.multiple_of(8 * block, 8)
                    mix_lines(first, 8, kc, ob, (2, 3), True, None, fixed)
                    return carry

                lax.fori_loop(0, lines // 8, eight_lines, 0)

    def mix_group(g):
        for kc in range(kept // 128):
            for ob in range(channels // 16):
                mix_lines(LINES * g, LINES, kc, ob, (0, 1), False, fixed, mixed)

    def layer(step):
        last = columns // PIECE - 1
        edges = [(g, n) for g in range(groups) for n in sorted({0, last})]
        ends = [(g, n) for g in sorted({0, groups - 1}) for n in range(1, last)]
        inside = [(g, n) for g in range(1, groups - 1) for n in range(1, last)]
        order = edges + ends + inside
        copies = halo_copies(step)

        def multiply(g, n, slot):
            left = mixed[LINES * g : LINES * (g + 1)].reshape(LINES * channels, double + SLABS * LINES)
            before[slot] = jnp.dot(
                left, rhs_cols[g, :, PIECE * n : PIECE * (n + 1)], preferred_element_type=F32
            )

        def finish(g, n, slot):
            active = gelu(before[slot]).astype(BF16)
            out = jnp.dot(project_map[...], active, preferred_element_type=F32)
            first = 8 + LINES * g
            place = slice(128 + PIECE * n, 128 + PIECE * (n + 1))
            ext[step, 0, first : first + LINES, place] = out[:LINES]
            ext[step, 1, first : first + LINES, place] = out[LINES:]

        mix_group(0)
        for t in range(len(order) + 1):
            if t < len(order):
                g, n = order[t]
                multiply(g, n, t % 2)
                if t < len(edges) and n == 0 and g + 1 < groups:
                    mix_group(g + 1)
            if t > 0:
                finish(*order[t - 1], (t - 1) % 2)
            if t == len(edges):
                for i in (0, 1, 4, 5, 6, 7):
                    copies[i].start()
            if t == len(edges) + len(ends):
                for i in (2, 3):
                    copies[i].start()

    def halo_copies(step):
        tall, across_all = pl.ds(8, lines), pl.ds(128, columns)
        line_ends = {
            1: (pl.ds(lines, 8), pl.ds(0, 8)),
            -1: (pl.ds(8, 8), pl.ds(8 + lines, 8)),
            0: (tall, tall),
        }
        col_ends = {
            1: (pl.ds(columns, 128), pl.ds(0, 128)),
            -1: (pl.ds(128, 128), pl.ds(128 + columns, 128)),
            0: (across_all, across_all),
        }
        copies = []
        for i, (dr, dc) in enumerate(
            [(1, 0), (-1, 0), (0, 1), (0, -1), (1, 1), (1, -1), (-1, 1), (-1, -1)]
        ):
            here_l, there_l = line_ends[dc]
            here_c, there_c = col_ends[dr]
            copies.append(
                pltpu.make_async_remote_copy(
                    src_ref=ext.at[step, :, here_l, here_c],
                    dst_ref=ext.at[step, :, there_l, there_c],
                    send_sem=halo_send.at[step, i],
                    recv_sem=halo_recv.at[step, i],
                    device_id={
                        "row": lax.rem(row + dr + row_count, row_count),
                        "col": lax.rem(col + dc + col_count, col_count),
                    },
                    device_id_type=MESH,
                )
            )
        return copies

    def halos(step):
        for copy in halo_copies(step):
            copy.wait()
        view = ext.at[step]

        @pl.when(row == 0)
        def _():
            view[:, :, 0:128] = jnp.zeros((2, lines + 16, 128), F32)

        @pl.when(row == row_count - 1)
        def _():
            view[:, :, 128 + columns :] = jnp.zeros((2, lines + 16, 128), F32)

        @pl.when(col == 0)
        def _():
            view[:, 0:8, :] = jnp.zeros((2, 8, columns + 256), F32)

        @pl.when(col == col_count - 1)
        def _():
            view[:, 8 + lines :, :] = jnp.zeros((2, 8, columns + 256), F32)

    def operate(step, g):
        laps, fields = [], []
        for p in range(2):
            first = 8 + LINES * g
            beside = (
                ext[step, p, first - 1 : first - 1 + LINES, :]
                + ext[step, p, first + 1 : first + 1 + LINES, :]
            )
            centre = ext[step, p, first : first + LINES, :]
            both = 4.0 * centre + beside
            width = columns + 256
            around = pltpu.roll(both, 1, 1) + pltpu.roll(both, width - 1, 1)
            total = (4.0 * beside - 20.0 * centre + around) * (1.0 / 6.0)
            laps.append(total[:, 128 : 128 + columns])
            fields.append(centre[:, 128 : 128 + columns])
        wave, damping = wave_ref[rows_of(g), :], damp_ref[rows_of(g), :]
        real = -laps[0] - wave * (fields[0] + damping * fields[1])
        imag = -laps[1] - wave * (fields[1] - damping * fields[0])
        return real, imag

    def pair(first, second):
        return (
            folded(first[0] * second[0] + first[1] * second[1]),
            folded(first[0] * second[1] - first[1] * second[0]),
        )

    def add(a, b):
        return [x + y for x, y in zip(a, b)]

    wave_reduce(0)
    arrived(all_feat, 1, row_count, recv_sems)
    re, im = unrotated(all_feat[...].reshape(2 * lines, double))
    for g in range(2):
        modes[2 + g, :, :kept] = re[g * lines : (g + 1) * lines]
        modes[2 + g, :, kept:] = im[g * lines : (g + 1) * lines]
    mix_fixed()
    for copy in back_copies:
        copy.wait()

    arrived(all_wave.at[0], 3, row_count, recv_sems)
    total_square = col_total(0)[0:1, :]
    beta = jnp.sqrt(total_square + norm_eps)
    inverse_beta = 1.0 / beta
    re, im = unrotated(all_wave[0].reshape(2 * lines, double))
    for p in range(2):
        modes[p, :, :kept] = re[p * lines : (p + 1) * lines] * (grid_scale * inverse_beta)
        modes[p, :, kept:] = im[p * lines : (p + 1) * lines] * (grid_scale * inverse_beta)
    for g in range(groups):
        for p in range(2):
            field_slabs(g, 3 * p, right_ref[p, rows_of(g), :] * (grid_scale * inverse_beta))
    layer(0)
    halos(0)
    sums = [jnp.zeros((8, 128), F32)] * 3
    for g in range(groups):
        lines_of = rows_of(g)
        result = operate(0, g)
        for p in range(2):
            applied[0, p, lines_of, :] = result[p]
            top, rest = split(result[p])
            high[p * lines + LINES * g : p * lines + LINES * (g + 1), :] = top
            low[p * lines + LINES * g : p * lines + LINES * (g + 1), :] = rest
        start = (right_ref[0, lines_of, :], right_ref[1, lines_of, :])
        square = folded(result[0] * result[0] + result[1] * result[1])
        sums = add(sums, (*pair(start, result), square))
    send_modes(1, scalar_tile(sums))
    wave_reduce(1)
    arrived(all_wave.at[1], 6, row_count, recv_sems)
    totals = col_total(1)
    unit_square = total_square * inverse_beta * inverse_beta
    a = (totals[0:1, :] * inverse_beta, totals[1:2, :] * inverse_beta)
    a_square = a[0] * a[0] + a[1] * a[1]
    rest_square = jnp.maximum(totals[2:3, :] - a_square * (2.0 - unit_square), 0.0)
    c = jnp.sqrt(rest_square + norm_eps)
    inverse_c = 1.0 / c
    a_over = (a[0] * inverse_beta, a[1] * inverse_beta)

    def next_vector(w, v):
        scaled = cmul(a_over, v)
        return (w[0] - scaled[0]) * inverse_c, (w[1] - scaled[1]) * inverse_c

    old, new = (all_wave[i].reshape(2 * lines, double) for i in range(2))
    planes = next_vector((new[:lines], new[lines:]), (old[:lines], old[lines:]))
    for p in range(2):
        re, im = unrotated(planes[p])
        modes[p, :, :kept] = re * grid_scale
        modes[p, :, kept:] = im * grid_scale
    for g in range(groups):
        lines_of = rows_of(g)
        vector = next_vector(
            (applied[0, 0, lines_of, :], applied[0, 1, lines_of, :]),
            (right_ref[0, lines_of, :], right_ref[1, lines_of, :]),
        )
        for p in range(2):
            basis[p, lines_of, :] = vector[p]
            field_slabs(g, 3 * p, vector[p] * grid_scale)
    layer(1)
    halos(1)
    sums = [jnp.zeros((8, 128), F32)] * 5
    for g in range(groups):
        lines_of = rows_of(g)
        result = operate(1, g)
        for p in range(2):
            applied[1, p, lines_of, :] = result[p]
        start = (right_ref[0, lines_of, :], right_ref[1, lines_of, :])
        vector = (basis[0, lines_of, :], basis[1, lines_of, :])
        square = folded(result[0] * result[0] + result[1] * result[1])
        sums = add(sums, (*pair(start, result), *pair(vector, result), square))
    got_scal[row] = scalar_tile(sums)
    spread(lambda there: got_scal.at[row], got_scal, 8, "row", row, row_count)
    arrived(got_scal, 8, row_count, recv_sems)
    total = got_scal[0]
    for r in range(1, row_count):
        total = total + got_scal[r]
    col_scal[2, col] = total
    spread(lambda there: col_scal.at[2, col], col_scal.at[2], 9, "col", col, col_count)
    arrived(col_scal.at[2], 9, col_count, recv_sems)
    total = col_scal[2, 0]
    for r in range(1, col_count):
        total = total + col_scal[2, r]
    totals = jnp.sum(total, axis=1, keepdims=True)
    b = (totals[0:1, :] * inverse_beta, totals[1:2, :] * inverse_beta)
    d = (totals[2:3, :], totals[3:4, :])
    b_square = b[0] * b[0] + b[1] * b[1]
    d_square = d[0] * d[0] + d[1] * d[1]
    second_square = rest_square * inverse_c * inverse_c
    overlap = (norm_eps * inverse_beta * inverse_beta) * inverse_c
    between = conj_cmul(b, d)
    between = between[0] * a[0] - between[1] * a[1]
    last_square = (
        totals[4:5, :]
        - b_square * (2.0 - unit_square)
        - d_square * (2.0 - second_square)
        + 2.0 * overlap * between
    )
    e = jnp.sqrt(jnp.maximum(last_square, 0.0) + norm_eps)
    y0, y1 = small_solve(beta, a, b, c, d, e)
    for g in range(groups):
        lines_of = rows_of(g)
        inner = slice(8 + LINES * g, 8 + LINES * (g + 1))
        z0, z1, w0, w1 = (
            [ext[0, p, inner, 128 : 128 + columns] for p in range(2)],
            [ext[1, p, inner, 128 : 128 + columns] for p in range(2)],
            [applied[0, p, lines_of, :] for p in range(2)],
            [applied[1, p, lines_of, :] for p in range(2)],
        )
        z0, z1, w0, w1 = cmul(y0, z0), cmul(y1, z1), cmul(y0, w0), cmul(y1, w1)
        for p in range(2):
            solution_ref[p, lines_of, :] = z0[p] + z1[p]
            residual_ref[p, lines_of, :] = right_ref[p, lines_of, :] - w0[p] - w1[p]

    arrived(got_feat, 0, row_count, send_sems)
    arrived(all_feat, 1, row_count, send_sems)
    for step in range(2):
        arrived(got_wave.at[step], 2 + 3 * step, row_count, send_sems)
        arrived(all_wave.at[step], 3 + 3 * step, row_count, send_sems)
        arrived(col_scal.at[step], 4 + 3 * step, col_count, send_sems)
    arrived(got_scal, 8, row_count, send_sems)
    arrived(col_scal.at[2], 9, col_count, send_sems)


def deliver(solution_in, residual_in, solution_out, residual_out, held, sems):
    moves = []
    for i, (source, target) in enumerate(
        [(solution_in, solution_out), (residual_in, residual_out)]
    ):
        for p in range(2):
            k = 2 * i + p
            arrive = pltpu.make_async_copy(source.at[p], held.at[k], sems.at[0, k])
            leave = pltpu.make_async_copy(held.at[k], target.at[p], sems.at[1, k])
            moves.append((arrive, leave))
    for arrive, _ in moves:
        arrive.start()
    for arrive, leave in moves:
        arrive.wait()
        leave.start()
    for _, leave in moves:
        leave.wait()


def shards(
    row_count,
    col_count,
    kept,
    forcing,
    medium_index,
    absorbing_mask,
    source_rows,
    source_cols,
    refraction,
    lift_weight,
    lift_bias,
    spectral_weight,
    point_weight,
    layer_bias,
    project_weight,
):
    _, lines, columns = forcing.shape
    channels = point_weight.shape[0]
    grid_cols = columns * row_count
    groups = lines // LINES
    double = 2 * kept
    assert row_count * 8 == 2 * lines

    table_high, table_low, table_back = base_tables(columns, kept, grid_cols)
    phases = phase_table(row_count, kept)

    field = jax.ShapeDtypeStruct((2, lines, columns), F32)
    vmem = pl.BlockSpec(memory_space=pltpu.VMEM)
    smem = pl.BlockSpec(memory_space=pltpu.SMEM)
    hbm = pl.BlockSpec(memory_space=pl.ANY)
    dma = pltpu.SemaphoreType.DMA
    results = pl.pallas_call(
        functools.partial(kernel, row_count, col_count, kept),
        out_shape=(field, field),
        in_specs=[vmem] * 3 + [smem] * 5 + [vmem] * 2 + [hbm] + [vmem] * 3 + [hbm] * 4,
        out_specs=(vmem, vmem),
        scratch_shapes=[
            pltpu.VMEM((columns, double), BF16),
            pltpu.VMEM((columns, double), BF16),
            pltpu.VMEM((8, double), F32),
            pltpu.VMEM((2, channels, channels, kept), BF16),
            pltpu.VMEM((2, 5, channels, kept), F32),
            pltpu.VMEM((2 * LINES, LINES * channels), BF16),
            pltpu.VMEM((lines, columns), F32),
            pltpu.VMEM((lines, columns), F32),
            pltpu.VMEM((2, lines, columns), F32),
            pltpu.VMEM((groups, double + SLABS * LINES, columns), BF16),
            pltpu.VMEM((lines, channels, double + SLABS * LINES), BF16),
            pltpu.VMEM((lines, channels, double), F32),
            pltpu.VMEM((4, lines, double), F32),
            pltpu.VMEM((2 * lines, columns), BF16),
            pltpu.VMEM((2 * lines, columns), BF16),
            pltpu.VMEM((row_count, 8, double), F32),
            pltpu.VMEM((row_count, 8, double), F32),
            pltpu.VMEM((row_count, 8, double), F32),
            pltpu.VMEM((2, row_count, 8, double + 128), F32),
            pltpu.VMEM((2, row_count, 8, double + 128), F32),
            pltpu.VMEM((2, row_count, 8, double), F32),
            pltpu.VMEM((row_count, 8, 128), F32),
            pltpu.VMEM((3, col_count, 8, 128), F32),
            pltpu.VMEM((2, LINES * channels, PIECE), F32),
            pltpu.VMEM((2, 2, lines + 16, columns + 256), F32),
            pltpu.VMEM((2, 2, lines, columns), F32),
            pltpu.VMEM((2, lines, columns), F32),
            dma((4 + groups,)),
            dma((2, 8)),
            dma((2, 8)),
            dma((10,)),
            dma((10,)),
        ],
        compiler_params=pltpu.CompilerParams(
            collective_id=0, has_side_effects=True, vmem_limit_bytes=56 * 2**20
        ),
        name="krylov",
    )(
        forcing,
        medium_index,
        absorbing_mask,
        source_rows,
        source_cols,
        refraction,
        lift_weight,
        lift_bias,
        lift_weight,
        lift_bias.reshape(1, -1),
        spectral_weight.transpose(0, 2, 3, 1),
        point_weight,
        layer_bias.reshape(1, -1),
        project_weight.T,
        table_high,
        table_low,
        table_back,
        phases,
    )
    return pl.pallas_call(
        deliver,
        out_shape=(field, field),
        in_specs=[hbm] * 2,
        out_specs=[hbm] * 2,
        scratch_shapes=[pltpu.VMEM((4, lines, columns), F32), dma((2, 4))],
        name="deliver",
    )(*results)


def solution(mesh):
    return jax.shard_map(
        functools.partial(shards, mesh.shape["row"], mesh.shape["col"], K),
        mesh=mesh,
        in_specs=(
            P(None, "col", "row"),
            P("col", "row"),
            P("col", "row"),
            P(),
            P(),
            P(),
            P(),
            P(),
            P(),
            P(),
            P(),
            P(),
        ),
        out_specs=(P(None, "col", "row"), P(None, "col", "row")),
        check_vma=False,
    )
```

```python
import functools
import math

import jax
import jax.numpy as jnp
import numpy as np
import ml_dtypes
from jax import lax
from jax.experimental import pallas as pl
from jax.experimental.pallas import tpu as pltpu
from jax.sharding import PartitionSpec as P

K = 256

wave_base = 0.23
source_gain = 8.0
norm_eps = 1e-06

MESH = pl.DeviceIdType.MESH
F32 = jnp.float32
BF16 = jnp.bfloat16
LINES = 16
SLABS = 16
PIECE = 256


def forward_tables(tile_cols, kept_modes, grid_cols):
    positions = np.arange(tile_cols, dtype=np.int64)
    mode_index = np.arange(kept_modes, dtype=np.int64)
    angles = (positions[:, None] * mode_index[None, :] % grid_cols) * (2.0 * math.pi / grid_cols)
    scale = 1.0 / math.sqrt(grid_cols)
    table = np.concatenate([np.cos(angles), -np.sin(angles)], axis=1) * scale
    high = table.astype(np.float32).astype(ml_dtypes.bfloat16)
    low = (table - high.astype(np.float64)).astype(np.float32).astype(ml_dtypes.bfloat16)
    return high, low


def back_tables(tile_cols, kept_modes, grid_cols):
    odd = 2 * np.arange(tile_cols // 2, dtype=np.int64) + 1
    mode_index = np.arange(kept_modes, dtype=np.int64)
    angles = (mode_index[:, None] * odd[None, :] % (2 * grid_cols)) * (math.pi / grid_cols)
    scale = 1.0 / math.sqrt(grid_cols)
    table = np.stack([np.cos(angles), -np.sin(angles)]) * scale
    return table.astype(np.float32).astype(ml_dtypes.bfloat16)


def phase_table(row_count, tile_cols, kept_modes):
    grid_cols = row_count * tile_cols
    first = 2 * tile_cols * np.arange(row_count, dtype=np.int64)
    mode_index = np.arange(kept_modes, dtype=np.int64)
    parts = []
    for place in (first, first + tile_cols - 1):
        angles = (place[:, None] * mode_index[None, :] % (2 * grid_cols)) * (math.pi / grid_cols)
        parts += [np.cos(angles), np.sin(angles)]
    table = np.concatenate(parts, axis=1).astype(np.float32)
    return np.ascontiguousarray(np.broadcast_to(table[:, None, :], (row_count, 8, 4 * kept_modes)))


def split(x):
    high = x.astype(BF16)
    return high, (x - high.astype(F32)).astype(BF16)


def three_way(x):
    high, low = split(x)
    return high, low, (x - high.astype(F32) - low.astype(F32)).astype(BF16)


def gelu(x):
    return 0.5 * x * (1.0 + lax.erf(x * math.sqrt(0.5)))


def cmul(a, b):
    return a[0] * b[0] - a[1] * b[1], a[0] * b[1] + a[1] * b[0]


def conj_cmul(a, b):
    return a[0] * b[0] + a[1] * b[1], a[0] * b[1] - a[1] * b[0]


def small_solve(beta, a, b, c, d, e):
    gram_first = a[0] * a[0] + a[1] * a[1] + c * c
    gram_second = b[0] * b[0] + b[1] * b[1] + d[0] * d[0] + d[1] * d[1] + e * e
    cross = conj_cmul(a, b)
    cross = (cross[0] + c * d[0], cross[1] + c * d[1])
    ad = cmul(a, d)
    minor = (ad[0] - b[0] * c, ad[1] - b[1] * c)
    determinant = (
        minor[0] * minor[0]
        + minor[1] * minor[1]
        + (a[0] * a[0] + a[1] * a[1]) * e * e
        + c * c * e * e
    )
    first = (beta * a[0], -beta * a[1])
    second = (beta * b[0], -beta * b[1])
    t = cmul(cross, second)
    y0 = ((gram_second * first[0] - t[0]) / determinant, (gram_second * first[1] - t[1]) / determinant)
    t = conj_cmul(cross, first)
    y1 = ((gram_first * second[0] - t[0]) / determinant, (gram_first * second[1] - t[1]) / determinant)
    return y0, y1


def kernel(
    row_count,
    col_count,
    kept,
    forcing,
    medium,
    mask,
    source_rows,
    source_cols,
    refraction,
    lift_scalars,
    bias_scalars,
    lift_weight,
    lift_bias,
    spectral_weight,
    point_weight,
    layer_bias,
    project_weight,
    table_high,
    table_low,
    table_back,
    phases,
    solution_ref,
    residual_ref,
    fwd_high,
    fwd_low,
    phase,
    weights,
    mode_map,
    project_map,
    wave_ref,
    damp_ref,
    right_ref,
    even_cols,
    odd_cols,
    mixed,
    fixed,
    modes,
    high,
    low,
    send_feat,
    got_feat,
    all_feat,
    send_wave,
    got_wave,
    all_wave,
    got_scal,
    col_scal,
    before,
    ext,
    applied,
    basis,
    table_sems,
    halo_send,
    halo_recv,
    send_sems,
    recv_sems,
):
    lines, columns = mask.shape
    channels = point_weight.shape[0]
    groups = lines // LINES
    double = 2 * kept
    wide = SLABS * LINES
    half = columns // 2
    row = lax.axis_index("row")
    col = lax.axis_index("col")
    grid_scale = math.sqrt(lines * col_count * columns * row_count)

    table_copies = [
        pltpu.make_async_copy(table_high, fwd_high, table_sems.at[0]),
        pltpu.make_async_copy(table_low, fwd_low, table_sems.at[1]),
        pltpu.make_async_copy(phases.at[row], phase, table_sems.at[2]),
    ]
    back_copies = [
        copy
        for g in range(groups)
        for copy in (
            pltpu.make_async_copy(table_back.at[0], even_cols.at[g, pl.ds(0, kept)], table_sems.at[4 + 2 * g]),
            pltpu.make_async_copy(table_back.at[1], odd_cols.at[g, pl.ds(wide, kept)], table_sems.at[5 + 2 * g]),
        )
    ]
    weight_copy = pltpu.make_async_copy(spectral_weight, weights, table_sems.at[3])
    for copy in [*table_copies, weight_copy, *back_copies]:
        copy.start()

    barrier = pltpu.get_barrier_semaphore()
    greeted = 0
    for d in range(1, row_count):
        pl.semaphore_signal(
            barrier, inc=1, device_id={"row": lax.rem(row + d, row_count)}, device_id_type=MESH
        )
        greeted += 1
    for d in range(1, col_count):
        pl.semaphore_signal(
            barrier, inc=1, device_id={"col": lax.rem(col + d, col_count)}, device_id_type=MESH
        )
        greeted += 1
    for dr in (1, row_count - 1):
        for dc in (1, col_count - 1):
            pl.semaphore_signal(
                barrier,
                inc=1,
                device_id={
                    "row": lax.rem(row + dr, row_count),
                    "col": lax.rem(col + dc, col_count),
                },
                device_id_type=MESH,
            )
            greeted += 1

    def spread(source, target, index, axis, me, count):
        for d in range(1, count):
            there = lax.rem(me + d, count)
            pltpu.make_async_remote_copy(
                src_ref=source(there),
                dst_ref=target.at[me],
                send_sem=send_sems.at[index],
                recv_sem=recv_sems.at[index],
                device_id={axis: there},
                device_id_type=MESH,
            ).start()

    def arrived(target, index, count, sems):
        whole = target.at[pl.ds(0, count - 1)]
        pltpu.make_async_copy(whole, whole, sems.at[index]).wait()

    def forward(out):
        spectrum = (
            jnp.dot(high[...], fwd_high[...], preferred_element_type=F32)
            + jnp.dot(high[...], fwd_low[...], preferred_element_type=F32)
            + jnp.dot(low[...], fwd_high[...], preferred_element_type=F32)
        )
        cosine, sine = phase[0:1, :kept], phase[0:1, kept:double]
        re, im = spectrum[:, :kept], spectrum[:, kept:]
        out[:, :, 0:kept] = (re * cosine + im * sine).reshape(row_count, 8, kept)
        out[:, :, kept:double] = (im * cosine - re * sine).reshape(row_count, 8, kept)

    def unrotated(both):
        cosine, sine = phase[0:1, double : double + kept], phase[0:1, double + kept :]
        re, im = both[:, :kept], both[:, kept:]
        return re * cosine - im * sine, im * cosine + re * sine

    flip = jnp.where(
        lax.broadcasted_iota(jnp.int32, (128, 128), 0)
        + lax.broadcasted_iota(jnp.int32, (128, 128), 1)
        == 127,
        1.0,
        0.0,
    ).astype(BF16)

    def reversed_lanes(x):
        height, blocks = x.shape[0], x.shape[1] // 128
        parts = [
            part[:, 128 * i : 128 * i + 128] for part in three_way(x) for i in reversed(range(blocks))
        ]
        turned = jnp.dot(jnp.concatenate(parts, axis=0), flip, preferred_element_type=F32)
        pieces = turned.reshape(3, blocks, height, 128)
        total = pieces[0] + pieces[1] + pieces[2]
        return jnp.concatenate([total[i] for i in range(blocks)], axis=1)

    def slab(g, j, even, odd):
        even_cols[g, kept + LINES * j : kept + LINES * (j + 1), :] = even
        odd_cols[g, LINES * j : LINES * (j + 1), :] = odd

    def field_slabs(g, j, value):
        right, left = value[:, half:], reversed_lanes(value[:, :half])
        even, odd = split(0.5 * (right + left)), split(0.5 * (right - left))
        slab(g, j, even[0], odd[0])
        slab(g, j + 1, even[1], odd[1])
        slab(g, j + 2, even[0], odd[0])

    def rows_of(g):
        return slice(LINES * g, LINES * (g + 1))

    def folded(x):
        total = jnp.zeros((8, 128), F32)
        for i in range(x.shape[0] // 8):
            for j in range(x.shape[1] // 128):
                total = total + x[8 * i : 8 * i + 8, 128 * j : 128 * j + 128]
        return total

    def scalar_tile(parts):
        place = lax.broadcasted_iota(jnp.int32, (8, 128), 0)
        tile = jnp.zeros((8, 128), F32)
        for i, part in enumerate(parts):
            tile = jnp.where(place == i, jnp.sum(part, axis=0, keepdims=True), tile)
        return tile

    for g in range(groups):
        lines_of = rows_of(g)
        kind = medium[lines_of, :]
        refractive = jnp.zeros((LINES, columns), F32)
        for level in range(refraction.shape[0]):
            refractive = jnp.where(kind == level, refraction[level], refractive)
        damping = 0.1 + mask[lines_of, :].astype(F32)
        damp_ref[lines_of, :] = damping
        scaled = wave_base * refractive
        wave_ref[lines_of, :] = scaled * scaled
        field_slabs(g, 6, refractive)
        top, rest = split(refractive)
        high[lines_of, :] = top
        low[lines_of, :] = rest
        field_slabs(g, 9, damping)
        top, rest = split(damping)
        high[lines + LINES * g : lines + LINES * (g + 1), :] = top
        low[lines + LINES * g : lines + LINES * (g + 1), :] = rest
        ones = jnp.ones((LINES, half), BF16)
        zeros = jnp.zeros_like(ones)
        slab(g, 12, ones, zeros)
        slab(g, 13, ones, zeros)
        slab(g, 14, zeros, zeros)
        slab(g, 15, zeros, zeros)
    for copy in table_copies:
        copy.wait()
    forward(send_feat)
    pl.semaphore_wait(barrier, greeted)
    spread(lambda there: send_feat.at[there], got_feat, 0, "row", row, row_count)

    sources = source_rows.shape[0]
    place = lax.broadcasted_iota(jnp.int32, (sources, 128), 0)
    col_of = jnp.zeros((sources, 128), jnp.int32)
    for i in range(sources):
        col_of = jnp.where(place == i, source_cols[i] - columns * row, col_of)
    lane = lax.broadcasted_iota(jnp.int32, (sources, 128), 1)
    col_hits = jnp.concatenate(
        [jnp.where(col_of == lane + 128 * j, 1.0, 0.0) for j in range(columns // 128)], axis=1
    ).astype(BF16)
    place = lax.broadcasted_iota(jnp.int32, (lines, sources), 1)
    row_of = jnp.zeros((lines, sources), jnp.int32)
    for i in range(sources):
        row_of = jnp.where(place == i, source_rows[i] - lines * col, row_of)
    line_hits = jnp.where(
        row_of == lax.broadcasted_iota(jnp.int32, (lines, sources), 0), 1.0, 0.0
    ).astype(BF16)
    source_count = jnp.dot(line_hits, col_hits, preferred_element_type=F32)
    square = jnp.zeros((8, 128), F32)
    for g in range(groups):
        lines_of = rows_of(g)
        for p in range(2):
            field = forcing[p, lines_of, :]
            if p == 0:
                field = field + source_gain * source_count[lines_of, :]
            right_ref[p, lines_of, :] = field
            square = square + folded(field * field)
            top, rest = split(field)
            high[p * lines + LINES * g : p * lines + LINES * (g + 1), :] = top
            low[p * lines + LINES * g : p * lines + LINES * (g + 1), :] = rest
    def send_modes(step, tile):
        forward(send_wave.at[step])
        for r in range(row_count):
            send_wave[step, r, :, double:] = tile
        spread(
            lambda there: send_wave.at[step, there], got_wave.at[step], 2 + 3 * step, "row", row, row_count
        )

    send_modes(0, scalar_tile([square]))

    lift = jnp.concatenate(
        [lift_weight[...], lift_bias[...], jnp.zeros((3, channels), F32)], axis=0
    )
    lift_parts = three_way(lift)
    point = jnp.zeros((8, channels), F32)
    for part in lift_parts:
        point = point + jnp.dot(part, point_weight[...], preferred_element_type=F32)
    channel_row = lax.broadcasted_iota(jnp.int32, (8, channels), 0)
    point = point + jnp.where(channel_row == 4, layer_bias[...], 0.0)
    top, rest = split(point)
    from_row = lax.broadcasted_iota(jnp.int32, (8, wide), 0)
    slab_of = lax.broadcasted_iota(jnp.int32, (8, wide), 1) // LINES
    first_slab = 3 * from_row
    pick_top = ((slab_of == first_slab) | ((slab_of == first_slab + 1) & (from_row < 4))) & (from_row < 5)
    pick_rest = ((slab_of == first_slab + 2) & (from_row < 4)) | ((slab_of == 13) & (from_row == 4))
    over_rows = (((0,), (0,)), ((), ()))
    spread_out = lax.dot_general(
        top.astype(F32), jnp.where(pick_top, 1.0, 0.0), over_rows, preferred_element_type=F32
    ) + lax.dot_general(
        rest.astype(F32), jnp.where(pick_rest, 1.0, 0.0), over_rows, preferred_element_type=F32
    )
    line_of = lax.broadcasted_iota(jnp.int32, (channels, wide), 1) % LINES
    for i in range(LINES):
        masked = jnp.where(line_of == i, spread_out, 0.0).astype(BF16)
        for g in range(groups):
            mixed[LINES * g + i, :, kept : kept + wide] = masked
    all_rows = LINES * channels
    tiles = jnp.where(
        lax.broadcasted_iota(jnp.int32, (channels, all_rows), 0)
        == lax.broadcasted_iota(jnp.int32, (channels, all_rows), 1) % channels,
        1.0,
        0.0,
    )
    across = lax.dot_general(
        project_weight[...].astype(F32), tiles, (((1,), (0,)), ((), ())), preferred_element_type=F32
    )
    own_line = (
        lax.broadcasted_iota(jnp.int32, (LINES, all_rows), 0)
        == lax.broadcasted_iota(jnp.int32, (LINES, all_rows), 1) // channels
    )
    for p in range(2):
        project_map[LINES * p : LINES * (p + 1), :] = jnp.where(
            own_line, across[p : p + 1, :], 0.0
        ).astype(BF16)

    mode_of = lax.broadcasted_iota(jnp.int32, (1, 128), 1)
    weight_copy.wait()
    for part in range(2):
        for ob in range(channels // 16):
            outs = pl.ds(16 * ob, 16)
            for kc in range(kept // 128):
                some = pl.ds(128 * kc, 128)
                used = 5 if kc == 0 else 4

                def one_channel(c, sums):
                    weight = weights[part, c, outs, some].astype(F32)
                    factors = [lift_scalars[g, c] for g in range(4)] + [bias_scalars[c]]
                    return tuple(x + f * weight for x, f in zip(sums, factors))

                sums = lax.fori_loop(
                    0, channels, one_channel, (jnp.zeros((16, 128), F32),) * used, unroll=8
                )
                twice = jnp.where(mode_of == 0, 1.0, 2.0) if kc == 0 else 2.0
                for g in range(4):
                    mode_map[part, g, outs, some] = sums[g] * twice
                anchor = jnp.where(mode_of == 0, math.sqrt(columns * row_count), 0.0)
                mode_map[part, 4, outs, some] = (
                    sums[4] * anchor if kc == 0 else jnp.zeros((16, 128), F32)
                )

    def reduced(got, source):
        got[row] = source[row]
        total = got[0]
        for r in range(1, row_count):
            total = total + got[r]
        return total

    arrived(got_feat, 0, row_count, recv_sems)
    all_feat[row] = reduced(got_feat, send_feat)
    spread(lambda there: all_feat.at[row], all_feat, 1, "row", row, row_count)

    def wave_reduce(step):
        index = 2 + 3 * step
        arrived(got_wave.at[step], index, row_count, recv_sems)
        total = reduced(got_wave.at[step], send_wave.at[step])
        all_wave[step, row] = total[:, :double]
        spread(
            lambda there: all_wave.at[step, row], all_wave.at[step], index + 1, "row", row, row_count
        )
        col_scal[step, col] = total[:, double:]
        spread(
            lambda there: col_scal.at[step, col], col_scal.at[step], index + 2, "col", col, col_count
        )

    def col_total(step):
        arrived(col_scal.at[step], 4 + 3 * step, col_count, recv_sems)
        total = col_scal[step, 0]
        for r in range(1, col_count):
            total = total + col_scal[step, r]
        return jnp.sum(total, axis=1, keepdims=True)

    def mix_lines(first, count, kc, ob, channels_in, bias, source, store):
        low_k, high_k = pl.ds(128 * kc, 128), pl.ds(kept + 128 * kc, 128)
        store_k = pl.ds(store.shape[2] - kept + 128 * kc, 128)
        outs = pl.ds(16 * ob, 16)
        maps = [(mode_map[0, g, outs, low_k], mode_map[1, g, outs, low_k]) for g in channels_in]
        start = (mode_map[0, 4, outs, low_k], mode_map[1, 4, outs, low_k]) if bias else None
        for block in range(count // 8):
            top = first + 8 * block
            parts = [
                (modes[g, pl.ds(top, 8), low_k], modes[g, pl.ds(top, 8), high_k]) for g in channels_in
            ]
            for i in range(8):
                line = top + i
                if bias:
                    re, im = start
                else:
                    re, im = source[line, outs, low_k], source[line, outs, high_k]
                for (mode_re, mode_im), (map_re, map_im) in zip(parts, maps):
                    one_re, one_im = mode_re[i : i + 1], mode_im[i : i + 1]
                    re = re + (map_re * one_re - map_im * one_im)
                    im = im + (map_re * one_im + map_im * one_re)
                store[line, outs, low_k] = re.astype(store.dtype)
                store[line, outs, store_k] = im.astype(store.dtype)

    def mix_fixed():
        for kc in range(kept // 128):
            for ob in range(channels // 16):

                def eight_lines(block, carry):
                    first = pl.multiple_of(8 * block, 8)
                    mix_lines(first, 8, kc, ob, (2, 3), True, None, fixed)
                    return carry

                lax.fori_loop(0, lines // 8, eight_lines, 0)

    def mix_group(g):
        for kc in range(kept // 128):
            for ob in range(channels // 16):
                mix_lines(LINES * g, LINES, kc, ob, (0, 1), False, fixed, mixed)

    def layer(step):
        outer = half // PIECE - 1
        edges = [(g, outer) for g in range(groups)]
        ends = [(g, n) for g in sorted({0, groups - 1}) for n in range(outer)]
        inside = [(g, n) for g in range(1, groups - 1) for n in range(outer)]
        order = edges + ends + inside
        copies = halo_copies(step)

        def multiply(g, n, slot):
            left = mixed[LINES * g : LINES * (g + 1)].reshape(LINES * channels, double + wide)
            piece = slice(PIECE * n, PIECE * (n + 1))
            before[slot, 0] = jnp.dot(
                left[:, : kept + wide], even_cols[g, :, piece], preferred_element_type=F32
            )
            before[slot, 1] = jnp.dot(
                left[:, kept:], odd_cols[g, :, piece], preferred_element_type=F32
            )

        def finish(g, n, slot):
            lines_of = slice(8 + LINES * g, 8 + LINES * (g + 1))
            even, odd = before[slot, 0], before[slot, 1]
            for side in range(2):
                active = gelu(even + odd if side else even - odd).astype(BF16)
                out = jnp.dot(project_map[...], active, preferred_element_type=F32)
                if side:
                    first = 128 + half + PIECE * n
                else:
                    first = 128 + half - PIECE * (n + 1)
                    out = reversed_lanes(out)
                place = slice(first, first + PIECE)
                ext[step, 0, lines_of, place] = out[:LINES]
                ext[step, 1, lines_of, place] = out[LINES:]

        mix_group(0)
        for t in range(len(order) + 1):
            if t < len(order):
                g, n = order[t]
                multiply(g, n, t % 2)
                if t < len(edges) and g + 1 < groups:
                    mix_group(g + 1)
            if t > 0:
                finish(*order[t - 1], (t - 1) % 2)
            if t == len(edges):
                for i in (0, 1, 4, 5, 6, 7):
                    copies[i].start()
            if t == len(edges) + len(ends):
                for i in (2, 3):
                    copies[i].start()

    def halo_copies(step):
        tall, across_all = pl.ds(8, lines), pl.ds(128, columns)
        line_ends = {
            1: (pl.ds(lines, 8), pl.ds(0, 8)),
            -1: (pl.ds(8, 8), pl.ds(8 + lines, 8)),
            0: (tall, tall),
        }
        col_ends = {
            1: (pl.ds(columns, 128), pl.ds(0, 128)),
            -1: (pl.ds(128, 128), pl.ds(128 + columns, 128)),
            0: (across_all, across_all),
        }
        copies = []
        for i, (dr, dc) in enumerate(
            [(1, 0), (-1, 0), (0, 1), (0, -1), (1, 1), (1, -1), (-1, 1), (-1, -1)]
        ):
            here_l, there_l = line_ends[dc]
            here_c, there_c = col_ends[dr]
            copies.append(
                pltpu.make_async_remote_copy(
                    src_ref=ext.at[step, :, here_l, here_c],
                    dst_ref=ext.at[step, :, there_l, there_c],
                    send_sem=halo_send.at[step, i],
                    recv_sem=halo_recv.at[step, i],
                    device_id={
                        "row": lax.rem(row + dr + row_count, row_count),
                        "col": lax.rem(col + dc + col_count, col_count),
                    },
                    device_id_type=MESH,
                )
            )
        return copies

    def halos(step):
        for copy in halo_copies(step):
            copy.wait()
        view = ext.at[step]

        @pl.when(row == 0)
        def _():
            view[:, :, 0:128] = jnp.zeros((2, lines + 16, 128), F32)

        @pl.when(row == row_count - 1)
        def _():
            view[:, :, 128 + columns :] = jnp.zeros((2, lines + 16, 128), F32)

        @pl.when(col == 0)
        def _():
            view[:, 0:8, :] = jnp.zeros((2, 8, columns + 256), F32)

        @pl.when(col == col_count - 1)
        def _():
            view[:, 8 + lines :, :] = jnp.zeros((2, 8, columns + 256), F32)

    def operate(step, g):
        laps, fields = [], []
        for p in range(2):
            first = 8 + LINES * g
            beside = (
                ext[step, p, first - 1 : first - 1 + LINES, :]
                + ext[step, p, first + 1 : first + 1 + LINES, :]
            )
            centre = ext[step, p, first : first + LINES, :]
            both = 4.0 * centre + beside
            width = columns + 256
            around = pltpu.roll(both, 1, 1) + pltpu.roll(both, width - 1, 1)
            total = (4.0 * beside - 20.0 * centre + around) * (1.0 / 6.0)
            laps.append(total[:, 128 : 128 + columns])
            fields.append(centre[:, 128 : 128 + columns])
        wave, damping = wave_ref[rows_of(g), :], damp_ref[rows_of(g), :]
        real = -laps[0] - wave * (fields[0] + damping * fields[1])
        imag = -laps[1] - wave * (fields[1] - damping * fields[0])
        return real, imag

    def pair(first, second):
        return (
            folded(first[0] * second[0] + first[1] * second[1]),
            folded(first[0] * second[1] - first[1] * second[0]),
        )

    def add(a, b):
        return [x + y for x, y in zip(a, b)]

    wave_reduce(0)
    arrived(all_feat, 1, row_count, recv_sems)
    re, im = unrotated(all_feat[...].reshape(2 * lines, double))
    for g in range(2):
        modes[2 + g, :, :kept] = re[g * lines : (g + 1) * lines]
        modes[2 + g, :, kept:] = im[g * lines : (g + 1) * lines]
    mix_fixed()
    for copy in back_copies:
        copy.wait()

    arrived(all_wave.at[0], 3, row_count, recv_sems)
    total_square = col_total(0)[0:1, :]
    beta = jnp.sqrt(total_square + norm_eps)
    inverse_beta = 1.0 / beta
    re, im = unrotated(all_wave[0].reshape(2 * lines, double))
    for p in range(2):
        modes[p, :, :kept] = re[p * lines : (p + 1) * lines] * (grid_scale * inverse_beta)
        modes[p, :, kept:] = im[p * lines : (p + 1) * lines] * (grid_scale * inverse_beta)
    for g in range(groups):
        for p in range(2):
            field_slabs(g, 3 * p, right_ref[p, rows_of(g), :] * (grid_scale * inverse_beta))
    layer(0)
    halos(0)
    sums = [jnp.zeros((8, 128), F32)] * 3
    for g in range(groups):
        lines_of = rows_of(g)
        result = operate(0, g)
        for p in range(2):
            applied[0, p, lines_of, :] = result[p]
            top, rest = split(result[p])
            high[p * lines + LINES * g : p * lines + LINES * (g + 1), :] = top
            low[p * lines + LINES * g : p * lines + LINES * (g + 1), :] = rest
        start = (right_ref[0, lines_of, :], right_ref[1, lines_of, :])
        square = folded(result[0] * result[0] + result[1] * result[1])
        sums = add(sums, (*pair(start, result), square))
    send_modes(1, scalar_tile(sums))
    wave_reduce(1)
    arrived(all_wave.at[1], 6, row_count, recv_sems)
    totals = col_total(1)
    unit_square = total_square * inverse_beta * inverse_beta
    a = (totals[0:1, :] * inverse_beta, totals[1:2, :] * inverse_beta)
    a_square = a[0] * a[0] + a[1] * a[1]
    rest_square = jnp.maximum(totals[2:3, :] - a_square * (2.0 - unit_square), 0.0)
    c = jnp.sqrt(rest_square + norm_eps)
    inverse_c = 1.0 / c
    a_over = (a[0] * inverse_beta, a[1] * inverse_beta)

    def next_vector(w, v):
        scaled = cmul(a_over, v)
        return (w[0] - scaled[0]) * inverse_c, (w[1] - scaled[1]) * inverse_c

    old, new = (all_wave[i].reshape(2 * lines, double) for i in range(2))
    planes = next_vector((new[:lines], new[lines:]), (old[:lines], old[lines:]))
    for p in range(2):
        re, im = unrotated(planes[p])
        modes[p, :, :kept] = re * grid_scale
        modes[p, :, kept:] = im * grid_scale
    for g in range(groups):
        lines_of = rows_of(g)
        vector = next_vector(
            (applied[0, 0, lines_of, :], applied[0, 1, lines_of, :]),
            (right_ref[0, lines_of, :], right_ref[1, lines_of, :]),
        )
        for p in range(2):
            basis[p, lines_of, :] = vector[p]
            field_slabs(g, 3 * p, vector[p] * grid_scale)
    layer(1)
    halos(1)
    sums = [jnp.zeros((8, 128), F32)] * 5
    for g in range(groups):
        lines_of = rows_of(g)
        result = operate(1, g)
        for p in range(2):
            applied[1, p, lines_of, :] = result[p]
        start = (right_ref[0, lines_of, :], right_ref[1, lines_of, :])
        vector = (basis[0, lines_of, :], basis[1, lines_of, :])
        square = folded(result[0] * result[0] + result[1] * result[1])
        sums = add(sums, (*pair(start, result), *pair(vector, result), square))
    got_scal[row] = scalar_tile(sums)
    spread(lambda there: got_scal.at[row], got_scal, 8, "row", row, row_count)
    arrived(got_scal, 8, row_count, recv_sems)
    total = got_scal[0]
    for r in range(1, row_count):
        total = total + got_scal[r]
    col_scal[2, col] = total
    spread(lambda there: col_scal.at[2, col], col_scal.at[2], 9, "col", col, col_count)
    arrived(col_scal.at[2], 9, col_count, recv_sems)
    total = col_scal[2, 0]
    for r in range(1, col_count):
        total = total + col_scal[2, r]
    totals = jnp.sum(total, axis=1, keepdims=True)
    b = (totals[0:1, :] * inverse_beta, totals[1:2, :] * inverse_beta)
    d = (totals[2:3, :], totals[3:4, :])
    b_square = b[0] * b[0] + b[1] * b[1]
    d_square = d[0] * d[0] + d[1] * d[1]
    second_square = rest_square * inverse_c * inverse_c
    overlap = (norm_eps * inverse_beta * inverse_beta) * inverse_c
    between = conj_cmul(b, d)
    between = between[0] * a[0] - between[1] * a[1]
    last_square = (
        totals[4:5, :]
        - b_square * (2.0 - unit_square)
        - d_square * (2.0 - second_square)
        + 2.0 * overlap * between
    )
    e = jnp.sqrt(jnp.maximum(last_square, 0.0) + norm_eps)
    y0, y1 = small_solve(beta, a, b, c, d, e)
    for g in range(groups):
        lines_of = rows_of(g)
        inner = slice(8 + LINES * g, 8 + LINES * (g + 1))
        z0, z1, w0, w1 = (
            [ext[0, p, inner, 128 : 128 + columns] for p in range(2)],
            [ext[1, p, inner, 128 : 128 + columns] for p in range(2)],
            [applied[0, p, lines_of, :] for p in range(2)],
            [applied[1, p, lines_of, :] for p in range(2)],
        )
        z0, z1, w0, w1 = cmul(y0, z0), cmul(y1, z1), cmul(y0, w0), cmul(y1, w1)
        for p in range(2):
            solution_ref[p, lines_of, :] = z0[p] + z1[p]
            residual_ref[p, lines_of, :] = right_ref[p, lines_of, :] - w0[p] - w1[p]

    arrived(got_feat, 0, row_count, send_sems)
    arrived(all_feat, 1, row_count, send_sems)
    for step in range(2):
        arrived(got_wave.at[step], 2 + 3 * step, row_count, send_sems)
        arrived(all_wave.at[step], 3 + 3 * step, row_count, send_sems)
        arrived(col_scal.at[step], 4 + 3 * step, col_count, send_sems)
    arrived(got_scal, 8, row_count, send_sems)
    arrived(col_scal.at[2], 9, col_count, send_sems)


def deliver(solution_in, residual_in, solution_out, residual_out, held, sems):
    moves = []
    for i, (source, target) in enumerate(
        [(solution_in, solution_out), (residual_in, residual_out)]
    ):
        for p in range(2):
            k = 2 * i + p
            arrive = pltpu.make_async_copy(source.at[p], held.at[k], sems.at[0, k])
            leave = pltpu.make_async_copy(held.at[k], target.at[p], sems.at[1, k])
            moves.append((arrive, leave))
    for arrive, _ in moves:
        arrive.start()
    for arrive, leave in moves:
        arrive.wait()
        leave.start()
    for _, leave in moves:
        leave.wait()


def shards(
    row_count,
    col_count,
    kept,
    forcing,
    medium_index,
    absorbing_mask,
    source_rows,
    source_cols,
    refraction,
    lift_weight,
    lift_bias,
    spectral_weight,
    point_weight,
    layer_bias,
    project_weight,
):
    _, lines, columns = forcing.shape
    channels = point_weight.shape[0]
    grid_cols = columns * row_count
    groups = lines // LINES
    double = 2 * kept
    assert row_count * 8 == 2 * lines

    table_high, table_low = forward_tables(columns, kept, grid_cols)
    table_back = back_tables(columns, kept, grid_cols)
    phases = phase_table(row_count, columns, kept)

    field = jax.ShapeDtypeStruct((2, lines, columns), F32)
    vmem = pl.BlockSpec(memory_space=pltpu.VMEM)
    smem = pl.BlockSpec(memory_space=pltpu.SMEM)
    hbm = pl.BlockSpec(memory_space=pl.ANY)
    dma = pltpu.SemaphoreType.DMA
    results = pl.pallas_call(
        functools.partial(kernel, row_count, col_count, kept),
        out_shape=(field, field),
        in_specs=[vmem] * 3 + [smem] * 5 + [vmem] * 2 + [hbm] + [vmem] * 3 + [hbm] * 4,
        out_specs=(vmem, vmem),
        scratch_shapes=[
            pltpu.VMEM((columns, double), BF16),
            pltpu.VMEM((columns, double), BF16),
            pltpu.VMEM((8, 2 * double), F32),
            pltpu.VMEM((2, channels, channels, kept), BF16),
            pltpu.VMEM((2, 5, channels, kept), F32),
            pltpu.VMEM((2 * LINES, LINES * channels), BF16),
            pltpu.VMEM((lines, columns), F32),
            pltpu.VMEM((lines, columns), F32),
            pltpu.VMEM((2, lines, columns), F32),
            pltpu.VMEM((groups, kept + SLABS * LINES, columns // 2), BF16),
            pltpu.VMEM((groups, kept + SLABS * LINES, columns // 2), BF16),
            pltpu.VMEM((lines, channels, double + SLABS * LINES), BF16),
            pltpu.VMEM((lines, channels, double), F32),
            pltpu.VMEM((4, lines, double), F32),
            pltpu.VMEM((2 * lines, columns), BF16),
            pltpu.VMEM((2 * lines, columns), BF16),
            pltpu.VMEM((row_count, 8, double), F32),
            pltpu.VMEM((row_count, 8, double), F32),
            pltpu.VMEM((row_count, 8, double), F32),
            pltpu.VMEM((2, row_count, 8, double + 128), F32),
            pltpu.VMEM((2, row_count, 8, double + 128), F32),
            pltpu.VMEM((2, row_count, 8, double), F32),
            pltpu.VMEM((row_count, 8, 128), F32),
            pltpu.VMEM((3, col_count, 8, 128), F32),
            pltpu.VMEM((2, 2, LINES * channels, PIECE), F32),
            pltpu.VMEM((2, 2, lines + 16, columns + 256), F32),
            pltpu.VMEM((2, 2, lines, columns), F32),
            pltpu.VMEM((2, lines, columns), F32),
            dma((4 + 2 * groups,)),
            dma((2, 8)),
            dma((2, 8)),
            dma((10,)),
            dma((10,)),
        ],
        compiler_params=pltpu.CompilerParams(
            collective_id=0, has_side_effects=True, vmem_limit_bytes=56 * 2**20
        ),
        name="krylov",
    )(
        forcing,
        medium_index,
        absorbing_mask,
        source_rows,
        source_cols,
        refraction,
        lift_weight,
        lift_bias,
        lift_weight,
        lift_bias.reshape(1, -1),
        spectral_weight.transpose(0, 2, 3, 1),
        point_weight,
        layer_bias.reshape(1, -1),
        project_weight.T,
        table_high,
        table_low,
        table_back,
        phases,
    )
    return pl.pallas_call(
        deliver,
        out_shape=(field, field),
        in_specs=[hbm] * 2,
        out_specs=[hbm] * 2,
        scratch_shapes=[pltpu.VMEM((4, lines, columns), F32), dma((2, 4))],
        name="deliver",
    )(*results)


def solution(mesh):
    return jax.shard_map(
        functools.partial(shards, mesh.shape["row"], mesh.shape["col"], K),
        mesh=mesh,
        in_specs=(
            P(None, "col", "row"),
            P("col", "row"),
            P("col", "row"),
            P(),
            P(),
            P(),
            P(),
            P(),
            P(),
            P(),
            P(),
            P(),
        ),
        out_specs=(P(None, "col", "row"), P(None, "col", "row")),
        check_vma=False,
    )
```

```python
import functools
import math

import jax
import jax.numpy as jnp
import numpy as np
import ml_dtypes
from jax import lax
from jax.experimental import pallas as pl
from jax.experimental.pallas import tpu as pltpu
from jax.sharding import PartitionSpec as P

K = 256

wave_base = 0.23
source_gain = 8.0
norm_eps = 1e-06

MESH = pl.DeviceIdType.MESH
F32 = jnp.float32
BF16 = jnp.bfloat16
LINES = 16
SLABS = 16
PIECE = 256


def forward_tables(tile_cols, kept_modes, grid_cols):
    positions = np.arange(tile_cols, dtype=np.int64)
    mode_index = np.arange(kept_modes, dtype=np.int64)
    angles = (positions[:, None] * mode_index[None, :] % grid_cols) * (2.0 * math.pi / grid_cols)
    scale = 1.0 / math.sqrt(grid_cols)
    table = np.concatenate([np.cos(angles), -np.sin(angles)], axis=1) * scale
    high = table.astype(np.float32).astype(ml_dtypes.bfloat16)
    low = (table - high.astype(np.float64)).astype(np.float32).astype(ml_dtypes.bfloat16)
    return high, low


def back_tables(tile_cols, kept_modes, grid_cols):
    odd = 2 * np.arange(tile_cols // 2, dtype=np.int64) + 1
    mode_index = np.arange(kept_modes, dtype=np.int64)
    angles = (mode_index[:, None] * odd[None, :] % (2 * grid_cols)) * (math.pi / grid_cols)
    scale = 1.0 / math.sqrt(grid_cols)
    table = np.stack([np.cos(angles), -np.sin(angles)]) * scale
    return table.astype(np.float32).astype(ml_dtypes.bfloat16)


def phase_table(row_count, tile_cols, kept_modes):
    grid_cols = row_count * tile_cols
    first = 2 * tile_cols * np.arange(row_count, dtype=np.int64)
    mode_index = np.arange(kept_modes, dtype=np.int64)
    parts = []
    for place in (first, first + tile_cols - 1):
        angles = (place[:, None] * mode_index[None, :] % (2 * grid_cols)) * (math.pi / grid_cols)
        parts += [np.cos(angles), np.sin(angles)]
    table = np.concatenate(parts, axis=1).astype(np.float32)
    return np.ascontiguousarray(np.broadcast_to(table[:, None, :], (row_count, 8, 4 * kept_modes)))


def split(x):
    high = x.astype(BF16)
    return high, (x - high.astype(F32)).astype(BF16)


def three_way(x):
    high, low = split(x)
    return high, low, (x - high.astype(F32) - low.astype(F32)).astype(BF16)


def gelu(x):
    return 0.5 * x * (1.0 + lax.erf(x * math.sqrt(0.5)))


def cmul(a, b):
    return a[0] * b[0] - a[1] * b[1], a[0] * b[1] + a[1] * b[0]


def conj_cmul(a, b):
    return a[0] * b[0] + a[1] * b[1], a[0] * b[1] - a[1] * b[0]


def small_solve(beta, a, b, c, d, e):
    gram_first = a[0] * a[0] + a[1] * a[1] + c * c
    gram_second = b[0] * b[0] + b[1] * b[1] + d[0] * d[0] + d[1] * d[1] + e * e
    cross = conj_cmul(a, b)
    cross = (cross[0] + c * d[0], cross[1] + c * d[1])
    ad = cmul(a, d)
    minor = (ad[0] - b[0] * c, ad[1] - b[1] * c)
    determinant = (
        minor[0] * minor[0]
        + minor[1] * minor[1]
        + (a[0] * a[0] + a[1] * a[1]) * e * e
        + c * c * e * e
    )
    first = (beta * a[0], -beta * a[1])
    second = (beta * b[0], -beta * b[1])
    t = cmul(cross, second)
    y0 = ((gram_second * first[0] - t[0]) / determinant, (gram_second * first[1] - t[1]) / determinant)
    t = conj_cmul(cross, first)
    y1 = ((gram_first * second[0] - t[0]) / determinant, (gram_first * second[1] - t[1]) / determinant)
    return y0, y1


def kernel(
    row_count,
    col_count,
    kept,
    forcing,
    medium,
    mask,
    source_rows,
    source_cols,
    refraction,
    lift_scalars,
    bias_scalars,
    lift_weight,
    lift_bias,
    spectral_weight,
    point_weight,
    layer_bias,
    project_weight,
    table_high,
    table_low,
    table_back,
    phases,
    solution_ref,
    residual_ref,
    fwd_high,
    fwd_low,
    phase,
    weights,
    mode_map,
    project_map,
    wave_ref,
    feature_ref,
    right_ref,
    even_cols,
    odd_cols,
    mixed,
    fixed,
    modes,
    high,
    low,
    send_feat,
    got_feat,
    all_feat,
    send_wave,
    got_wave,
    all_wave,
    got_scal,
    col_scal,
    before,
    ext,
    applied,
    basis,
    table_sems,
    halo_send,
    halo_recv,
    send_sems,
    recv_sems,
):
    lines, columns = mask.shape
    channels = point_weight.shape[0]
    groups = lines // LINES
    double = 2 * kept
    wide = SLABS * LINES
    half = columns // 2
    row = lax.axis_index("row")
    col = lax.axis_index("col")
    grid_scale = math.sqrt(lines * col_count * columns * row_count)

    table_copies = [
        pltpu.make_async_copy(table_high, fwd_high, table_sems.at[0]),
        pltpu.make_async_copy(table_low, fwd_low, table_sems.at[1]),
        pltpu.make_async_copy(phases.at[row], phase, table_sems.at[2]),
    ]
    back_copies = [
        copy
        for g in range(groups)
        for copy in (
            pltpu.make_async_copy(table_back.at[0], even_cols.at[g, pl.ds(0, kept)], table_sems.at[4 + 2 * g]),
            pltpu.make_async_copy(table_back.at[1], odd_cols.at[g, pl.ds(wide, kept)], table_sems.at[5 + 2 * g]),
        )
    ]
    weight_copy = pltpu.make_async_copy(spectral_weight, weights, table_sems.at[3])
    for copy in [*table_copies, weight_copy, *back_copies]:
        copy.start()

    barrier = pltpu.get_barrier_semaphore()
    greeted = 0
    for d in range(1, row_count):
        pl.semaphore_signal(
            barrier, inc=1, device_id={"row": lax.rem(row + d, row_count)}, device_id_type=MESH
        )
        greeted += 1
    for d in range(1, col_count):
        pl.semaphore_signal(
            barrier, inc=1, device_id={"col": lax.rem(col + d, col_count)}, device_id_type=MESH
        )
        greeted += 1
    for dr in (1, row_count - 1):
        for dc in (1, col_count - 1):
            pl.semaphore_signal(
                barrier,
                inc=1,
                device_id={
                    "row": lax.rem(row + dr, row_count),
                    "col": lax.rem(col + dc, col_count),
                },
                device_id_type=MESH,
            )
            greeted += 1

    def spread(source, target, index, axis, me, count):
        for d in range(1, count):
            there = lax.rem(me + d, count)
            pltpu.make_async_remote_copy(
                src_ref=source(there),
                dst_ref=target.at[me],
                send_sem=send_sems.at[index],
                recv_sem=recv_sems.at[index],
                device_id={axis: there},
                device_id_type=MESH,
            ).start()

    def arrived(target, index, count, sems):
        whole = target.at[pl.ds(0, count - 1)]
        pltpu.make_async_copy(whole, whole, sems.at[index]).wait()

    def forward(kind, out):
        spectrum = (
            jnp.dot(high[kind], fwd_high[...], preferred_element_type=F32)
            + jnp.dot(high[kind], fwd_low[...], preferred_element_type=F32)
            + jnp.dot(low[kind], fwd_high[...], preferred_element_type=F32)
        )
        cosine, sine = phase[0:1, :kept], phase[0:1, kept:double]
        re, im = spectrum[:, :kept], spectrum[:, kept:]
        out[:, :, 0:kept] = (re * cosine + im * sine).reshape(row_count, 8, kept)
        out[:, :, kept:double] = (im * cosine - re * sine).reshape(row_count, 8, kept)

    def unrotated(both):
        cosine, sine = phase[0:1, double : double + kept], phase[0:1, double + kept :]
        re, im = both[:, :kept], both[:, kept:]
        return re * cosine - im * sine, im * cosine + re * sine

    flip = jnp.where(
        lax.broadcasted_iota(jnp.int32, (128, 128), 0)
        + lax.broadcasted_iota(jnp.int32, (128, 128), 1)
        == 127,
        1.0,
        0.0,
    ).astype(BF16)

    def reversed_lanes(x):
        height, blocks = x.shape[0], x.shape[1] // 128
        parts = [
            part[:, 128 * i : 128 * i + 128] for part in three_way(x) for i in reversed(range(blocks))
        ]
        turned = jnp.dot(jnp.concatenate(parts, axis=0), flip, preferred_element_type=F32)
        pieces = turned.reshape(3, blocks, height, 128)
        total = pieces[0] + pieces[1] + pieces[2]
        return jnp.concatenate([total[i] for i in range(blocks)], axis=1)

    def slab(g, j, even, odd):
        even_cols[g, kept + LINES * j : kept + LINES * (j + 1), :] = even
        odd_cols[g, LINES * j : LINES * (j + 1), :] = odd

    def field_slabs(g, j, value):
        right, left = value[:, half:], reversed_lanes(value[:, :half])
        even, odd = split(0.5 * (right + left)), split(0.5 * (right - left))
        slab(g, j, even[0], odd[0])
        slab(g, j + 1, even[1], odd[1])
        slab(g, j + 2, even[0], odd[0])

    def rows_of(g):
        return slice(LINES * g, LINES * (g + 1))

    def folded(x):
        total = jnp.zeros((8, 128), F32)
        for i in range(x.shape[0] // 8):
            for j in range(x.shape[1] // 128):
                total = total + x[8 * i : 8 * i + 8, 128 * j : 128 * j + 128]
        return total

    def scalar_tile(parts):
        place = lax.broadcasted_iota(jnp.int32, (8, 128), 0)
        tile = jnp.zeros((8, 128), F32)
        for i, part in enumerate(parts):
            tile = jnp.where(place == i, jnp.sum(part, axis=0, keepdims=True), tile)
        return tile

    for g in range(groups):
        lines_of = rows_of(g)
        kind = medium[lines_of, :]
        refractive = jnp.zeros((LINES, columns), F32)
        for level in range(refraction.shape[0]):
            refractive = jnp.where(kind == level, refraction[level], refractive)
        damping = 0.1 + mask[lines_of, :].astype(F32)
        scaled = wave_base * refractive
        wave_ref[lines_of, :] = scaled * scaled
        feature_ref[0, lines_of, :] = refractive
        feature_ref[1, lines_of, :] = damping
        for i, feature in enumerate((refractive, damping)):
            top, rest = split(feature)
            place = slice(lines * i + LINES * g, lines * i + LINES * (g + 1))
            high[0, place, :] = top
            low[0, place, :] = rest
    for copy in table_copies:
        copy.wait()
    forward(0, send_feat)
    pl.semaphore_wait(barrier, greeted)
    spread(lambda there: send_feat.at[there], got_feat, 0, "row", row, row_count)

    sources = source_rows.shape[0]
    place = lax.broadcasted_iota(jnp.int32, (sources, 128), 0)
    col_of = jnp.zeros((sources, 128), jnp.int32)
    for i in range(sources):
        col_of = jnp.where(place == i, source_cols[i] - columns * row, col_of)
    lane = lax.broadcasted_iota(jnp.int32, (sources, 128), 1)
    col_hits = jnp.concatenate(
        [jnp.where(col_of == lane + 128 * j, 1.0, 0.0) for j in range(columns // 128)], axis=1
    ).astype(BF16)
    place = lax.broadcasted_iota(jnp.int32, (lines, sources), 1)
    row_of = jnp.zeros((lines, sources), jnp.int32)
    for i in range(sources):
        row_of = jnp.where(place == i, source_rows[i] - lines * col, row_of)
    line_hits = jnp.where(
        row_of == lax.broadcasted_iota(jnp.int32, (lines, sources), 0), 1.0, 0.0
    ).astype(BF16)
    source_count = jnp.dot(line_hits, col_hits, preferred_element_type=F32)
    square = jnp.zeros((8, 128), F32)
    for g in range(groups):
        lines_of = rows_of(g)
        for p in range(2):
            field = forcing[p, lines_of, :]
            if p == 0:
                field = field + source_gain * source_count[lines_of, :]
            right_ref[p, lines_of, :] = field
            square = square + folded(field * field)
            top, rest = split(field)
            high[1, p * lines + LINES * g : p * lines + LINES * (g + 1), :] = top
            low[1, p * lines + LINES * g : p * lines + LINES * (g + 1), :] = rest
    def send_modes(step, tile):
        forward(1, send_wave.at[step])
        for r in range(row_count):
            send_wave[step, r, :, double:] = tile
        spread(
            lambda there: send_wave.at[step, there], got_wave.at[step], 2 + 3 * step, "row", row, row_count
        )

    send_modes(0, scalar_tile([square]))

    mode_of = lax.broadcasted_iota(jnp.int32, (1, 128), 1)

    def fold(ob, kc):
        outs, some = pl.ds(16 * ob, 16), pl.ds(128 * kc, 128)
        used = 5 if kc == 0 else 4
        twice = jnp.where(mode_of == 0, 1.0, 2.0) if kc == 0 else 2.0
        both = []
        for part in range(2):

            def one_channel(c, sums):
                weight = weights[part, c, outs, some].astype(F32)
                factors = [lift_scalars[g, c] for g in range(4)] + [bias_scalars[c]]
                return tuple(x + f * weight for x, f in zip(sums, factors))

            both.append(
                lax.fori_loop(
                    0, channels, one_channel, (jnp.zeros((16, 128), F32),) * used, unroll=8
                )
            )
        for g in range(4):
            re, im = both[0][g] * twice, both[1][g] * twice
            mode_map[0, g, outs, some] = re
            mode_map[1, g, outs, some] = re + im
            mode_map[2, g, outs, some] = im - re
        anchor = jnp.where(mode_of == 0, math.sqrt(columns * row_count), 0.0)
        for part in range(2):
            mode_map[part, 4, outs, some] = (
                both[part][4] * anchor if kc == 0 else jnp.zeros((16, 128), F32)
            )

    def reduced(got, source):
        got[row] = source[row]
        total = got[0]
        for r in range(1, row_count):
            total = total + got[r]
        return total

    blocks = [(ob, kc) for ob in range(channels // 16) for kc in range(kept // 128)]
    weight_copy.wait()
    for block in blocks[: len(blocks) // 2]:
        fold(*block)
    arrived(got_feat, 0, row_count, recv_sems)
    all_feat[row] = reduced(got_feat, send_feat)
    spread(lambda there: all_feat.at[row], all_feat, 1, "row", row, row_count)

    def wave_reduce(step):
        index = 2 + 3 * step
        arrived(got_wave.at[step], index, row_count, recv_sems)
        total = reduced(got_wave.at[step], send_wave.at[step])
        all_wave[step, row] = total[:, :double]
        spread(
            lambda there: all_wave.at[step, row], all_wave.at[step], index + 1, "row", row, row_count
        )
        col_scal[step, col] = total[:, double:]
        spread(
            lambda there: col_scal.at[step, col], col_scal.at[step], index + 2, "col", col, col_count
        )

    def col_total(step):
        arrived(col_scal.at[step], 4 + 3 * step, col_count, recv_sems)
        total = col_scal[step, 0]
        for r in range(1, col_count):
            total = total + col_scal[step, r]
        return jnp.sum(total, axis=1, keepdims=True)

    def mix_lines(first, count, kc, ob, channels_in, bias, source, store):
        low_k, high_k = pl.ds(128 * kc, 128), pl.ds(kept + 128 * kc, 128)
        store_k = pl.ds(store.shape[2] - kept + 128 * kc, 128)
        outs = pl.ds(16 * ob, 16)
        maps = [tuple(mode_map[i, g, outs, low_k] for i in range(3)) for g in channels_in]
        start = (mode_map[0, 4, outs, low_k], mode_map[1, 4, outs, low_k]) if bias else None
        for block in range(count // 8):
            top = first + 8 * block
            parts = [
                (modes[g, pl.ds(top, 8), low_k], modes[g, pl.ds(top, 8), high_k]) for g in channels_in
            ]
            parts = [(mode_re, mode_im, mode_re + mode_im) for mode_re, mode_im in parts]
            for i in range(8):
                line = top + i
                if bias:
                    re, im = start
                else:
                    re, im = source[line, outs, low_k], source[line, outs, high_k]
                shared = None
                for (mode_re, mode_im, mode_sum), (map_re, map_sum, map_less) in zip(parts, maps):
                    product = map_re * mode_sum[i : i + 1]
                    shared = product if shared is None else shared + product
                    re = re - map_sum * mode_im[i : i + 1]
                    im = im + map_less * mode_re[i : i + 1]
                re, im = re + shared, im + shared
                store[line, outs, low_k] = re.astype(store.dtype)
                store[line, outs, store_k] = im.astype(store.dtype)

    def mix_fixed():
        for kc in range(kept // 128):
            for ob in range(channels // 16):

                def eight_lines(block, carry):
                    first = pl.multiple_of(8 * block, 8)
                    mix_lines(first, 8, kc, ob, (2, 3), True, None, fixed)
                    return carry

                lax.fori_loop(0, lines // 8, eight_lines, 0)

    def mix_group(g):
        for kc in range(kept // 128):
            for ob in range(channels // 16):
                mix_lines(LINES * g, LINES, kc, ob, (0, 1), False, fixed, mixed)

    def layer(step):
        outer = half // PIECE - 1
        edges = [(g, outer) for g in range(groups)]
        ends = [(g, n) for g in sorted({0, groups - 1}) for n in range(outer)]
        inside = [(g, n) for g in range(1, groups - 1) for n in range(outer)]
        order = edges + ends + inside
        copies = halo_copies(step)

        def multiply(g, n, slot):
            left = mixed[LINES * g : LINES * (g + 1)].reshape(LINES * channels, double + wide)
            piece = slice(PIECE * n, PIECE * (n + 1))
            before[slot, 0] = jnp.dot(
                left[:, : kept + wide], even_cols[g, :, piece], preferred_element_type=F32
            )
            before[slot, 1] = jnp.dot(
                left[:, kept:], odd_cols[g, :, piece], preferred_element_type=F32
            )

        def finish(g, n, slot):
            lines_of = slice(8 + LINES * g, 8 + LINES * (g + 1))
            even, odd = before[slot, 0], before[slot, 1]
            for side in range(2):
                active = gelu(even + odd if side else even - odd).astype(BF16)
                out = jnp.dot(project_map[...], active, preferred_element_type=F32)
                if side:
                    first = 128 + half + PIECE * n
                else:
                    first = 128 + half - PIECE * (n + 1)
                    out = reversed_lanes(out)
                place = slice(first, first + PIECE)
                ext[step, 0, lines_of, place] = out[:LINES]
                ext[step, 1, lines_of, place] = out[LINES:]

        mix_group(0)
        for t in range(len(order) + 1):
            if t < len(order):
                g, n = order[t]
                multiply(g, n, t % 2)
                if t < len(edges) and g + 1 < groups:
                    mix_group(g + 1)
            if t > 0:
                finish(*order[t - 1], (t - 1) % 2)
            if t == len(edges):
                for i in (0, 1, 4, 5, 6, 7):
                    copies[i].start()
            if t == len(edges) + len(ends):
                for i in (2, 3):
                    copies[i].start()

    def halo_copies(step):
        tall, across_all = pl.ds(8, lines), pl.ds(128, columns)
        line_ends = {
            1: (pl.ds(lines, 8), pl.ds(0, 8)),
            -1: (pl.ds(8, 8), pl.ds(8 + lines, 8)),
            0: (tall, tall),
        }
        col_ends = {
            1: (pl.ds(columns, 128), pl.ds(0, 128)),
            -1: (pl.ds(128, 128), pl.ds(128 + columns, 128)),
            0: (across_all, across_all),
        }
        copies = []
        for i, (dr, dc) in enumerate(
            [(1, 0), (-1, 0), (0, 1), (0, -1), (1, 1), (1, -1), (-1, 1), (-1, -1)]
        ):
            here_l, there_l = line_ends[dc]
            here_c, there_c = col_ends[dr]
            copies.append(
                pltpu.make_async_remote_copy(
                    src_ref=ext.at[step, :, here_l, here_c],
                    dst_ref=ext.at[step, :, there_l, there_c],
                    send_sem=halo_send.at[step, i],
                    recv_sem=halo_recv.at[step, i],
                    device_id={
                        "row": lax.rem(row + dr + row_count, row_count),
                        "col": lax.rem(col + dc + col_count, col_count),
                    },
                    device_id_type=MESH,
                )
            )
        return copies

    def halos(step):
        for copy in halo_copies(step):
            copy.wait()
        view = ext.at[step]

        @pl.when(row == 0)
        def _():
            view[:, :, 0:128] = jnp.zeros((2, lines + 16, 128), F32)

        @pl.when(row == row_count - 1)
        def _():
            view[:, :, 128 + columns :] = jnp.zeros((2, lines + 16, 128), F32)

        @pl.when(col == 0)
        def _():
            view[:, 0:8, :] = jnp.zeros((2, 8, columns + 256), F32)

        @pl.when(col == col_count - 1)
        def _():
            view[:, 8 + lines :, :] = jnp.zeros((2, 8, columns + 256), F32)

    def operate(step, g):
        laps, fields = [], []
        for p in range(2):
            first = 8 + LINES * g
            beside = (
                ext[step, p, first - 1 : first - 1 + LINES, :]
                + ext[step, p, first + 1 : first + 1 + LINES, :]
            )
            centre = ext[step, p, first : first + LINES, :]
            both = 4.0 * centre + beside
            width = columns + 256
            around = pltpu.roll(both, 1, 1) + pltpu.roll(both, width - 1, 1)
            total = (4.0 * beside - 20.0 * centre + around) * (1.0 / 6.0)
            laps.append(total[:, 128 : 128 + columns])
            fields.append(centre[:, 128 : 128 + columns])
        wave, damping = wave_ref[rows_of(g), :], feature_ref[1, rows_of(g), :]
        real = -laps[0] - wave * (fields[0] + damping * fields[1])
        imag = -laps[1] - wave * (fields[1] - damping * fields[0])
        return real, imag

    def pair(first, second):
        return (
            folded(first[0] * second[0] + first[1] * second[1]),
            folded(first[0] * second[1] - first[1] * second[0]),
        )

    def add(a, b):
        return [x + y for x, y in zip(a, b)]

    for block in blocks[len(blocks) // 2 :]:
        fold(*block)
    wave_reduce(0)

    lift = jnp.concatenate(
        [lift_weight[...], lift_bias[...], jnp.zeros((3, channels), F32)], axis=0
    )
    lift_parts = three_way(lift)
    point = jnp.zeros((8, channels), F32)
    for part in lift_parts:
        point = point + jnp.dot(part, point_weight[...], preferred_element_type=F32)
    channel_row = lax.broadcasted_iota(jnp.int32, (8, channels), 0)
    point = point + jnp.where(channel_row == 4, layer_bias[...], 0.0)
    top, rest = split(point)
    from_row = lax.broadcasted_iota(jnp.int32, (8, wide), 0)
    slab_of = lax.broadcasted_iota(jnp.int32, (8, wide), 1) // LINES
    first_slab = 3 * from_row
    pick_top = ((slab_of == first_slab) | ((slab_of == first_slab + 1) & (from_row < 4))) & (from_row < 5)
    pick_rest = ((slab_of == first_slab + 2) & (from_row < 4)) | ((slab_of == 13) & (from_row == 4))
    over_rows = (((0,), (0,)), ((), ()))
    spread_out = lax.dot_general(
        top.astype(F32), jnp.where(pick_top, 1.0, 0.0), over_rows, preferred_element_type=F32
    ) + lax.dot_general(
        rest.astype(F32), jnp.where(pick_rest, 1.0, 0.0), over_rows, preferred_element_type=F32
    )
    line_of = lax.broadcasted_iota(jnp.int32, (channels, wide), 1) % LINES
    for i in range(LINES):
        masked = jnp.where(line_of == i, spread_out, 0.0).astype(BF16)
        for g in range(groups):
            mixed[LINES * g + i, :, kept : kept + wide] = masked
    all_rows = LINES * channels
    tiles = jnp.where(
        lax.broadcasted_iota(jnp.int32, (channels, all_rows), 0)
        == lax.broadcasted_iota(jnp.int32, (channels, all_rows), 1) % channels,
        1.0,
        0.0,
    )
    across = lax.dot_general(
        project_weight[...].astype(F32), tiles, (((1,), (0,)), ((), ())), preferred_element_type=F32
    )
    own_line = (
        lax.broadcasted_iota(jnp.int32, (LINES, all_rows), 0)
        == lax.broadcasted_iota(jnp.int32, (LINES, all_rows), 1) // channels
    )
    for p in range(2):
        project_map[LINES * p : LINES * (p + 1), :] = jnp.where(
            own_line, across[p : p + 1, :], 0.0
        ).astype(BF16)

    for g in range(groups):
        ones = jnp.ones((LINES, half), BF16)
        zeros = jnp.zeros_like(ones)
        slab(g, 12, ones, zeros)
        slab(g, 13, ones, zeros)
        slab(g, 14, zeros, zeros)
        slab(g, 15, zeros, zeros)
        for i in range(2):
            field_slabs(g, 6 + 3 * i, feature_ref[i, rows_of(g), :])

    arrived(all_feat, 1, row_count, recv_sems)
    re, im = unrotated(all_feat[...].reshape(2 * lines, double))
    for g in range(2):
        modes[2 + g, :, :kept] = re[g * lines : (g + 1) * lines]
        modes[2 + g, :, kept:] = im[g * lines : (g + 1) * lines]
    mix_fixed()
    for copy in back_copies:
        copy.wait()

    arrived(all_wave.at[0], 3, row_count, recv_sems)
    total_square = col_total(0)[0:1, :]
    beta = jnp.sqrt(total_square + norm_eps)
    inverse_beta = 1.0 / beta
    re, im = unrotated(all_wave[0].reshape(2 * lines, double))
    for p in range(2):
        modes[p, :, :kept] = re[p * lines : (p + 1) * lines] * (grid_scale * inverse_beta)
        modes[p, :, kept:] = im[p * lines : (p + 1) * lines] * (grid_scale * inverse_beta)
    for g in range(groups):
        for p in range(2):
            field_slabs(g, 3 * p, right_ref[p, rows_of(g), :] * (grid_scale * inverse_beta))
    layer(0)
    halos(0)
    sums = [jnp.zeros((8, 128), F32)] * 3
    for g in range(groups):
        lines_of = rows_of(g)
        result = operate(0, g)
        for p in range(2):
            applied[0, p, lines_of, :] = result[p]
            top, rest = split(result[p])
            high[1, p * lines + LINES * g : p * lines + LINES * (g + 1), :] = top
            low[1, p * lines + LINES * g : p * lines + LINES * (g + 1), :] = rest
        start = (right_ref[0, lines_of, :], right_ref[1, lines_of, :])
        square = folded(result[0] * result[0] + result[1] * result[1])
        sums = add(sums, (*pair(start, result), square))
    send_modes(1, scalar_tile(sums))
    wave_reduce(1)
    arrived(all_wave.at[1], 6, row_count, recv_sems)
    totals = col_total(1)
    unit_square = total_square * inverse_beta * inverse_beta
    a = (totals[0:1, :] * inverse_beta, totals[1:2, :] * inverse_beta)
    a_square = a[0] * a[0] + a[1] * a[1]
    rest_square = jnp.maximum(totals[2:3, :] - a_square * (2.0 - unit_square), 0.0)
    c = jnp.sqrt(rest_square + norm_eps)
    inverse_c = 1.0 / c
    a_over = (a[0] * inverse_beta, a[1] * inverse_beta)

    def next_vector(w, v):
        scaled = cmul(a_over, v)
        return (w[0] - scaled[0]) * inverse_c, (w[1] - scaled[1]) * inverse_c

    old, new = (all_wave[i].reshape(2 * lines, double) for i in range(2))
    planes = next_vector((new[:lines], new[lines:]), (old[:lines], old[lines:]))
    for p in range(2):
        re, im = unrotated(planes[p])
        modes[p, :, :kept] = re * grid_scale
        modes[p, :, kept:] = im * grid_scale
    for g in range(groups):
        lines_of = rows_of(g)
        vector = next_vector(
            (applied[0, 0, lines_of, :], applied[0, 1, lines_of, :]),
            (right_ref[0, lines_of, :], right_ref[1, lines_of, :]),
        )
        for p in range(2):
            basis[p, lines_of, :] = vector[p]
            field_slabs(g, 3 * p, vector[p] * grid_scale)
    layer(1)
    halos(1)
    sums = [jnp.zeros((8, 128), F32)] * 5
    for g in range(groups):
        lines_of = rows_of(g)
        result = operate(1, g)
        for p in range(2):
            applied[1, p, lines_of, :] = result[p]
        start = (right_ref[0, lines_of, :], right_ref[1, lines_of, :])
        vector = (basis[0, lines_of, :], basis[1, lines_of, :])
        square = folded(result[0] * result[0] + result[1] * result[1])
        sums = add(sums, (*pair(start, result), *pair(vector, result), square))
    got_scal[row] = scalar_tile(sums)
    spread(lambda there: got_scal.at[row], got_scal, 8, "row", row, row_count)
    arrived(got_scal, 8, row_count, recv_sems)
    total = got_scal[0]
    for r in range(1, row_count):
        total = total + got_scal[r]
    col_scal[2, col] = total
    spread(lambda there: col_scal.at[2, col], col_scal.at[2], 9, "col", col, col_count)
    arrived(col_scal.at[2], 9, col_count, recv_sems)
    total = col_scal[2, 0]
    for r in range(1, col_count):
        total = total + col_scal[2, r]
    totals = jnp.sum(total, axis=1, keepdims=True)
    b = (totals[0:1, :] * inverse_beta, totals[1:2, :] * inverse_beta)
    d = (totals[2:3, :], totals[3:4, :])
    b_square = b[0] * b[0] + b[1] * b[1]
    d_square = d[0] * d[0] + d[1] * d[1]
    second_square = rest_square * inverse_c * inverse_c
    overlap = (norm_eps * inverse_beta * inverse_beta) * inverse_c
    between = conj_cmul(b, d)
    between = between[0] * a[0] - between[1] * a[1]
    last_square = (
        totals[4:5, :]
        - b_square * (2.0 - unit_square)
        - d_square * (2.0 - second_square)
        + 2.0 * overlap * between
    )
    e = jnp.sqrt(jnp.maximum(last_square, 0.0) + norm_eps)
    y0, y1 = small_solve(beta, a, b, c, d, e)
    for g in range(groups):
        lines_of = rows_of(g)
        inner = slice(8 + LINES * g, 8 + LINES * (g + 1))
        z0, z1, w0, w1 = (
            [ext[0, p, inner, 128 : 128 + columns] for p in range(2)],
            [ext[1, p, inner, 128 : 128 + columns] for p in range(2)],
            [applied[0, p, lines_of, :] for p in range(2)],
            [applied[1, p, lines_of, :] for p in range(2)],
        )
        z0, z1, w0, w1 = cmul(y0, z0), cmul(y1, z1), cmul(y0, w0), cmul(y1, w1)
        for p in range(2):
            solution_ref[p, lines_of, :] = z0[p] + z1[p]
            residual_ref[p, lines_of, :] = right_ref[p, lines_of, :] - w0[p] - w1[p]

    arrived(got_feat, 0, row_count, send_sems)
    arrived(all_feat, 1, row_count, send_sems)
    for step in range(2):
        arrived(got_wave.at[step], 2 + 3 * step, row_count, send_sems)
        arrived(all_wave.at[step], 3 + 3 * step, row_count, send_sems)
        arrived(col_scal.at[step], 4 + 3 * step, col_count, send_sems)
    arrived(got_scal, 8, row_count, send_sems)
    arrived(col_scal.at[2], 9, col_count, send_sems)


def deliver(solution_in, residual_in, solution_out, residual_out, sems):
    copies = [
        pltpu.make_async_copy(solution_in, solution_out, sems.at[0]),
        pltpu.make_async_copy(residual_in, residual_out, sems.at[1]),
    ]
    for copy in copies:
        copy.start()
    for copy in copies:
        copy.wait()


def shards(
    row_count,
    col_count,
    kept,
    forcing,
    medium_index,
    absorbing_mask,
    source_rows,
    source_cols,
    refraction,
    lift_weight,
    lift_bias,
    spectral_weight,
    point_weight,
    layer_bias,
    project_weight,
):
    _, lines, columns = forcing.shape
    channels = point_weight.shape[0]
    grid_cols = columns * row_count
    groups = lines // LINES
    double = 2 * kept
    assert row_count * 8 == 2 * lines

    table_high, table_low = forward_tables(columns, kept, grid_cols)
    table_back = back_tables(columns, kept, grid_cols)
    phases = phase_table(row_count, columns, kept)

    field = jax.ShapeDtypeStruct((2, lines, columns), F32)
    vmem = pl.BlockSpec(memory_space=pltpu.VMEM)
    smem = pl.BlockSpec(memory_space=pltpu.SMEM)
    hbm = pl.BlockSpec(memory_space=pl.ANY)
    dma = pltpu.SemaphoreType.DMA
    results = pl.pallas_call(
        functools.partial(kernel, row_count, col_count, kept),
        out_shape=(pltpu.VMEM(field.shape, F32), pltpu.VMEM(field.shape, F32)),
        in_specs=[vmem] * 3 + [smem] * 5 + [vmem] * 2 + [hbm] + [vmem] * 3 + [hbm] * 4,
        out_specs=(vmem, vmem),
        scratch_shapes=[
            pltpu.VMEM((columns, double), BF16),
            pltpu.VMEM((columns, double), BF16),
            pltpu.VMEM((8, 2 * double), F32),
            pltpu.VMEM((2, channels, channels, kept), BF16),
            pltpu.VMEM((3, 5, channels, kept), F32),
            pltpu.VMEM((2 * LINES, LINES * channels), BF16),
            pltpu.VMEM((lines, columns), F32),
            pltpu.VMEM((2, lines, columns), F32),
            pltpu.VMEM((2, lines, columns), F32),
            pltpu.VMEM((groups, kept + SLABS * LINES, columns // 2), BF16),
            pltpu.VMEM((groups, kept + SLABS * LINES, columns // 2), BF16),
            pltpu.VMEM((lines, channels, double + SLABS * LINES), BF16),
            pltpu.VMEM((lines, channels, double), F32),
            pltpu.VMEM((4, lines, double), F32),
            pltpu.VMEM((2, 2 * lines, columns), BF16),
            pltpu.VMEM((2, 2 * lines, columns), BF16),
            pltpu.VMEM((row_count, 8, double), F32),
            pltpu.VMEM((row_count, 8, double), F32),
            pltpu.VMEM((row_count, 8, double), F32),
            pltpu.VMEM((2, row_count, 8, double + 128), F32),
            pltpu.VMEM((2, row_count, 8, double + 128), F32),
            pltpu.VMEM((2, row_count, 8, double), F32),
            pltpu.VMEM((row_count, 8, 128), F32),
            pltpu.VMEM((3, col_count, 8, 128), F32),
            pltpu.VMEM((2, 2, LINES * channels, PIECE), F32),
            pltpu.VMEM((2, 2, lines + 16, columns + 256), F32),
            pltpu.VMEM((2, 2, lines, columns), F32),
            pltpu.VMEM((2, lines, columns), F32),
            dma((4 + 2 * groups,)),
            dma((2, 8)),
            dma((2, 8)),
            dma((10,)),
            dma((10,)),
        ],
        compiler_params=pltpu.CompilerParams(
            collective_id=0, has_side_effects=True, vmem_limit_bytes=56 * 2**20
        ),
        name="krylov",
    )(
        forcing,
        medium_index,
        absorbing_mask,
        source_rows,
        source_cols,
        refraction,
        lift_weight,
        lift_bias,
        lift_weight,
        lift_bias.reshape(1, -1),
        spectral_weight.transpose(0, 2, 3, 1),
        point_weight,
        layer_bias.reshape(1, -1),
        project_weight.T,
        table_high,
        table_low,
        table_back,
        phases,
    )
    return pl.pallas_call(
        deliver,
        out_shape=(field, field),
        in_specs=[vmem] * 2,
        out_specs=[hbm] * 2,
        scratch_shapes=[dma((2,))],
        name="deliver",
    )(*[pltpu.with_memory_space_constraint(x, pltpu.VMEM) for x in results])


def solution(mesh):
    return jax.shard_map(
        functools.partial(shards, mesh.shape["row"], mesh.shape["col"], K),
        mesh=mesh,
        in_specs=(
            P(None, "col", "row"),
            P("col", "row"),
            P("col", "row"),
            P(),
            P(),
            P(),
            P(),
            P(),
            P(),
            P(),
            P(),
            P(),
        ),
        out_specs=(P(None, "col", "row"), P(None, "col", "row")),
        check_vma=False,
    )
```

```python
import functools
import math

import jax
import jax.numpy as jnp
import numpy as np
import ml_dtypes
from jax import lax
from jax.experimental import pallas as pl
from jax.experimental.pallas import tpu as pltpu
from jax.sharding import PartitionSpec as P

K = 256

wave_base = 0.23
source_gain = 8.0
norm_eps = 1e-06

MESH = pl.DeviceIdType.MESH
F32 = jnp.float32
BF16 = jnp.bfloat16
LINES = 16
SLABS = 16
PIECE = 256


def forward_tables(tile_cols, kept_modes, grid_cols):
    positions = np.arange(tile_cols, dtype=np.int64)
    mode_index = np.arange(kept_modes, dtype=np.int64)
    angles = (positions[:, None] * mode_index[None, :] % grid_cols) * (2.0 * math.pi / grid_cols)
    scale = 1.0 / math.sqrt(grid_cols)
    table = np.concatenate([np.cos(angles), -np.sin(angles)], axis=1) * scale
    high = table.astype(np.float32).astype(ml_dtypes.bfloat16)
    low = (table - high.astype(np.float64)).astype(np.float32).astype(ml_dtypes.bfloat16)
    return high, low


def back_tables(tile_cols, kept_modes, grid_cols):
    odd = 2 * np.arange(tile_cols // 2, dtype=np.int64) + 1
    mode_index = np.arange(kept_modes, dtype=np.int64)
    angles = (mode_index[:, None] * odd[None, :] % (2 * grid_cols)) * (math.pi / grid_cols)
    scale = math.sqrt(0.5 / grid_cols)
    table = np.stack([np.cos(angles), -np.sin(angles)]) * scale
    return table.astype(np.float32).astype(ml_dtypes.bfloat16)


def phase_table(row_count, tile_cols, kept_modes):
    grid_cols = row_count * tile_cols
    first = 2 * tile_cols * np.arange(row_count, dtype=np.int64)
    mode_index = np.arange(kept_modes, dtype=np.int64)
    parts = []
    for place in (first, first + tile_cols - 1):
        angles = (place[:, None] * mode_index[None, :] % (2 * grid_cols)) * (math.pi / grid_cols)
        parts += [np.cos(angles), np.sin(angles)]
    table = np.concatenate(parts, axis=1).astype(np.float32)
    return np.ascontiguousarray(np.broadcast_to(table[:, None, :], (row_count, 8, 4 * kept_modes)))


def split(x):
    high = x.astype(BF16)
    return high, (x - high.astype(F32)).astype(BF16)


def three_way(x):
    high, low = split(x)
    return high, low, (x - high.astype(F32) - low.astype(F32)).astype(BF16)


def scaled_gelu(z):
    return z + z * lax.erf(z)


def cmul(a, b):
    return a[0] * b[0] - a[1] * b[1], a[0] * b[1] + a[1] * b[0]


def conj_cmul(a, b):
    return a[0] * b[0] + a[1] * b[1], a[0] * b[1] - a[1] * b[0]


def small_solve(beta, a, b, c, d, e):
    gram_first = a[0] * a[0] + a[1] * a[1] + c * c
    gram_second = b[0] * b[0] + b[1] * b[1] + d[0] * d[0] + d[1] * d[1] + e * e
    cross = conj_cmul(a, b)
    cross = (cross[0] + c * d[0], cross[1] + c * d[1])
    ad = cmul(a, d)
    minor = (ad[0] - b[0] * c, ad[1] - b[1] * c)
    determinant = (
        minor[0] * minor[0]
        + minor[1] * minor[1]
        + (a[0] * a[0] + a[1] * a[1]) * e * e
        + c * c * e * e
    )
    first = (beta * a[0], -beta * a[1])
    second = (beta * b[0], -beta * b[1])
    t = cmul(cross, second)
    y0 = ((gram_second * first[0] - t[0]) / determinant, (gram_second * first[1] - t[1]) / determinant)
    t = conj_cmul(cross, first)
    y1 = ((gram_first * second[0] - t[0]) / determinant, (gram_first * second[1] - t[1]) / determinant)
    return y0, y1


def kernel(
    row_count,
    col_count,
    kept,
    forcing,
    medium,
    mask,
    source_rows,
    source_cols,
    refraction,
    lift_scalars,
    bias_scalars,
    lift_weight,
    lift_bias,
    spectral_weight,
    point_weight,
    layer_bias,
    project_weight,
    table_high,
    table_low,
    table_back,
    phases,
    solution_ref,
    residual_ref,
    fwd_high,
    fwd_low,
    phase,
    weights,
    mode_map,
    project_map,
    wave_ref,
    feature_ref,
    right_ref,
    even_cols,
    odd_cols,
    mixed,
    fixed,
    modes,
    high,
    low,
    send_feat,
    got_feat,
    all_feat,
    send_wave,
    got_wave,
    all_wave,
    got_scal,
    col_scal,
    before,
    ext,
    applied,
    basis,
    half_ref,
    table_sems,
    halo_send,
    halo_recv,
    send_sems,
    recv_sems,
):
    lines, columns = mask.shape
    channels = point_weight.shape[0]
    groups = lines // LINES
    double = 2 * kept
    wide = SLABS * LINES
    half = columns // 2
    row = lax.axis_index("row")
    col = lax.axis_index("col")
    grid_scale = math.sqrt(lines * col_count * columns * row_count)

    table_copies = [
        pltpu.make_async_copy(table_high, fwd_high, table_sems.at[0]),
        pltpu.make_async_copy(table_low, fwd_low, table_sems.at[1]),
        pltpu.make_async_copy(phases.at[row], phase, table_sems.at[2]),
    ]
    back_copies = [
        copy
        for g in range(groups)
        for copy in (
            pltpu.make_async_copy(table_back.at[0], even_cols.at[g, pl.ds(0, kept)], table_sems.at[4 + 2 * g]),
            pltpu.make_async_copy(table_back.at[1], odd_cols.at[g, pl.ds(wide, kept)], table_sems.at[5 + 2 * g]),
        )
    ]
    weight_copy = pltpu.make_async_copy(spectral_weight, weights, table_sems.at[3])
    for copy in [*table_copies, weight_copy, *back_copies]:
        copy.start()

    barrier = pltpu.get_barrier_semaphore()
    greeted = 0
    for d in range(1, row_count):
        pl.semaphore_signal(
            barrier, inc=1, device_id={"row": lax.rem(row + d, row_count)}, device_id_type=MESH
        )
        greeted += 1
    for d in range(1, col_count):
        pl.semaphore_signal(
            barrier, inc=1, device_id={"col": lax.rem(col + d, col_count)}, device_id_type=MESH
        )
        greeted += 1
    for dr in (1, row_count - 1):
        for dc in (1, col_count - 1):
            pl.semaphore_signal(
                barrier,
                inc=1,
                device_id={
                    "row": lax.rem(row + dr, row_count),
                    "col": lax.rem(col + dc, col_count),
                },
                device_id_type=MESH,
            )
            greeted += 1

    def spread(source, target, index, axis, me, count):
        for d in range(1, count):
            there = lax.rem(me + d, count)
            pltpu.make_async_remote_copy(
                src_ref=source(there),
                dst_ref=target.at[me],
                send_sem=send_sems.at[index],
                recv_sem=recv_sems.at[index],
                device_id={axis: there},
                device_id_type=MESH,
            ).start()

    def arrived(target, index, count, sems):
        whole = target.at[pl.ds(0, count - 1)]
        pltpu.make_async_copy(whole, whole, sems.at[index]).wait()

    def forward(kind, out):
        spectrum = (
            jnp.dot(high[kind], fwd_high[...], preferred_element_type=F32)
            + jnp.dot(high[kind], fwd_low[...], preferred_element_type=F32)
            + jnp.dot(low[kind], fwd_high[...], preferred_element_type=F32)
        )
        cosine, sine = phase[0:1, :kept], phase[0:1, kept:double]
        re, im = spectrum[:, :kept], spectrum[:, kept:]
        out[:, :, 0:kept] = (re * cosine + im * sine).reshape(row_count, 8, kept)
        out[:, :, kept:double] = (im * cosine - re * sine).reshape(row_count, 8, kept)

    def unrotated(both):
        cosine, sine = phase[0:1, double : double + kept], phase[0:1, double + kept :]
        re, im = both[:, :kept], both[:, kept:]
        return re * cosine - im * sine, im * cosine + re * sine

    flip = jnp.where(
        lax.broadcasted_iota(jnp.int32, (128, 128), 0)
        + lax.broadcasted_iota(jnp.int32, (128, 128), 1)
        == 127,
        1.0,
        0.0,
    ).astype(BF16)

    def reversed_lanes(x):
        height, blocks = x.shape[0], x.shape[1] // 128
        parts = [
            part[:, 128 * i : 128 * i + 128] for part in three_way(x) for i in reversed(range(blocks))
        ]
        turned = jnp.dot(jnp.concatenate(parts, axis=0), flip, preferred_element_type=F32)
        pieces = turned.reshape(3, blocks, height, 128)
        total = pieces[0] + pieces[1] + pieces[2]
        return jnp.concatenate([total[i] for i in range(blocks)], axis=1)

    def slab(g, j, even, odd):
        even_cols[g, kept + LINES * j : kept + LINES * (j + 1), :] = even
        odd_cols[g, LINES * j : LINES * (j + 1), :] = odd

    def halves(value):
        right, left = value[:, half:], reversed_lanes(value[:, :half])
        return 0.5 * (right + left), 0.5 * (right - left)

    def field_slabs(g, j, even, odd):
        even, odd = split(even), split(odd)
        slab(g, j, even[0], odd[0])
        slab(g, j + 1, even[1], odd[1])
        slab(g, j + 2, even[0], odd[0])

    def keep_halves(which, source):
        for g in range(groups):
            for p in range(2):
                even, odd = halves(source[p, rows_of(g), :])
                half_ref[which, 0, p, rows_of(g), :] = even
                half_ref[which, 1, p, rows_of(g), :] = odd

    def rows_of(g):
        return slice(LINES * g, LINES * (g + 1))

    def folded(x):
        total = jnp.zeros((8, 128), F32)
        for i in range(x.shape[0] // 8):
            for j in range(x.shape[1] // 128):
                total = total + x[8 * i : 8 * i + 8, 128 * j : 128 * j + 128]
        return total

    def scalar_tile(parts):
        place = lax.broadcasted_iota(jnp.int32, (8, 128), 0)
        tile = jnp.zeros((8, 128), F32)
        for i, part in enumerate(parts):
            tile = jnp.where(place == i, jnp.sum(part, axis=0, keepdims=True), tile)
        return tile

    for g in range(groups):
        lines_of = rows_of(g)
        kind = medium[lines_of, :]
        refractive = jnp.zeros((LINES, columns), F32)
        for level in range(refraction.shape[0]):
            refractive = jnp.where(kind == level, refraction[level], refractive)
        damping = 0.1 + mask[lines_of, :].astype(F32)
        scaled = wave_base * refractive
        wave_ref[lines_of, :] = scaled * scaled
        feature_ref[0, lines_of, :] = refractive
        feature_ref[1, lines_of, :] = damping
        for i, feature in enumerate((refractive, damping)):
            top, rest = split(feature)
            place = slice(lines * i + LINES * g, lines * i + LINES * (g + 1))
            high[0, place, :] = top
            low[0, place, :] = rest
    for copy in table_copies:
        copy.wait()
    forward(0, send_feat)
    pl.semaphore_wait(barrier, greeted)
    spread(lambda there: send_feat.at[there], got_feat, 0, "row", row, row_count)

    sources = source_rows.shape[0]
    place = lax.broadcasted_iota(jnp.int32, (sources, 128), 0)
    col_of = jnp.zeros((sources, 128), jnp.int32)
    for i in range(sources):
        col_of = jnp.where(place == i, source_cols[i] - columns * row, col_of)
    lane = lax.broadcasted_iota(jnp.int32, (sources, 128), 1)
    col_hits = jnp.concatenate(
        [jnp.where(col_of == lane + 128 * j, 1.0, 0.0) for j in range(columns // 128)], axis=1
    ).astype(BF16)
    place = lax.broadcasted_iota(jnp.int32, (lines, sources), 1)
    row_of = jnp.zeros((lines, sources), jnp.int32)
    for i in range(sources):
        row_of = jnp.where(place == i, source_rows[i] - lines * col, row_of)
    line_hits = jnp.where(
        row_of == lax.broadcasted_iota(jnp.int32, (lines, sources), 0), 1.0, 0.0
    ).astype(BF16)
    source_count = jnp.dot(line_hits, col_hits, preferred_element_type=F32)
    square = jnp.zeros((8, 128), F32)
    for g in range(groups):
        lines_of = rows_of(g)
        for p in range(2):
            field = forcing[p, lines_of, :]
            if p == 0:
                field = field + source_gain * source_count[lines_of, :]
            right_ref[p, lines_of, :] = field
            square = square + folded(field * field)
            top, rest = split(field)
            high[1, p * lines + LINES * g : p * lines + LINES * (g + 1), :] = top
            low[1, p * lines + LINES * g : p * lines + LINES * (g + 1), :] = rest
    def send_modes(step, tile):
        forward(1, send_wave.at[step])
        for r in range(row_count):
            send_wave[step, r, :, double:] = tile
        spread(
            lambda there: send_wave.at[step, there], got_wave.at[step], 2 + 3 * step, "row", row, row_count
        )

    send_modes(0, scalar_tile([square]))

    mode_of = lax.broadcasted_iota(jnp.int32, (1, 128), 1)

    def fold(ob, kc):
        outs, some = pl.ds(16 * ob, 16), pl.ds(128 * kc, 128)
        used = 5 if kc == 0 else 4
        twice = jnp.where(mode_of == 0, 1.0, 2.0) if kc == 0 else 2.0
        both = []
        for part in range(2):

            def one_channel(c, sums):
                weight = weights[part, c, outs, some].astype(F32)
                factors = [lift_scalars[g, c] for g in range(4)] + [bias_scalars[c]]
                return tuple(x + f * weight for x, f in zip(sums, factors))

            both.append(
                lax.fori_loop(
                    0, channels, one_channel, (jnp.zeros((16, 128), F32),) * used, unroll=8
                )
            )
        for g in range(4):
            re, im = both[0][g] * twice, both[1][g] * twice
            mode_map[0, g, outs, some] = re
            mode_map[1, g, outs, some] = re + im
            mode_map[2, g, outs, some] = im - re
        anchor = jnp.where(mode_of == 0, math.sqrt(columns * row_count), 0.0)
        for part in range(2):
            mode_map[part, 4, outs, some] = (
                both[part][4] * anchor if kc == 0 else jnp.zeros((16, 128), F32)
            )

    def reduced(got, source):
        got[row] = source[row]
        total = got[0]
        for r in range(1, row_count):
            total = total + got[r]
        return total

    blocks = [(ob, kc) for ob in range(channels // 16) for kc in range(kept // 128)]
    weight_copy.wait()
    for block in blocks[: len(blocks) // 2]:
        fold(*block)
    arrived(got_feat, 0, row_count, recv_sems)
    all_feat[row] = reduced(got_feat, send_feat)
    spread(lambda there: all_feat.at[row], all_feat, 1, "row", row, row_count)

    def wave_reduce(step):
        index = 2 + 3 * step
        arrived(got_wave.at[step], index, row_count, recv_sems)
        total = reduced(got_wave.at[step], send_wave.at[step])
        all_wave[step, row] = total[:, :double]
        spread(
            lambda there: all_wave.at[step, row], all_wave.at[step], index + 1, "row", row, row_count
        )
        col_scal[step, col] = total[:, double:]
        spread(
            lambda there: col_scal.at[step, col], col_scal.at[step], index + 2, "col", col, col_count
        )

    def col_total(step):
        arrived(col_scal.at[step], 4 + 3 * step, col_count, recv_sems)
        total = col_scal[step, 0]
        for r in range(1, col_count):
            total = total + col_scal[step, r]
        return jnp.sum(total, axis=1, keepdims=True)

    def mix_lines(first, count, kc, ob, channels_in, bias, source, store):
        low_k, high_k = pl.ds(128 * kc, 128), pl.ds(kept + 128 * kc, 128)
        store_k = pl.ds(store.shape[2] - kept + 128 * kc, 128)
        outs = pl.ds(16 * ob, 16)
        maps = [tuple(mode_map[i, g, outs, low_k] for i in range(3)) for g in channels_in]
        start = (mode_map[0, 4, outs, low_k], mode_map[1, 4, outs, low_k]) if bias else None
        for block in range(count // 8):
            top = first + 8 * block
            parts = [
                (modes[g, pl.ds(top, 8), low_k], modes[g, pl.ds(top, 8), high_k]) for g in channels_in
            ]
            parts = [(mode_re, mode_im, mode_re + mode_im) for mode_re, mode_im in parts]
            for i in range(8):
                line = top + i
                if bias:
                    re, im = start
                else:
                    re, im = source[line, outs, low_k], source[line, outs, high_k]
                shared = None
                for (mode_re, mode_im, mode_sum), (map_re, map_sum, map_less) in zip(parts, maps):
                    product = map_re * mode_sum[i : i + 1]
                    shared = product if shared is None else shared + product
                    re = re - map_sum * mode_im[i : i + 1]
                    im = im + map_less * mode_re[i : i + 1]
                re, im = re + shared, im + shared
                store[line, outs, low_k] = re.astype(store.dtype)
                store[line, outs, store_k] = im.astype(store.dtype)

    def mix_fixed():
        for kc in range(kept // 128):
            for ob in range(channels // 16):

                def eight_lines(block, carry):
                    first = pl.multiple_of(8 * block, 8)
                    mix_lines(first, 8, kc, ob, (2, 3), True, None, fixed)
                    return carry

                lax.fori_loop(0, lines // 8, eight_lines, 0)

    def mix_group(g):
        for kc in range(kept // 128):
            for ob in range(channels // 16):
                mix_lines(LINES * g, LINES, kc, ob, (0, 1), False, fixed, mixed)

    def layer(step):
        outer = half // PIECE - 1
        edges = [(g, outer) for g in range(groups)]
        ends = [(g, n) for g in sorted({0, groups - 1}) for n in range(outer)]
        inside = [(g, n) for g in range(1, groups - 1) for n in range(outer)]
        order = edges + ends + inside

        def multiply(g, n, slot):
            left = mixed[LINES * g : LINES * (g + 1)].reshape(LINES * channels, double + wide)
            piece = slice(PIECE * n, PIECE * (n + 1))
            before[slot, 0] = jnp.dot(
                left[:, : kept + wide], even_cols[g, :, piece], preferred_element_type=F32
            )
            before[slot, 1] = jnp.dot(
                left[:, kept:], odd_cols[g, :, piece], preferred_element_type=F32
            )

        def finish(g, n, slot):
            lines_of = slice(8 + LINES * g, 8 + LINES * (g + 1))
            even, odd = before[slot, 0], before[slot, 1]
            for side in range(2):
                active = scaled_gelu(even + odd if side else even - odd).astype(BF16)
                out = jnp.dot(project_map[...], active, preferred_element_type=F32)
                out = out * math.sqrt(0.5)
                if side:
                    first = 128 + half + PIECE * n
                else:
                    first = 128 + half - PIECE * (n + 1)
                    out = reversed_lanes(out)
                place = slice(first, first + PIECE)
                ext[step, 0, lines_of, place] = out[:LINES]
                ext[step, 1, lines_of, place] = out[LINES:]

        mix_group(0)
        for t in range(len(order) + 1):
            if t < len(order):
                g, n = order[t]
                multiply(g, n, t % 2)
                if t < len(edges) and g + 1 < groups:
                    mix_group(g + 1)
            if t > 0:
                finish(*order[t - 1], (t - 1) % 2)
            if t == len(edges):
                for copy in halo_copies(step, (0, 1, 4, 5, 6, 7)):
                    copy.start()
            if t == len(edges) + len(ends):
                for copy in halo_copies(step, (2, 3)):
                    copy.start()

    def halo_copies(step, wanted):
        tall, across_all = pl.ds(8, lines), pl.ds(128, columns)
        line_ends = {
            1: (pl.ds(7 + lines, 1), pl.ds(7, 1)),
            -1: (pl.ds(8, 1), pl.ds(8 + lines, 1)),
            0: (tall, tall),
        }
        col_ends = {
            1: (pl.ds(columns, 128), pl.ds(0, 128)),
            -1: (pl.ds(128, 128), pl.ds(128 + columns, 128)),
            0: (across_all, across_all),
        }
        copies = []
        for i, (dr, dc) in enumerate(
            [(1, 0), (-1, 0), (0, 1), (0, -1), (1, 1), (1, -1), (-1, 1), (-1, -1)]
        ):
            if i not in wanted:
                continue
            here_l, there_l = line_ends[dc]
            here_c, there_c = col_ends[dr]
            copies.append(
                pltpu.make_async_remote_copy(
                    src_ref=ext.at[step, :, here_l, here_c],
                    dst_ref=ext.at[step, :, there_l, there_c],
                    send_sem=halo_send.at[step, i],
                    recv_sem=halo_recv.at[step, i],
                    device_id={
                        "row": lax.rem(row + dr + row_count, row_count),
                        "col": lax.rem(col + dc + col_count, col_count),
                    },
                    device_id_type=MESH,
                )
            )
        return copies

    def side_halos(step):
        for copy in halo_copies(step, (0, 1, 4, 5, 6, 7)):
            copy.wait()
        view = ext.at[step]

        @pl.when(row == 0)
        def _():
            view[:, :, 0:128] = jnp.zeros((2, lines + 16, 128), F32)

        @pl.when(row == row_count - 1)
        def _():
            view[:, :, 128 + columns :] = jnp.zeros((2, lines + 16, 128), F32)

    def line_halos(step):
        for copy in halo_copies(step, (2, 3)):
            copy.wait()
        view = ext.at[step]

        @pl.when(col == 0)
        def _():
            view[:, 0:8, :] = jnp.zeros((2, 8, columns + 256), F32)

        @pl.when(col == col_count - 1)
        def _():
            view[:, 8 + lines :, :] = jnp.zeros((2, 8, columns + 256), F32)

    def operated(step, each):
        side_halos(step)
        for g in range(1, groups - 1):
            each(g)
        line_halos(step)
        for g in sorted({0, groups - 1}):
            each(g)

    def operate(step, g):
        laps, fields = [], []
        for p in range(2):
            first = 8 + LINES * g
            beside = (
                ext[step, p, first - 1 : first - 1 + LINES, :]
                + ext[step, p, first + 1 : first + 1 + LINES, :]
            )
            centre = ext[step, p, first : first + LINES, :]
            both = 4.0 * centre + beside
            width = columns + 256
            around = pltpu.roll(both, 1, 1) + pltpu.roll(both, width - 1, 1)
            total = (4.0 * beside - 20.0 * centre + around) * (1.0 / 6.0)
            laps.append(total[:, 128 : 128 + columns])
            fields.append(centre[:, 128 : 128 + columns])
        wave, damping = wave_ref[rows_of(g), :], feature_ref[1, rows_of(g), :]
        real = -laps[0] - wave * (fields[0] + damping * fields[1])
        imag = -laps[1] - wave * (fields[1] - damping * fields[0])
        return real, imag

    def pair(first, second):
        return (
            folded(first[0] * second[0] + first[1] * second[1]),
            folded(first[0] * second[1] - first[1] * second[0]),
        )

    def add(a, b):
        return [x + y for x, y in zip(a, b)]

    for block in blocks[len(blocks) // 2 :]:
        fold(*block)
    wave_reduce(0)

    lift = jnp.concatenate(
        [lift_weight[...], lift_bias[...], jnp.zeros((3, channels), F32)], axis=0
    )
    lift_parts = three_way(lift)
    point = jnp.zeros((8, channels), F32)
    for part in lift_parts:
        point = point + jnp.dot(part, point_weight[...], preferred_element_type=F32)
    channel_row = lax.broadcasted_iota(jnp.int32, (8, channels), 0)
    point = (point + jnp.where(channel_row == 4, layer_bias[...], 0.0)) * math.sqrt(0.5)
    top, rest = split(point)
    from_row = lax.broadcasted_iota(jnp.int32, (8, wide), 0)
    slab_of = lax.broadcasted_iota(jnp.int32, (8, wide), 1) // LINES
    first_slab = 3 * from_row
    pick_top = ((slab_of == first_slab) | ((slab_of == first_slab + 1) & (from_row < 4))) & (from_row < 5)
    pick_rest = ((slab_of == first_slab + 2) & (from_row < 4)) | ((slab_of == 13) & (from_row == 4))
    over_rows = (((0,), (0,)), ((), ()))
    spread_out = lax.dot_general(
        top.astype(F32), jnp.where(pick_top, 1.0, 0.0), over_rows, preferred_element_type=F32
    ) + lax.dot_general(
        rest.astype(F32), jnp.where(pick_rest, 1.0, 0.0), over_rows, preferred_element_type=F32
    )
    line_of = lax.broadcasted_iota(jnp.int32, (channels, wide), 1) % LINES
    for i in range(LINES):
        masked = jnp.where(line_of == i, spread_out, 0.0).astype(BF16)
        for g in range(groups):
            mixed[LINES * g + i, :, kept : kept + wide] = masked
    all_rows = LINES * channels
    tiles = jnp.where(
        lax.broadcasted_iota(jnp.int32, (channels, all_rows), 0)
        == lax.broadcasted_iota(jnp.int32, (channels, all_rows), 1) % channels,
        1.0,
        0.0,
    )
    across = lax.dot_general(
        project_weight[...].astype(F32), tiles, (((1,), (0,)), ((), ())), preferred_element_type=F32
    )
    own_line = (
        lax.broadcasted_iota(jnp.int32, (LINES, all_rows), 0)
        == lax.broadcasted_iota(jnp.int32, (LINES, all_rows), 1) // channels
    )
    for p in range(2):
        project_map[LINES * p : LINES * (p + 1), :] = jnp.where(
            own_line, across[p : p + 1, :], 0.0
        ).astype(BF16)

    for g in range(groups):
        ones = jnp.ones((LINES, half), BF16)
        zeros = jnp.zeros_like(ones)
        slab(g, 12, ones, zeros)
        slab(g, 13, ones, zeros)
        slab(g, 14, zeros, zeros)
        slab(g, 15, zeros, zeros)
        for i in range(2):
            field_slabs(g, 6 + 3 * i, *halves(feature_ref[i, rows_of(g), :]))
    keep_halves(0, right_ref)

    arrived(all_feat, 1, row_count, recv_sems)
    re, im = unrotated(all_feat[...].reshape(2 * lines, double))
    for g in range(2):
        modes[2 + g, :, :kept] = re[g * lines : (g + 1) * lines]
        modes[2 + g, :, kept:] = im[g * lines : (g + 1) * lines]
    mix_fixed()
    for copy in back_copies:
        copy.wait()

    arrived(all_wave.at[0], 3, row_count, recv_sems)
    total_square = col_total(0)[0:1, :]
    beta = jnp.sqrt(total_square + norm_eps)
    inverse_beta = 1.0 / beta
    re, im = unrotated(all_wave[0].reshape(2 * lines, double))
    for p in range(2):
        modes[p, :, :kept] = re[p * lines : (p + 1) * lines] * (grid_scale * inverse_beta)
        modes[p, :, kept:] = im[p * lines : (p + 1) * lines] * (grid_scale * inverse_beta)
    for g in range(groups):
        for p in range(2):
            even, odd = (
                half_ref[0, i, p, rows_of(g), :] * (grid_scale * inverse_beta) for i in range(2)
            )
            field_slabs(g, 3 * p, even, odd)
    layer(0)
    sums = [jnp.zeros((8, 128), F32)] * 3

    def first_applied(g):
        lines_of = rows_of(g)
        result = operate(0, g)
        for p in range(2):
            applied[0, p, lines_of, :] = result[p]
            top, rest = split(result[p])
            high[1, p * lines + LINES * g : p * lines + LINES * (g + 1), :] = top
            low[1, p * lines + LINES * g : p * lines + LINES * (g + 1), :] = rest
        start = (right_ref[0, lines_of, :], right_ref[1, lines_of, :])
        square = folded(result[0] * result[0] + result[1] * result[1])
        sums[:] = add(sums, (*pair(start, result), square))

    operated(0, first_applied)
    send_modes(1, scalar_tile(sums))
    keep_halves(1, applied.at[0])
    wave_reduce(1)
    arrived(all_wave.at[1], 6, row_count, recv_sems)
    totals = col_total(1)
    unit_square = total_square * inverse_beta * inverse_beta
    a = (totals[0:1, :] * inverse_beta, totals[1:2, :] * inverse_beta)
    a_square = a[0] * a[0] + a[1] * a[1]
    rest_square = jnp.maximum(totals[2:3, :] - a_square * (2.0 - unit_square), 0.0)
    c = jnp.sqrt(rest_square + norm_eps)
    inverse_c = 1.0 / c
    a_over = (a[0] * inverse_beta, a[1] * inverse_beta)

    def next_vector(w, v):
        scaled = cmul(a_over, v)
        return (w[0] - scaled[0]) * inverse_c, (w[1] - scaled[1]) * inverse_c

    old, new = (all_wave[i].reshape(2 * lines, double) for i in range(2))
    planes = next_vector((new[:lines], new[lines:]), (old[:lines], old[lines:]))
    for p in range(2):
        re, im = unrotated(planes[p])
        modes[p, :, :kept] = re * grid_scale
        modes[p, :, kept:] = im * grid_scale
    for g in range(groups):
        lines_of = rows_of(g)
        vector = next_vector(
            (applied[0, 0, lines_of, :], applied[0, 1, lines_of, :]),
            (right_ref[0, lines_of, :], right_ref[1, lines_of, :]),
        )
        for p in range(2):
            basis[p, lines_of, :] = vector[p]
        even, odd = (
            next_vector(
                [half_ref[1, i, p, lines_of, :] for p in range(2)],
                [half_ref[0, i, p, lines_of, :] for p in range(2)],
            )
            for i in range(2)
        )
        for p in range(2):
            field_slabs(g, 3 * p, even[p] * grid_scale, odd[p] * grid_scale)
    layer(1)
    sums = [jnp.zeros((8, 128), F32)] * 5

    def second_applied(g):
        lines_of = rows_of(g)
        result = operate(1, g)
        for p in range(2):
            applied[1, p, lines_of, :] = result[p]
        start = (right_ref[0, lines_of, :], right_ref[1, lines_of, :])
        vector = (basis[0, lines_of, :], basis[1, lines_of, :])
        square = folded(result[0] * result[0] + result[1] * result[1])
        sums[:] = add(sums, (*pair(start, result), *pair(vector, result), square))

    operated(1, second_applied)
    got_scal[row] = scalar_tile(sums)
    spread(lambda there: got_scal.at[row], got_scal, 8, "row", row, row_count)
    arrived(got_scal, 8, row_count, recv_sems)
    total = got_scal[0]
    for r in range(1, row_count):
        total = total + got_scal[r]
    col_scal[2, col] = total
    spread(lambda there: col_scal.at[2, col], col_scal.at[2], 9, "col", col, col_count)
    arrived(col_scal.at[2], 9, col_count, recv_sems)
    total = col_scal[2, 0]
    for r in range(1, col_count):
        total = total + col_scal[2, r]
    totals = jnp.sum(total, axis=1, keepdims=True)
    b = (totals[0:1, :] * inverse_beta, totals[1:2, :] * inverse_beta)
    d = (totals[2:3, :], totals[3:4, :])
    b_square = b[0] * b[0] + b[1] * b[1]
    d_square = d[0] * d[0] + d[1] * d[1]
    second_square = rest_square * inverse_c * inverse_c
    overlap = (norm_eps * inverse_beta * inverse_beta) * inverse_c
    between = conj_cmul(b, d)
    between = between[0] * a[0] - between[1] * a[1]
    last_square = (
        totals[4:5, :]
        - b_square * (2.0 - unit_square)
        - d_square * (2.0 - second_square)
        + 2.0 * overlap * between
    )
    e = jnp.sqrt(jnp.maximum(last_square, 0.0) + norm_eps)
    y0, y1 = small_solve(beta, a, b, c, d, e)
    for g in range(groups):
        lines_of = rows_of(g)
        inner = slice(8 + LINES * g, 8 + LINES * (g + 1))
        z0, z1, w0, w1 = (
            [ext[0, p, inner, 128 : 128 + columns] for p in range(2)],
            [ext[1, p, inner, 128 : 128 + columns] for p in range(2)],
            [applied[0, p, lines_of, :] for p in range(2)],
            [applied[1, p, lines_of, :] for p in range(2)],
        )
        z0, z1, w0, w1 = cmul(y0, z0), cmul(y1, z1), cmul(y0, w0), cmul(y1, w1)
        for p in range(2):
            solution_ref[p, lines_of, :] = z0[p] + z1[p]
            residual_ref[p, lines_of, :] = right_ref[p, lines_of, :] - w0[p] - w1[p]

    arrived(got_feat, 0, row_count, send_sems)
    arrived(all_feat, 1, row_count, send_sems)
    for step in range(2):
        arrived(got_wave.at[step], 2 + 3 * step, row_count, send_sems)
        arrived(all_wave.at[step], 3 + 3 * step, row_count, send_sems)
        arrived(col_scal.at[step], 4 + 3 * step, col_count, send_sems)
    arrived(got_scal, 8, row_count, send_sems)
    arrived(col_scal.at[2], 9, col_count, send_sems)


def deliver(solution_in, residual_in, solution_out, residual_out, sems):
    copies = [
        pltpu.make_async_copy(solution_in, solution_out, sems.at[0]),
        pltpu.make_async_copy(residual_in, residual_out, sems.at[1]),
    ]
    for copy in copies:
        copy.start()
    for copy in copies:
        copy.wait()


def shards(
    row_count,
    col_count,
    kept,
    forcing,
    medium_index,
    absorbing_mask,
    source_rows,
    source_cols,
    refraction,
    lift_weight,
    lift_bias,
    spectral_weight,
    point_weight,
    layer_bias,
    project_weight,
):
    _, lines, columns = forcing.shape
    channels = point_weight.shape[0]
    grid_cols = columns * row_count
    groups = lines // LINES
    double = 2 * kept
    assert row_count * 8 == 2 * lines

    table_high, table_low = forward_tables(columns, kept, grid_cols)
    table_back = back_tables(columns, kept, grid_cols)
    phases = phase_table(row_count, columns, kept)

    field = jax.ShapeDtypeStruct((2, lines, columns), F32)
    vmem = pl.BlockSpec(memory_space=pltpu.VMEM)
    smem = pl.BlockSpec(memory_space=pltpu.SMEM)
    hbm = pl.BlockSpec(memory_space=pl.ANY)
    dma = pltpu.SemaphoreType.DMA
    results = pl.pallas_call(
        functools.partial(kernel, row_count, col_count, kept),
        out_shape=(pltpu.VMEM(field.shape, F32), pltpu.VMEM(field.shape, F32)),
        in_specs=[vmem] * 3 + [smem] * 5 + [vmem] * 2 + [hbm] + [vmem] * 3 + [hbm] * 4,
        out_specs=(vmem, vmem),
        scratch_shapes=[
            pltpu.VMEM((columns, double), BF16),
            pltpu.VMEM((columns, double), BF16),
            pltpu.VMEM((8, 2 * double), F32),
            pltpu.VMEM((2, channels, channels, kept), BF16),
            pltpu.VMEM((3, 5, channels, kept), F32),
            pltpu.VMEM((2 * LINES, LINES * channels), BF16),
            pltpu.VMEM((lines, columns), F32),
            pltpu.VMEM((2, lines, columns), F32),
            pltpu.VMEM((2, lines, columns), F32),
            pltpu.VMEM((groups, kept + SLABS * LINES, columns // 2), BF16),
            pltpu.VMEM((groups, kept + SLABS * LINES, columns // 2), BF16),
            pltpu.VMEM((lines, channels, double + SLABS * LINES), BF16),
            pltpu.VMEM((lines, channels, double), F32),
            pltpu.VMEM((4, lines, double), F32),
            pltpu.VMEM((2, 2 * lines, columns), BF16),
            pltpu.VMEM((2, 2 * lines, columns), BF16),
            pltpu.VMEM((row_count, 8, double), F32),
            pltpu.VMEM((row_count, 8, double), F32),
            pltpu.VMEM((row_count, 8, double), F32),
            pltpu.VMEM((2, row_count, 8, double + 128), F32),
            pltpu.VMEM((2, row_count, 8, double + 128), F32),
            pltpu.VMEM((2, row_count, 8, double), F32),
            pltpu.VMEM((row_count, 8, 128), F32),
            pltpu.VMEM((3, col_count, 8, 128), F32),
            pltpu.VMEM((2, 2, LINES * channels, PIECE), F32),
            pltpu.VMEM((2, 2, lines + 16, columns + 256), F32),
            pltpu.VMEM((2, 2, lines, columns), F32),
            pltpu.VMEM((2, lines, columns), F32),
            pltpu.VMEM((2, 2, 2, lines, columns // 2), F32),
            dma((4 + 2 * groups,)),
            dma((2, 8)),
            dma((2, 8)),
            dma((10,)),
            dma((10,)),
        ],
        compiler_params=pltpu.CompilerParams(
            collective_id=0, has_side_effects=True, vmem_limit_bytes=56 * 2**20
        ),
        name="krylov",
    )(
        forcing,
        medium_index,
        absorbing_mask,
        source_rows,
        source_cols,
        refraction,
        lift_weight,
        lift_bias,
        lift_weight,
        lift_bias.reshape(1, -1),
        spectral_weight.transpose(0, 2, 3, 1),
        point_weight,
        layer_bias.reshape(1, -1),
        project_weight.T,
        table_high,
        table_low,
        table_back,
        phases,
    )
    return pl.pallas_call(
        deliver,
        out_shape=(field, field),
        in_specs=[vmem] * 2,
        out_specs=[hbm] * 2,
        scratch_shapes=[dma((2,))],
        name="deliver",
    )(*[pltpu.with_memory_space_constraint(x, pltpu.VMEM) for x in results])


def solution(mesh):
    return jax.shard_map(
        functools.partial(shards, mesh.shape["row"], mesh.shape["col"], K),
        mesh=mesh,
        in_specs=(
            P(None, "col", "row"),
            P("col", "row"),
            P("col", "row"),
            P(),
            P(),
            P(),
            P(),
            P(),
            P(),
            P(),
            P(),
            P(),
        ),
        out_specs=(P(None, "col", "row"), P(None, "col", "row")),
        check_vma=False,
    )
```

```python
import functools
import math

import jax
import jax.numpy as jnp
import numpy as np
import ml_dtypes
from jax import lax
from jax.experimental import pallas as pl
from jax.experimental.pallas import tpu as pltpu
from jax.sharding import PartitionSpec as P

K = 256

wave_base = 0.23
source_gain = 8.0
norm_eps = 1e-06

MESH = pl.DeviceIdType.MESH
F32 = jnp.float32
BF16 = jnp.bfloat16
LINES = 16
SLABS = 16
PIECE = 256


def forward_tables(tile_cols, kept_modes, grid_cols):
    positions = np.arange(tile_cols, dtype=np.int64)
    mode_index = np.arange(kept_modes, dtype=np.int64)
    angles = (positions[:, None] * mode_index[None, :] % grid_cols) * (2.0 * math.pi / grid_cols)
    scale = 1.0 / math.sqrt(grid_cols)
    table = np.concatenate([np.cos(angles), -np.sin(angles)], axis=1) * scale
    high = table.astype(np.float32).astype(ml_dtypes.bfloat16)
    low = (table - high.astype(np.float64)).astype(np.float32).astype(ml_dtypes.bfloat16)
    return high, low


def back_tables(tile_cols, kept_modes, grid_cols):
    odd = 2 * np.arange(tile_cols // 2, dtype=np.int64) + 1
    mode_index = np.arange(kept_modes, dtype=np.int64)
    angles = (mode_index[:, None] * odd[None, :] % (2 * grid_cols)) * (math.pi / grid_cols)
    scale = math.sqrt(0.5 / grid_cols)
    table = np.stack([np.cos(angles), -np.sin(angles)]) * scale
    return table.astype(np.float32).astype(ml_dtypes.bfloat16)


def phase_table(row_count, tile_cols, kept_modes):
    grid_cols = row_count * tile_cols
    first = 2 * tile_cols * np.arange(row_count, dtype=np.int64)
    mode_index = np.arange(kept_modes, dtype=np.int64)
    parts = []
    for place in (first, first + tile_cols - 1):
        angles = (place[:, None] * mode_index[None, :] % (2 * grid_cols)) * (math.pi / grid_cols)
        parts += [np.cos(angles), np.sin(angles)]
    table = np.concatenate(parts, axis=1).astype(np.float32)
    return np.ascontiguousarray(np.broadcast_to(table[:, None, :], (row_count, 8, 4 * kept_modes)))


def split(x):
    high = x.astype(BF16)
    return high, (x - high.astype(F32)).astype(BF16)


def three_way(x):
    high, low = split(x)
    return high, low, (x - high.astype(F32) - low.astype(F32)).astype(BF16)


def scaled_gelu(z):
    return z + z * lax.erf(z)


def cmul(a, b):
    return a[0] * b[0] - a[1] * b[1], a[0] * b[1] + a[1] * b[0]


def conj_cmul(a, b):
    return a[0] * b[0] + a[1] * b[1], a[0] * b[1] - a[1] * b[0]


def small_solve(beta, a, b, c, d, e):
    gram_first = a[0] * a[0] + a[1] * a[1] + c * c
    gram_second = b[0] * b[0] + b[1] * b[1] + d[0] * d[0] + d[1] * d[1] + e * e
    cross = conj_cmul(a, b)
    cross = (cross[0] + c * d[0], cross[1] + c * d[1])
    ad = cmul(a, d)
    minor = (ad[0] - b[0] * c, ad[1] - b[1] * c)
    determinant = (
        minor[0] * minor[0]
        + minor[1] * minor[1]
        + (a[0] * a[0] + a[1] * a[1]) * e * e
        + c * c * e * e
    )
    first = (beta * a[0], -beta * a[1])
    second = (beta * b[0], -beta * b[1])
    t = cmul(cross, second)
    y0 = ((gram_second * first[0] - t[0]) / determinant, (gram_second * first[1] - t[1]) / determinant)
    t = conj_cmul(cross, first)
    y1 = ((gram_first * second[0] - t[0]) / determinant, (gram_first * second[1] - t[1]) / determinant)
    return y0, y1


def far_first(axis, me, count):
    inner = 2 if axis == "col" else 4
    if count % inner or count == inner:
        return [lax.rem(me + d, count) for d in range(1, count)]
    outer = count // inner

    def hops(step):
        a, b = step
        along = min(b, inner - b) if axis == "row" else 0.5 * b
        return min(a, outer - a) + along

    steps = [(a, b) for a in range(outer) for b in range(inner) if a or b]
    steps.sort(key=hops, reverse=True)
    return [
        lax.rem(me // inner + a, outer) * inner + lax.rem(lax.rem(me, inner) + b, inner)
        for a, b in steps
    ]


def kernel(
    row_count,
    col_count,
    kept,
    forcing_in,
    medium_in,
    mask_in,
    source_rows,
    source_cols,
    refraction,
    lift_scalars,
    bias_scalars,
    lift_weight,
    lift_bias,
    spectral_weight,
    point_weight,
    layer_bias,
    project_weight,
    table_high,
    table_low,
    table_back,
    phases,
    solution_ref,
    residual_ref,
    forcing,
    medium,
    mask,
    fwd_high,
    fwd_low,
    phase,
    weights,
    mode_map,
    project_map,
    wave_ref,
    feature_ref,
    right_ref,
    even_cols,
    odd_cols,
    mixed,
    fixed,
    modes,
    high,
    low,
    send_feat,
    got_feat,
    all_feat,
    send_wave,
    got_wave,
    all_wave,
    got_scal,
    col_scal,
    before,
    ext,
    applied,
    basis,
    half_ref,
    table_sems,
    halo_send,
    halo_recv,
    send_sems,
    recv_sems,
):
    lines, columns = mask.shape
    channels = point_weight.shape[0]
    groups = lines // LINES
    double = 2 * kept
    wide = SLABS * LINES
    half = columns // 2
    row = lax.axis_index("row")
    col = lax.axis_index("col")
    grid_scale = math.sqrt(lines * col_count * columns * row_count)

    first_load = 4 + 2 * groups
    media_copies = [
        pltpu.make_async_copy(medium_in, medium, table_sems.at[first_load]),
        pltpu.make_async_copy(mask_in, mask, table_sems.at[first_load + 1]),
    ]
    forcing_copy = pltpu.make_async_copy(forcing_in, forcing, table_sems.at[first_load + 2])
    table_copies = [
        pltpu.make_async_copy(table_high, fwd_high, table_sems.at[0]),
        pltpu.make_async_copy(table_low, fwd_low, table_sems.at[1]),
        pltpu.make_async_copy(phases.at[row], phase, table_sems.at[2]),
    ]
    back_copies = [
        copy
        for g in range(groups)
        for copy in (
            pltpu.make_async_copy(table_back.at[0], even_cols.at[g, pl.ds(0, kept)], table_sems.at[4 + 2 * g]),
            pltpu.make_async_copy(table_back.at[1], odd_cols.at[g, pl.ds(wide, kept)], table_sems.at[5 + 2 * g]),
        )
    ]
    weight_copy = pltpu.make_async_copy(spectral_weight, weights, table_sems.at[3])
    for copy in [*media_copies, *table_copies, forcing_copy, weight_copy, *back_copies]:
        copy.start()

    barrier = pltpu.get_barrier_semaphore()
    greeted = 0
    for d in range(1, row_count):
        pl.semaphore_signal(
            barrier, inc=1, device_id={"row": lax.rem(row + d, row_count)}, device_id_type=MESH
        )
        greeted += 1
    for d in range(1, col_count):
        pl.semaphore_signal(
            barrier, inc=1, device_id={"col": lax.rem(col + d, col_count)}, device_id_type=MESH
        )
        greeted += 1
    for dr in (1, row_count - 1):
        for dc in (1, col_count - 1):
            pl.semaphore_signal(
                barrier,
                inc=1,
                device_id={
                    "row": lax.rem(row + dr, row_count),
                    "col": lax.rem(col + dc, col_count),
                },
                device_id_type=MESH,
            )
            greeted += 1

    def spread(source, target, index, axis, me, count):
        for there in far_first(axis, me, count):
            pltpu.make_async_remote_copy(
                src_ref=source(there),
                dst_ref=target.at[me],
                send_sem=send_sems.at[index],
                recv_sem=recv_sems.at[index],
                device_id={axis: there},
                device_id_type=MESH,
            ).start()

    def arrived(target, index, count, sems):
        whole = target.at[pl.ds(0, count - 1)]
        pltpu.make_async_copy(whole, whole, sems.at[index]).wait()

    def forward(kind, out):
        spectrum = (
            jnp.dot(high[kind], fwd_high[...], preferred_element_type=F32)
            + jnp.dot(high[kind], fwd_low[...], preferred_element_type=F32)
            + jnp.dot(low[kind], fwd_high[...], preferred_element_type=F32)
        )
        cosine, sine = phase[0:1, :kept], phase[0:1, kept:double]
        re, im = spectrum[:, :kept], spectrum[:, kept:]
        out[:, :, 0:kept] = (re * cosine + im * sine).reshape(row_count, 8, kept)
        out[:, :, kept:double] = (im * cosine - re * sine).reshape(row_count, 8, kept)

    def unrotated(both):
        cosine, sine = phase[0:1, double : double + kept], phase[0:1, double + kept :]
        re, im = both[:, :kept], both[:, kept:]
        return re * cosine - im * sine, im * cosine + re * sine

    flip = jnp.where(
        lax.broadcasted_iota(jnp.int32, (128, 128), 0)
        + lax.broadcasted_iota(jnp.int32, (128, 128), 1)
        == 127,
        1.0,
        0.0,
    ).astype(BF16)

    def reversed_lanes(x):
        height, blocks = x.shape[0], x.shape[1] // 128
        parts = [
            part[:, 128 * i : 128 * i + 128] for part in three_way(x) for i in reversed(range(blocks))
        ]
        turned = jnp.dot(jnp.concatenate(parts, axis=0), flip, preferred_element_type=F32)
        pieces = turned.reshape(3, blocks, height, 128)
        total = pieces[0] + pieces[1] + pieces[2]
        return jnp.concatenate([total[i] for i in range(blocks)], axis=1)

    def slab(g, j, even, odd):
        even_cols[g, kept + LINES * j : kept + LINES * (j + 1), :] = even
        odd_cols[g, LINES * j : LINES * (j + 1), :] = odd

    def halves(value):
        right, left = value[:, half:], reversed_lanes(value[:, :half])
        return 0.5 * (right + left), 0.5 * (right - left)

    def field_slabs(g, j, even, odd):
        even, odd = split(even), split(odd)
        slab(g, j, even[0], odd[0])
        slab(g, j + 1, even[1], odd[1])
        slab(g, j + 2, even[0], odd[0])

    def keep_halves(which, source):
        for g in range(groups):
            for p in range(2):
                even, odd = halves(source[p, rows_of(g), :])
                half_ref[which, 0, p, rows_of(g), :] = even
                half_ref[which, 1, p, rows_of(g), :] = odd

    def rows_of(g):
        return slice(LINES * g, LINES * (g + 1))

    def folded(x):
        total = jnp.zeros((8, 128), F32)
        for i in range(x.shape[0] // 8):
            for j in range(x.shape[1] // 128):
                total = total + x[8 * i : 8 * i + 8, 128 * j : 128 * j + 128]
        return total

    def scalar_tile(parts):
        place = lax.broadcasted_iota(jnp.int32, (8, 128), 0)
        tile = jnp.zeros((8, 128), F32)
        for i, part in enumerate(parts):
            tile = jnp.where(place == i, jnp.sum(part, axis=0, keepdims=True), tile)
        return tile

    for copy in media_copies:
        copy.wait()
    for g in range(groups):
        lines_of = rows_of(g)
        kind = medium[lines_of, :]
        refractive = jnp.zeros((LINES, columns), F32)
        for level in range(refraction.shape[0]):
            refractive = jnp.where(kind == level, refraction[level], refractive)
        damping = 0.1 + mask[lines_of, :].astype(F32)
        scaled = wave_base * refractive
        wave_ref[lines_of, :] = scaled * scaled
        feature_ref[0, lines_of, :] = refractive
        feature_ref[1, lines_of, :] = damping
        for i, feature in enumerate((refractive, damping)):
            top, rest = split(feature)
            place = slice(lines * i + LINES * g, lines * i + LINES * (g + 1))
            high[0, place, :] = top
            low[0, place, :] = rest
    for copy in table_copies:
        copy.wait()
    forward(0, send_feat)
    pl.semaphore_wait(barrier, greeted)
    spread(lambda there: send_feat.at[there], got_feat, 0, "row", row, row_count)

    sources = source_rows.shape[0]
    place = lax.broadcasted_iota(jnp.int32, (sources, 128), 0)
    col_of = jnp.zeros((sources, 128), jnp.int32)
    for i in range(sources):
        col_of = jnp.where(place == i, source_cols[i] - columns * row, col_of)
    lane = lax.broadcasted_iota(jnp.int32, (sources, 128), 1)
    col_hits = jnp.concatenate(
        [jnp.where(col_of == lane + 128 * j, 1.0, 0.0) for j in range(columns // 128)], axis=1
    ).astype(BF16)
    place = lax.broadcasted_iota(jnp.int32, (lines, sources), 1)
    row_of = jnp.zeros((lines, sources), jnp.int32)
    for i in range(sources):
        row_of = jnp.where(place == i, source_rows[i] - lines * col, row_of)
    line_hits = jnp.where(
        row_of == lax.broadcasted_iota(jnp.int32, (lines, sources), 0), 1.0, 0.0
    ).astype(BF16)
    source_count = jnp.dot(line_hits, col_hits, preferred_element_type=F32)
    square = jnp.zeros((8, 128), F32)
    forcing_copy.wait()
    for g in range(groups):
        lines_of = rows_of(g)
        for p in range(2):
            field = forcing[p, lines_of, :]
            if p == 0:
                field = field + source_gain * source_count[lines_of, :]
            right_ref[p, lines_of, :] = field
            square = square + folded(field * field)
            top, rest = split(field)
            high[1, p * lines + LINES * g : p * lines + LINES * (g + 1), :] = top
            low[1, p * lines + LINES * g : p * lines + LINES * (g + 1), :] = rest
    def send_modes(step, tile):
        forward(1, send_wave.at[step])
        for r in range(row_count):
            send_wave[step, r, :, double:] = tile
        spread(
            lambda there: send_wave.at[step, there], got_wave.at[step], 2 + 3 * step, "row", row, row_count
        )

    send_modes(0, scalar_tile([square]))

    mode_of = lax.broadcasted_iota(jnp.int32, (1, 128), 1)

    def fold(ob, kc):
        outs, some = pl.ds(16 * ob, 16), pl.ds(128 * kc, 128)
        used = 5 if kc == 0 else 4
        twice = jnp.where(mode_of == 0, 1.0, 2.0) if kc == 0 else 2.0
        both = []
        for part in range(2):

            def one_channel(c, sums):
                weight = weights[part, c, outs, some].astype(F32)
                factors = [lift_scalars[g, c] for g in range(4)] + [bias_scalars[c]]
                return tuple(x + f * weight for x, f in zip(sums, factors))

            both.append(
                lax.fori_loop(
                    0, channels, one_channel, (jnp.zeros((16, 128), F32),) * used, unroll=8
                )
            )
        for g in range(4):
            re, im = both[0][g] * twice, both[1][g] * twice
            mode_map[0, g, outs, some] = re
            mode_map[1, g, outs, some] = re + im
            mode_map[2, g, outs, some] = im - re
        anchor = jnp.where(mode_of == 0, math.sqrt(columns * row_count), 0.0)
        for part in range(2):
            mode_map[part, 4, outs, some] = (
                both[part][4] * anchor if kc == 0 else jnp.zeros((16, 128), F32)
            )

    def reduced(got, source):
        got[row] = source[row]
        total = got[0]
        for r in range(1, row_count):
            total = total + got[r]
        return total

    blocks = [(ob, kc) for ob in range(channels // 16) for kc in range(kept // 128)]
    weight_copy.wait()
    for block in blocks[: len(blocks) // 2]:
        fold(*block)
    arrived(got_feat, 0, row_count, recv_sems)
    all_feat[row] = reduced(got_feat, send_feat)
    spread(lambda there: all_feat.at[row], all_feat, 1, "row", row, row_count)

    def wave_reduce(step):
        index = 2 + 3 * step
        arrived(got_wave.at[step], index, row_count, recv_sems)
        total = reduced(got_wave.at[step], send_wave.at[step])
        all_wave[step, row] = total[:, :double]
        spread(
            lambda there: all_wave.at[step, row], all_wave.at[step], index + 1, "row", row, row_count
        )
        col_scal[step, col] = total[:, double:]
        spread(
            lambda there: col_scal.at[step, col], col_scal.at[step], index + 2, "col", col, col_count
        )

    def col_total(step):
        arrived(col_scal.at[step], 4 + 3 * step, col_count, recv_sems)
        total = col_scal[step, 0]
        for r in range(1, col_count):
            total = total + col_scal[step, r]
        return jnp.sum(total, axis=1, keepdims=True)

    def mix_lines(first, count, kc, ob, channels_in, bias, source, store):
        low_k, high_k = pl.ds(128 * kc, 128), pl.ds(kept + 128 * kc, 128)
        store_k = pl.ds(store.shape[2] - kept + 128 * kc, 128)
        outs = pl.ds(16 * ob, 16)
        maps = [tuple(mode_map[i, g, outs, low_k] for i in range(3)) for g in channels_in]
        start = (mode_map[0, 4, outs, low_k], mode_map[1, 4, outs, low_k]) if bias else None
        for block in range(count // 8):
            top = first + 8 * block
            parts = [
                (modes[g, pl.ds(top, 8), low_k], modes[g, pl.ds(top, 8), high_k]) for g in channels_in
            ]
            parts = [(mode_re, mode_im, mode_re + mode_im) for mode_re, mode_im in parts]
            for i in range(8):
                line = top + i
                if bias:
                    re, im = start
                else:
                    re, im = source[line, outs, low_k], source[line, outs, high_k]
                shared = None
                for (mode_re, mode_im, mode_sum), (map_re, map_sum, map_less) in zip(parts, maps):
                    product = map_re * mode_sum[i : i + 1]
                    shared = product if shared is None else shared + product
                    re = re - map_sum * mode_im[i : i + 1]
                    im = im + map_less * mode_re[i : i + 1]
                re, im = re + shared, im + shared
                store[line, outs, low_k] = re.astype(store.dtype)
                store[line, outs, store_k] = im.astype(store.dtype)

    def mix_fixed():
        for kc in range(kept // 128):
            for ob in range(channels // 16):

                def eight_lines(block, carry):
                    first = pl.multiple_of(8 * block, 8)
                    mix_lines(first, 8, kc, ob, (2, 3), True, None, fixed)
                    return carry

                lax.fori_loop(0, lines // 8, eight_lines, 0)

    def mix_part(first, count):
        for kc in range(kept // 128):
            for ob in range(channels // 16):
                mix_lines(first, count, kc, ob, (0, 1), False, fixed, mixed)

    def layer(step):
        outer = half // PIECE - 1
        edges = [(0, outer, 0), (0, outer, 1)] + [(g, outer, None) for g in range(1, groups)]
        ends = [(g, n, None) for g in sorted({0, groups - 1}) for n in range(outer)]
        inside = [(g, n, None) for g in range(1, groups - 1) for n in range(outer)]
        if inside:
            g, n, _ = inside.pop()
            inside += [(g, n, 0), (g, n, 1)]
        order = edges + ends + inside
        departures = {edges[-1 - groups // 2]: (0, 1), edges[-1]: range(2, 8), ends[-1]: (8, 9)}

        def place_of(part):
            return (0, LINES) if part is None else (LINES // 2 * part, LINES // 2)

        def multiply(g, n, part, slot):
            offset, count = place_of(part)
            first = LINES * g + offset
            rows = channels * count
            left = mixed[first : first + count].reshape(rows, double + wide)
            piece = slice(PIECE * n, PIECE * (n + 1))
            before[slot, 0, :rows] = jnp.dot(
                left[:, : kept + wide], even_cols[g, :, piece], preferred_element_type=F32
            )
            before[slot, 1, :rows] = jnp.dot(
                left[:, kept:], odd_cols[g, :, piece], preferred_element_type=F32
            )

        def finish(g, n, part, slot):
            offset, count = place_of(part)
            first_line = 8 + LINES * g + offset
            lines_of = slice(first_line, first_line + count)
            rows = channels * count
            project = project_map[:, channels * offset : channels * offset + rows]
            even, odd = before[slot, 0, :rows], before[slot, 1, :rows]
            for side in range(2):
                active = scaled_gelu(even + odd if side else even - odd).astype(BF16)
                out = jnp.dot(project, active, preferred_element_type=F32)
                out = jnp.concatenate(
                    [out[LINES * p + offset : LINES * p + offset + count] for p in range(2)], axis=0
                )
                out = out * math.sqrt(0.5)
                if side:
                    first = 128 + half + PIECE * n
                else:
                    first = 128 + half - PIECE * (n + 1)
                    out = reversed_lanes(out)
                place = slice(first, first + PIECE)
                ext[step, 0, lines_of, place] = out[:count]
                ext[step, 1, lines_of, place] = out[count:]

        mix_part(0, LINES // 2)
        for t in range(len(order) + 1):
            if t < len(order):
                multiply(*order[t], t % 2)
                if t == 0:
                    mix_part(LINES // 2, LINES // 2)
                elif t < groups:
                    mix_part(LINES * t, LINES)
            if t > 0:
                finish(*order[t - 1], (t - 1) % 2)
                for copy in halo_copies(step, departures.get(order[t - 1], ())):
                    copy.start()

    def halo_copies(step, wanted):
        tall, across_all = pl.ds(8, lines), pl.ds(128, columns)
        line_ends = {
            1: (pl.ds(7 + lines, 1), pl.ds(7, 1)),
            -1: (pl.ds(8, 1), pl.ds(8 + lines, 1)),
            0: (tall, tall),
        }
        col_ends = {
            1: (pl.ds(columns, 128), pl.ds(0, 128)),
            -1: (pl.ds(128, 128), pl.ds(128 + columns, 128)),
            0: (across_all, across_all),
        }
        copies = []
        moves = [(1, 0), (-1, 0), (1, 0), (-1, 0), (1, 1), (1, -1), (-1, 1), (-1, -1), (0, 1), (0, -1)]
        for i in wanted:
            dr, dc = moves[i]
            here_l, there_l = line_ends[dc]
            if i < 4:
                here_l = there_l = pl.ds(8 + (i // 2) * (lines // 2), lines // 2)
            here_c, there_c = col_ends[dr]
            copies.append(
                pltpu.make_async_remote_copy(
                    src_ref=ext.at[step, :, here_l, here_c],
                    dst_ref=ext.at[step, :, there_l, there_c],
                    send_sem=halo_send.at[step, i],
                    recv_sem=halo_recv.at[step, i],
                    device_id={
                        "row": lax.rem(row + dr + row_count, row_count),
                        "col": lax.rem(col + dc + col_count, col_count),
                    },
                    device_id_type=MESH,
                )
            )
        return copies

    def side_halos(step):
        for copy in halo_copies(step, range(8)):
            copy.wait()
        view = ext.at[step]

        @pl.when(row == 0)
        def _():
            view[:, :, 0:128] = jnp.zeros((2, lines + 16, 128), F32)

        @pl.when(row == row_count - 1)
        def _():
            view[:, :, 128 + columns :] = jnp.zeros((2, lines + 16, 128), F32)

    def line_halos(step):
        for copy in halo_copies(step, (8, 9)):
            copy.wait()
        view = ext.at[step]

        @pl.when(col == 0)
        def _():
            view[:, 0:8, :] = jnp.zeros((2, 8, columns + 256), F32)

        @pl.when(col == col_count - 1)
        def _():
            view[:, 8 + lines :, :] = jnp.zeros((2, 8, columns + 256), F32)

    def operated(step, each):
        side_halos(step)
        for g in range(1, groups - 1):
            each(g)
        line_halos(step)
        for g in sorted({0, groups - 1}):
            each(g)

    def operate(step, g):
        laps, fields = [], []
        for p in range(2):
            first = 8 + LINES * g
            beside = (
                ext[step, p, first - 1 : first - 1 + LINES, :]
                + ext[step, p, first + 1 : first + 1 + LINES, :]
            )
            centre = ext[step, p, first : first + LINES, :]
            both = 4.0 * centre + beside
            width = columns + 256
            around = pltpu.roll(both, 1, 1) + pltpu.roll(both, width - 1, 1)
            total = (4.0 * beside - 20.0 * centre + around) * (1.0 / 6.0)
            laps.append(total[:, 128 : 128 + columns])
            fields.append(centre[:, 128 : 128 + columns])
        wave, damping = wave_ref[rows_of(g), :], feature_ref[1, rows_of(g), :]
        real = -laps[0] - wave * (fields[0] + damping * fields[1])
        imag = -laps[1] - wave * (fields[1] - damping * fields[0])
        return real, imag

    def pair(first, second):
        return (
            folded(first[0] * second[0] + first[1] * second[1]),
            folded(first[0] * second[1] - first[1] * second[0]),
        )

    def add(a, b):
        return [x + y for x, y in zip(a, b)]

    for block in blocks[len(blocks) // 2 :]:
        fold(*block)
    wave_reduce(0)

    lift = jnp.concatenate(
        [lift_weight[...], lift_bias[...], jnp.zeros((3, channels), F32)], axis=0
    )
    lift_parts = three_way(lift)
    point = jnp.zeros((8, channels), F32)
    for part in lift_parts:
        point = point + jnp.dot(part, point_weight[...], preferred_element_type=F32)
    channel_row = lax.broadcasted_iota(jnp.int32, (8, channels), 0)
    point = (point + jnp.where(channel_row == 4, layer_bias[...], 0.0)) * math.sqrt(0.5)
    top, rest = split(point)
    from_row = lax.broadcasted_iota(jnp.int32, (8, wide), 0)
    slab_of = lax.broadcasted_iota(jnp.int32, (8, wide), 1) // LINES
    first_slab = 3 * from_row
    pick_top = ((slab_of == first_slab) | ((slab_of == first_slab + 1) & (from_row < 4))) & (from_row < 5)
    pick_rest = ((slab_of == first_slab + 2) & (from_row < 4)) | ((slab_of == 13) & (from_row == 4))
    over_rows = (((0,), (0,)), ((), ()))
    spread_out = lax.dot_general(
        top.astype(F32), jnp.where(pick_top, 1.0, 0.0), over_rows, preferred_element_type=F32
    ) + lax.dot_general(
        rest.astype(F32), jnp.where(pick_rest, 1.0, 0.0), over_rows, preferred_element_type=F32
    )
    line_of = lax.broadcasted_iota(jnp.int32, (channels, wide), 1) % LINES
    for i in range(LINES):
        masked = jnp.where(line_of == i, spread_out, 0.0).astype(BF16)
        for g in range(groups):
            mixed[LINES * g + i, :, kept : kept + wide] = masked
    all_rows = LINES * channels
    tiles = jnp.where(
        lax.broadcasted_iota(jnp.int32, (channels, all_rows), 0)
        == lax.broadcasted_iota(jnp.int32, (channels, all_rows), 1) % channels,
        1.0,
        0.0,
    )
    across = lax.dot_general(
        project_weight[...].astype(F32), tiles, (((1,), (0,)), ((), ())), preferred_element_type=F32
    )
    own_line = (
        lax.broadcasted_iota(jnp.int32, (LINES, all_rows), 0)
        == lax.broadcasted_iota(jnp.int32, (LINES, all_rows), 1) // channels
    )
    for p in range(2):
        project_map[LINES * p : LINES * (p + 1), :] = jnp.where(
            own_line, across[p : p + 1, :], 0.0
        ).astype(BF16)

    for g in range(groups):
        ones = jnp.ones((LINES, half), BF16)
        zeros = jnp.zeros_like(ones)
        slab(g, 12, ones, zeros)
        slab(g, 13, ones, zeros)
        slab(g, 14, zeros, zeros)
        slab(g, 15, zeros, zeros)
        for i in range(2):
            field_slabs(g, 6 + 3 * i, *halves(feature_ref[i, rows_of(g), :]))
    keep_halves(0, right_ref)

    arrived(all_feat, 1, row_count, recv_sems)
    re, im = unrotated(all_feat[...].reshape(2 * lines, double))
    for g in range(2):
        modes[2 + g, :, :kept] = re[g * lines : (g + 1) * lines]
        modes[2 + g, :, kept:] = im[g * lines : (g + 1) * lines]
    mix_fixed()
    for copy in back_copies:
        copy.wait()

    total_square = col_total(0)[0:1, :]
    beta = jnp.sqrt(total_square + norm_eps)
    inverse_beta = 1.0 / beta
    for g in range(groups):
        for p in range(2):
            even, odd = (
                half_ref[0, i, p, rows_of(g), :] * (grid_scale * inverse_beta) for i in range(2)
            )
            field_slabs(g, 3 * p, even, odd)
    arrived(all_wave.at[0], 3, row_count, recv_sems)
    re, im = unrotated(all_wave[0].reshape(2 * lines, double))
    for p in range(2):
        modes[p, :, :kept] = re[p * lines : (p + 1) * lines] * (grid_scale * inverse_beta)
        modes[p, :, kept:] = im[p * lines : (p + 1) * lines] * (grid_scale * inverse_beta)
    layer(0)
    sums = [jnp.zeros((8, 128), F32)] * 3

    def first_applied(g):
        lines_of = rows_of(g)
        result = operate(0, g)
        for p in range(2):
            applied[0, p, lines_of, :] = result[p]
            top, rest = split(result[p])
            high[1, p * lines + LINES * g : p * lines + LINES * (g + 1), :] = top
            low[1, p * lines + LINES * g : p * lines + LINES * (g + 1), :] = rest
        start = (right_ref[0, lines_of, :], right_ref[1, lines_of, :])
        square = folded(result[0] * result[0] + result[1] * result[1])
        sums[:] = add(sums, (*pair(start, result), square))

    operated(0, first_applied)
    send_modes(1, scalar_tile(sums))
    keep_halves(1, applied.at[0])
    wave_reduce(1)
    totals = col_total(1)
    unit_square = total_square * inverse_beta * inverse_beta
    a = (totals[0:1, :] * inverse_beta, totals[1:2, :] * inverse_beta)
    a_square = a[0] * a[0] + a[1] * a[1]
    rest_square = jnp.maximum(totals[2:3, :] - a_square * (2.0 - unit_square), 0.0)
    c = jnp.sqrt(rest_square + norm_eps)
    inverse_c = 1.0 / c
    a_over = (a[0] * inverse_beta, a[1] * inverse_beta)

    def next_vector(w, v):
        scaled = cmul(a_over, v)
        return (w[0] - scaled[0]) * inverse_c, (w[1] - scaled[1]) * inverse_c

    for g in range(groups):
        lines_of = rows_of(g)
        vector = next_vector(
            (applied[0, 0, lines_of, :], applied[0, 1, lines_of, :]),
            (right_ref[0, lines_of, :], right_ref[1, lines_of, :]),
        )
        for p in range(2):
            basis[p, lines_of, :] = vector[p]
        even, odd = (
            next_vector(
                [half_ref[1, i, p, lines_of, :] for p in range(2)],
                [half_ref[0, i, p, lines_of, :] for p in range(2)],
            )
            for i in range(2)
        )
        for p in range(2):
            field_slabs(g, 3 * p, even[p] * grid_scale, odd[p] * grid_scale)
    arrived(all_wave.at[1], 6, row_count, recv_sems)
    old, new = (all_wave[i].reshape(2 * lines, double) for i in range(2))
    planes = next_vector((new[:lines], new[lines:]), (old[:lines], old[lines:]))
    for p in range(2):
        re, im = unrotated(planes[p])
        modes[p, :, :kept] = re * grid_scale
        modes[p, :, kept:] = im * grid_scale
    layer(1)
    sums = [jnp.zeros((8, 128), F32)] * 5

    def second_applied(g):
        lines_of = rows_of(g)
        result = operate(1, g)
        for p in range(2):
            applied[1, p, lines_of, :] = result[p]
        start = (right_ref[0, lines_of, :], right_ref[1, lines_of, :])
        vector = (basis[0, lines_of, :], basis[1, lines_of, :])
        square = folded(result[0] * result[0] + result[1] * result[1])
        sums[:] = add(sums, (*pair(start, result), *pair(vector, result), square))

    operated(1, second_applied)
    got_scal[row] = scalar_tile(sums)
    spread(lambda there: got_scal.at[row], got_scal, 8, "row", row, row_count)
    arrived(got_scal, 8, row_count, recv_sems)
    total = got_scal[0]
    for r in range(1, row_count):
        total = total + got_scal[r]
    col_scal[2, col] = total
    spread(lambda there: col_scal.at[2, col], col_scal.at[2], 9, "col", col, col_count)
    arrived(col_scal.at[2], 9, col_count, recv_sems)
    total = col_scal[2, 0]
    for r in range(1, col_count):
        total = total + col_scal[2, r]
    totals = jnp.sum(total, axis=1, keepdims=True)
    b = (totals[0:1, :] * inverse_beta, totals[1:2, :] * inverse_beta)
    d = (totals[2:3, :], totals[3:4, :])
    b_square = b[0] * b[0] + b[1] * b[1]
    d_square = d[0] * d[0] + d[1] * d[1]
    second_square = rest_square * inverse_c * inverse_c
    overlap = (norm_eps * inverse_beta * inverse_beta) * inverse_c
    between = conj_cmul(b, d)
    between = between[0] * a[0] - between[1] * a[1]
    last_square = (
        totals[4:5, :]
        - b_square * (2.0 - unit_square)
        - d_square * (2.0 - second_square)
        + 2.0 * overlap * between
    )
    e = jnp.sqrt(jnp.maximum(last_square, 0.0) + norm_eps)
    y0, y1 = small_solve(beta, a, b, c, d, e)
    for g in range(groups):
        lines_of = rows_of(g)
        inner = slice(8 + LINES * g, 8 + LINES * (g + 1))
        z0, z1, w0, w1 = (
            [ext[0, p, inner, 128 : 128 + columns] for p in range(2)],
            [ext[1, p, inner, 128 : 128 + columns] for p in range(2)],
            [applied[0, p, lines_of, :] for p in range(2)],
            [applied[1, p, lines_of, :] for p in range(2)],
        )
        z0, z1, w0, w1 = cmul(y0, z0), cmul(y1, z1), cmul(y0, w0), cmul(y1, w1)
        for p in range(2):
            solution_ref[p, lines_of, :] = z0[p] + z1[p]
            residual_ref[p, lines_of, :] = right_ref[p, lines_of, :] - w0[p] - w1[p]

    arrived(got_feat, 0, row_count, send_sems)
    arrived(all_feat, 1, row_count, send_sems)
    for step in range(2):
        arrived(got_wave.at[step], 2 + 3 * step, row_count, send_sems)
        arrived(all_wave.at[step], 3 + 3 * step, row_count, send_sems)
        arrived(col_scal.at[step], 4 + 3 * step, col_count, send_sems)
    arrived(got_scal, 8, row_count, send_sems)
    arrived(col_scal.at[2], 9, col_count, send_sems)


def deliver(solution_in, residual_in, solution_out, residual_out, sems):
    copies = [
        pltpu.make_async_copy(solution_in, solution_out, sems.at[0]),
        pltpu.make_async_copy(residual_in, residual_out, sems.at[1]),
    ]
    for copy in copies:
        copy.start()
    for copy in copies:
        copy.wait()


def shards(
    row_count,
    col_count,
    kept,
    forcing,
    medium_index,
    absorbing_mask,
    source_rows,
    source_cols,
    refraction,
    lift_weight,
    lift_bias,
    spectral_weight,
    point_weight,
    layer_bias,
    project_weight,
):
    _, lines, columns = forcing.shape
    channels = point_weight.shape[0]
    grid_cols = columns * row_count
    groups = lines // LINES
    double = 2 * kept
    assert row_count * 8 == 2 * lines

    table_high, table_low = forward_tables(columns, kept, grid_cols)
    table_back = back_tables(columns, kept, grid_cols)
    phases = phase_table(row_count, columns, kept)

    field = jax.ShapeDtypeStruct((2, lines, columns), F32)
    vmem = pl.BlockSpec(memory_space=pltpu.VMEM)
    smem = pl.BlockSpec(memory_space=pltpu.SMEM)
    hbm = pl.BlockSpec(memory_space=pl.ANY)
    dma = pltpu.SemaphoreType.DMA
    results = pl.pallas_call(
        functools.partial(kernel, row_count, col_count, kept),
        out_shape=(pltpu.VMEM(field.shape, F32), pltpu.VMEM(field.shape, F32)),
        in_specs=[hbm] * 3 + [smem] * 5 + [vmem] * 2 + [hbm] + [vmem] * 3 + [hbm] * 4,
        out_specs=(vmem, vmem),
        scratch_shapes=[
            pltpu.VMEM((2, lines, columns), F32),
            pltpu.VMEM((lines, columns), jnp.int32),
            pltpu.VMEM((lines, columns), jnp.int32),
            pltpu.VMEM((columns, double), BF16),
            pltpu.VMEM((columns, double), BF16),
            pltpu.VMEM((8, 2 * double), F32),
            pltpu.VMEM((2, channels, channels, kept), BF16),
            pltpu.VMEM((3, 5, channels, kept), F32),
            pltpu.VMEM((2 * LINES, LINES * channels), BF16),
            pltpu.VMEM((lines, columns), F32),
            pltpu.VMEM((2, lines, columns), F32),
            pltpu.VMEM((2, lines, columns), F32),
            pltpu.VMEM((groups, kept + SLABS * LINES, columns // 2), BF16),
            pltpu.VMEM((groups, kept + SLABS * LINES, columns // 2), BF16),
            pltpu.VMEM((lines, channels, double + SLABS * LINES), BF16),
            pltpu.VMEM((lines, channels, double), F32),
            pltpu.VMEM((4, lines, double), F32),
            pltpu.VMEM((2, 2 * lines, columns), BF16),
            pltpu.VMEM((2, 2 * lines, columns), BF16),
            pltpu.VMEM((row_count, 8, double), F32),
            pltpu.VMEM((row_count, 8, double), F32),
            pltpu.VMEM((row_count, 8, double), F32),
            pltpu.VMEM((2, row_count, 8, double + 128), F32),
            pltpu.VMEM((2, row_count, 8, double + 128), F32),
            pltpu.VMEM((2, row_count, 8, double), F32),
            pltpu.VMEM((row_count, 8, 128), F32),
            pltpu.VMEM((3, col_count, 8, 128), F32),
            pltpu.VMEM((2, 2, LINES * channels, PIECE), F32),
            pltpu.VMEM((2, 2, lines + 16, columns + 256), F32),
            pltpu.VMEM((2, 2, lines, columns), F32),
            pltpu.VMEM((2, lines, columns), F32),
            pltpu.VMEM((2, 2, 2, lines, columns // 2), F32),
            dma((7 + 2 * groups,)),
            dma((2, 10)),
            dma((2, 10)),
            dma((10,)),
            dma((10,)),
        ],
        compiler_params=pltpu.CompilerParams(
            collective_id=0, has_side_effects=True, vmem_limit_bytes=56 * 2**20
        ),
        name="krylov",
    )(
        forcing,
        medium_index,
        absorbing_mask,
        source_rows,
        source_cols,
        refraction,
        lift_weight,
        lift_bias,
        lift_weight,
        lift_bias.reshape(1, -1),
        spectral_weight.transpose(0, 2, 3, 1),
        point_weight,
        layer_bias.reshape(1, -1),
        project_weight.T,
        table_high,
        table_low,
        table_back,
        phases,
    )
    return pl.pallas_call(
        deliver,
        out_shape=(field, field),
        in_specs=[vmem] * 2,
        out_specs=[hbm] * 2,
        scratch_shapes=[dma((2,))],
        name="deliver",
    )(*[pltpu.with_memory_space_constraint(x, pltpu.VMEM) for x in results])


def solution(mesh):
    return jax.shard_map(
        functools.partial(shards, mesh.shape["row"], mesh.shape["col"], K),
        mesh=mesh,
        in_specs=(
            P(None, "col", "row"),
            P("col", "row"),
            P("col", "row"),
            P(),
            P(),
            P(),
            P(),
            P(),
            P(),
            P(),
            P(),
            P(),
        ),
        out_specs=(P(None, "col", "row"), P(None, "col", "row")),
        check_vma=False,
    )
```

```python
import functools
import math

import jax
import jax.numpy as jnp
import numpy as np
import ml_dtypes
from jax import lax
from jax.experimental import pallas as pl
from jax.experimental.pallas import tpu as pltpu
from jax.sharding import PartitionSpec as P

K = 256

wave_base = 0.23
source_gain = 8.0
norm_eps = 1e-06

MESH = pl.DeviceIdType.MESH
F32 = jnp.float32
BF16 = jnp.bfloat16
LINES = 16
SLABS = 16
PIECE = 256


def forward_tables(tile_cols, kept_modes, grid_cols):
    positions = np.arange(tile_cols, dtype=np.int64)
    mode_index = np.arange(kept_modes, dtype=np.int64)
    angles = (positions[:, None] * mode_index[None, :] % grid_cols) * (2.0 * math.pi / grid_cols)
    scale = 1.0 / math.sqrt(grid_cols)
    table = np.concatenate([np.cos(angles), -np.sin(angles)], axis=1) * scale
    high = table.astype(np.float32).astype(ml_dtypes.bfloat16)
    low = (table - high.astype(np.float64)).astype(np.float32).astype(ml_dtypes.bfloat16)
    return high, low


def back_tables(tile_cols, kept_modes, grid_cols):
    odd = 2 * np.arange(tile_cols // 2, dtype=np.int64) + 1
    mode_index = np.arange(kept_modes, dtype=np.int64)
    angles = (mode_index[:, None] * odd[None, :] % (2 * grid_cols)) * (math.pi / grid_cols)
    scale = math.sqrt(0.5 / grid_cols)
    table = np.stack([np.cos(angles), -np.sin(angles)]) * scale
    return table.astype(np.float32).astype(ml_dtypes.bfloat16)


def phase_table(row_count, tile_cols, kept_modes):
    grid_cols = row_count * tile_cols
    first = 2 * tile_cols * np.arange(row_count, dtype=np.int64)
    mode_index = np.arange(kept_modes, dtype=np.int64)
    parts = []
    for place in (first, first + tile_cols - 1):
        angles = (place[:, None] * mode_index[None, :] % (2 * grid_cols)) * (math.pi / grid_cols)
        parts += [np.cos(angles), np.sin(angles)]
    table = np.concatenate(parts, axis=1).astype(np.float32)
    return np.ascontiguousarray(np.broadcast_to(table[:, None, :], (row_count, 8, 4 * kept_modes)))


def split(x):
    high = x.astype(BF16)
    return high, (x - high.astype(F32)).astype(BF16)


def three_way(x):
    high, low = split(x)
    return high, low, (x - high.astype(F32) - low.astype(F32)).astype(BF16)


def scaled_gelu(z):
    return z + z * lax.erf(z)


def cmul(a, b):
    return a[0] * b[0] - a[1] * b[1], a[0] * b[1] + a[1] * b[0]


def conj_cmul(a, b):
    return a[0] * b[0] + a[1] * b[1], a[0] * b[1] - a[1] * b[0]


def small_solve(beta, a, b, c, d, e):
    gram_first = a[0] * a[0] + a[1] * a[1] + c * c
    gram_second = b[0] * b[0] + b[1] * b[1] + d[0] * d[0] + d[1] * d[1] + e * e
    cross = conj_cmul(a, b)
    cross = (cross[0] + c * d[0], cross[1] + c * d[1])
    ad = cmul(a, d)
    minor = (ad[0] - b[0] * c, ad[1] - b[1] * c)
    determinant = (
        minor[0] * minor[0]
        + minor[1] * minor[1]
        + (a[0] * a[0] + a[1] * a[1]) * e * e
        + c * c * e * e
    )
    first = (beta * a[0], -beta * a[1])
    second = (beta * b[0], -beta * b[1])
    t = cmul(cross, second)
    y0 = ((gram_second * first[0] - t[0]) / determinant, (gram_second * first[1] - t[1]) / determinant)
    t = conj_cmul(cross, first)
    y1 = ((gram_first * second[0] - t[0]) / determinant, (gram_first * second[1] - t[1]) / determinant)
    return y0, y1


def far_first(axis, me, count):
    inner = 2 if axis == "col" else 4
    if count % inner or count == inner:
        return [lax.rem(me + d, count) for d in range(1, count)]
    outer = count // inner

    def hops(step):
        a, b = step
        along = min(b, inner - b) if axis == "row" else 0.5 * b
        return min(a, outer - a) + along

    steps = [(a, b) for a in range(outer) for b in range(inner) if a or b]
    steps.sort(key=hops, reverse=True)
    return [
        lax.rem(me // inner + a, outer) * inner + lax.rem(lax.rem(me, inner) + b, inner)
        for a, b in steps
    ]


def kernel(
    row_count,
    col_count,
    kept,
    forcing_in,
    medium_in,
    mask_in,
    source_rows,
    source_cols,
    refraction,
    lift_scalars,
    bias_scalars,
    lift_weight,
    lift_bias,
    spectral_weight,
    point_weight,
    layer_bias,
    project_weight,
    table_high,
    table_low,
    table_back,
    phases,
    solution_ref,
    residual_ref,
    forcing,
    medium,
    mask,
    fwd_high,
    fwd_low,
    phase,
    weights,
    mode_map,
    project_map,
    wave_ref,
    feature_ref,
    right_ref,
    even_cols,
    odd_cols,
    mixed,
    fixed,
    modes,
    high,
    low,
    send_feat,
    got_feat,
    all_feat,
    send_wave,
    got_wave,
    all_wave,
    got_scal,
    col_scal,
    before,
    ext,
    applied,
    basis,
    half_ref,
    table_sems,
    halo_send,
    halo_recv,
    send_sems,
    recv_sems,
):
    lines, columns = mask.shape
    channels = point_weight.shape[0]
    groups = lines // LINES
    double = 2 * kept
    wide = SLABS * LINES
    half = columns // 2
    row = lax.axis_index("row")
    col = lax.axis_index("col")
    grid_scale = math.sqrt(lines * col_count * columns * row_count)

    first_load = 4 + 2 * groups
    media_copies = [
        pltpu.make_async_copy(medium_in, medium, table_sems.at[first_load]),
        pltpu.make_async_copy(mask_in, mask, table_sems.at[first_load + 1]),
    ]
    forcing_copy = pltpu.make_async_copy(forcing_in, forcing, table_sems.at[first_load + 2])
    table_copies = [
        pltpu.make_async_copy(table_high, fwd_high, table_sems.at[0]),
        pltpu.make_async_copy(table_low, fwd_low, table_sems.at[1]),
        pltpu.make_async_copy(phases.at[row], phase, table_sems.at[2]),
    ]
    back_copies = [
        copy
        for g in range(groups)
        for copy in (
            pltpu.make_async_copy(table_back.at[0], even_cols.at[g, pl.ds(0, kept)], table_sems.at[4 + 2 * g]),
            pltpu.make_async_copy(table_back.at[1], odd_cols.at[g, pl.ds(wide, kept)], table_sems.at[5 + 2 * g]),
        )
    ]
    weight_copy = pltpu.make_async_copy(spectral_weight, weights, table_sems.at[3])
    for copy in [*media_copies, *table_copies, forcing_copy, weight_copy, *back_copies]:
        copy.start()

    barrier = pltpu.get_barrier_semaphore()
    greeted = 0
    for d in range(1, row_count):
        pl.semaphore_signal(
            barrier, inc=1, device_id={"row": lax.rem(row + d, row_count)}, device_id_type=MESH
        )
        greeted += 1
    for d in range(1, col_count):
        pl.semaphore_signal(
            barrier, inc=1, device_id={"col": lax.rem(col + d, col_count)}, device_id_type=MESH
        )
        greeted += 1
    for dr in (1, row_count - 1):
        for dc in (1, col_count - 1):
            pl.semaphore_signal(
                barrier,
                inc=1,
                device_id={
                    "row": lax.rem(row + dr, row_count),
                    "col": lax.rem(col + dc, col_count),
                },
                device_id_type=MESH,
            )
            greeted += 1

    def spread(source, target, index, axis, me, count):
        for there in far_first(axis, me, count):
            pltpu.make_async_remote_copy(
                src_ref=source(there),
                dst_ref=target.at[me],
                send_sem=send_sems.at[index],
                recv_sem=recv_sems.at[index],
                device_id={axis: there},
                device_id_type=MESH,
            ).start()

    def arrived(target, index, count, sems):
        whole = target.at[pl.ds(0, count - 1)]
        pltpu.make_async_copy(whole, whole, sems.at[index]).wait()

    def forward(kind, out):
        spectrum = (
            jnp.dot(high[kind], fwd_high[...], preferred_element_type=F32)
            + jnp.dot(high[kind], fwd_low[...], preferred_element_type=F32)
            + jnp.dot(low[kind], fwd_high[...], preferred_element_type=F32)
        )
        cosine, sine = phase[0:1, :kept], phase[0:1, kept:double]
        re, im = spectrum[:, :kept], spectrum[:, kept:]
        out[:, :, 0:kept] = (re * cosine + im * sine).reshape(row_count, 8, kept)
        out[:, :, kept:double] = (im * cosine - re * sine).reshape(row_count, 8, kept)

    def unrotated(both):
        cosine, sine = phase[0:1, double : double + kept], phase[0:1, double + kept :]
        re, im = both[:, :kept], both[:, kept:]
        return re * cosine - im * sine, im * cosine + re * sine

    flip = jnp.where(
        lax.broadcasted_iota(jnp.int32, (128, 128), 0)
        + lax.broadcasted_iota(jnp.int32, (128, 128), 1)
        == 127,
        1.0,
        0.0,
    ).astype(BF16)

    def reversed_lanes(x):
        height, blocks = x.shape[0], x.shape[1] // 128
        parts = [
            part[:, 128 * i : 128 * i + 128] for part in three_way(x) for i in reversed(range(blocks))
        ]
        turned = jnp.dot(jnp.concatenate(parts, axis=0), flip, preferred_element_type=F32)
        pieces = turned.reshape(3, blocks, height, 128)
        total = pieces[0] + pieces[1] + pieces[2]
        return jnp.concatenate([total[i] for i in range(blocks)], axis=1)

    def slab(g, j, even, odd):
        even_cols[g, kept + LINES * j : kept + LINES * (j + 1), :] = even
        odd_cols[g, LINES * j : LINES * (j + 1), :] = odd

    def halves(value):
        right, left = value[:, half:], reversed_lanes(value[:, :half])
        return 0.5 * (right + left), 0.5 * (right - left)

    def field_slabs(g, j, even, odd):
        even, odd = split(even), split(odd)
        slab(g, j, even[0], odd[0])
        slab(g, j + 1, even[1], odd[1])
        slab(g, j + 2, even[0], odd[0])

    def keep_halves(which, source):
        for g in range(groups):
            for p in range(2):
                even, odd = halves(source[p, rows_of(g), :])
                half_ref[which, 0, p, rows_of(g), :] = even
                half_ref[which, 1, p, rows_of(g), :] = odd

    def rows_of(g):
        return slice(LINES * g, LINES * (g + 1))

    def folded(x):
        total = jnp.zeros((8, 128), F32)
        for i in range(x.shape[0] // 8):
            for j in range(x.shape[1] // 128):
                total = total + x[8 * i : 8 * i + 8, 128 * j : 128 * j + 128]
        return total

    def scalar_tile(parts):
        place = lax.broadcasted_iota(jnp.int32, (8, 128), 0)
        tile = jnp.zeros((8, 128), F32)
        for i, part in enumerate(parts):
            tile = jnp.where(place == i, jnp.sum(part, axis=0, keepdims=True), tile)
        return tile

    for copy in media_copies:
        copy.wait()
    for g in range(groups):
        lines_of = rows_of(g)
        kind = medium[lines_of, :]
        refractive = jnp.zeros((LINES, columns), F32)
        for level in range(refraction.shape[0]):
            refractive = jnp.where(kind == level, refraction[level], refractive)
        damping = 0.1 + mask[lines_of, :].astype(F32)
        scaled = wave_base * refractive
        wave_ref[lines_of, :] = scaled * scaled
        feature_ref[0, lines_of, :] = refractive
        feature_ref[1, lines_of, :] = damping
        for i, feature in enumerate((refractive, damping)):
            top, rest = split(feature)
            place = slice(lines * i + LINES * g, lines * i + LINES * (g + 1))
            high[0, place, :] = top
            low[0, place, :] = rest
    for copy in table_copies:
        copy.wait()
    forward(0, send_feat)
    pl.semaphore_wait(barrier, greeted)
    spread(lambda there: send_feat.at[there], got_feat, 0, "row", row, row_count)

    sources = source_rows.shape[0]
    place = lax.broadcasted_iota(jnp.int32, (sources, 128), 0)
    col_of = jnp.zeros((sources, 128), jnp.int32)
    for i in range(sources):
        col_of = jnp.where(place == i, source_cols[i] - columns * row, col_of)
    lane = lax.broadcasted_iota(jnp.int32, (sources, 128), 1)
    col_hits = jnp.concatenate(
        [jnp.where(col_of == lane + 128 * j, 1.0, 0.0) for j in range(columns // 128)], axis=1
    ).astype(BF16)
    place = lax.broadcasted_iota(jnp.int32, (lines, sources), 1)
    row_of = jnp.zeros((lines, sources), jnp.int32)
    for i in range(sources):
        row_of = jnp.where(place == i, source_rows[i] - lines * col, row_of)
    line_hits = jnp.where(
        row_of == lax.broadcasted_iota(jnp.int32, (lines, sources), 0), 1.0, 0.0
    ).astype(BF16)
    source_count = jnp.dot(line_hits, col_hits, preferred_element_type=F32)
    square = jnp.zeros((8, 128), F32)
    forcing_copy.wait()
    for g in range(groups):
        lines_of = rows_of(g)
        for p in range(2):
            field = forcing[p, lines_of, :]
            if p == 0:
                field = field + source_gain * source_count[lines_of, :]
            right_ref[p, lines_of, :] = field
            square = square + folded(field * field)
            top, rest = split(field)
            high[1, p * lines + LINES * g : p * lines + LINES * (g + 1), :] = top
            low[1, p * lines + LINES * g : p * lines + LINES * (g + 1), :] = rest
    def send_modes(step, tile):
        forward(1, send_wave.at[step])
        for r in range(row_count):
            send_wave[step, r, :, double:] = tile
        spread(
            lambda there: send_wave.at[step, there], got_wave.at[step], 2 + 3 * step, "row", row, row_count
        )

    send_modes(0, scalar_tile([square]))

    mode_of = lax.broadcasted_iota(jnp.int32, (1, 128), 1)

    def fold(ob, kc):
        outs, some = pl.ds(16 * ob, 16), pl.ds(128 * kc, 128)
        used = 5 if kc == 0 else 4
        twice = jnp.where(mode_of == 0, 1.0, 2.0) if kc == 0 else 2.0
        both = []
        for part in range(2):

            def one_channel(c, sums):
                weight = weights[part, c, outs, some].astype(F32)
                factors = [lift_scalars[g, c] for g in range(4)] + [bias_scalars[c]]
                return tuple(x + f * weight for x, f in zip(sums, factors))

            both.append(
                lax.fori_loop(
                    0, channels, one_channel, (jnp.zeros((16, 128), F32),) * used, unroll=8
                )
            )
        for g in range(4):
            re, im = both[0][g] * twice, both[1][g] * twice
            mode_map[0, g, outs, some] = re
            mode_map[1, g, outs, some] = re + im
            mode_map[2, g, outs, some] = im - re
        anchor = jnp.where(mode_of == 0, math.sqrt(columns * row_count), 0.0)
        for part in range(2):
            mode_map[part, 4, outs, some] = (
                both[part][4] * anchor if kc == 0 else jnp.zeros((16, 128), F32)
            )

    def reduced(got, source):
        got[row] = source[row]
        total = got[0]
        for r in range(1, row_count):
            total = total + got[r]
        return total

    blocks = [(ob, kc) for ob in range(channels // 16) for kc in range(kept // 128)]
    weight_copy.wait()
    for block in blocks[: len(blocks) // 2]:
        fold(*block)
    arrived(got_feat, 0, row_count, recv_sems)
    all_feat[row] = reduced(got_feat, send_feat)
    spread(lambda there: all_feat.at[row], all_feat, 1, "row", row, row_count)

    def wave_reduce(step):
        index = 2 + 3 * step
        arrived(got_wave.at[step], index, row_count, recv_sems)
        total = reduced(got_wave.at[step], send_wave.at[step])
        all_wave[step, row] = total[:, :double]
        spread(
            lambda there: all_wave.at[step, row], all_wave.at[step], index + 1, "row", row, row_count
        )
        col_scal[step, col] = total[:, double:]
        spread(
            lambda there: col_scal.at[step, col], col_scal.at[step], index + 2, "col", col, col_count
        )

    def col_total(step):
        arrived(col_scal.at[step], 4 + 3 * step, col_count, recv_sems)
        total = col_scal[step, 0]
        for r in range(1, col_count):
            total = total + col_scal[step, r]
        return jnp.sum(total, axis=1, keepdims=True)

    def mix_lines(first, count, kc, ob, channels_in, bias, source, store):
        low_k, high_k = pl.ds(128 * kc, 128), pl.ds(kept + 128 * kc, 128)
        store_k = pl.ds(store.shape[2] - kept + 128 * kc, 128)
        outs = pl.ds(16 * ob, 16)
        maps = [tuple(mode_map[i, g, outs, low_k] for i in range(3)) for g in channels_in]
        start = (mode_map[0, 4, outs, low_k], mode_map[1, 4, outs, low_k]) if bias else None
        for block in range(count // 8):
            top = first + 8 * block
            parts = [
                (modes[g, pl.ds(top, 8), low_k], modes[g, pl.ds(top, 8), high_k]) for g in channels_in
            ]
            parts = [(mode_re, mode_im, mode_re + mode_im) for mode_re, mode_im in parts]
            for i in range(8):
                line = top + i
                if bias:
                    re, im = start
                else:
                    re, im = source[line, outs, low_k], source[line, outs, high_k]
                shared = None
                for (mode_re, mode_im, mode_sum), (map_re, map_sum, map_less) in zip(parts, maps):
                    product = map_re * mode_sum[i : i + 1]
                    shared = product if shared is None else shared + product
                    re = re - map_sum * mode_im[i : i + 1]
                    im = im + map_less * mode_re[i : i + 1]
                re, im = re + shared, im + shared
                store[line, outs, low_k] = re.astype(store.dtype)
                store[line, outs, store_k] = im.astype(store.dtype)

    def mix_fixed():
        for kc in range(kept // 128):
            for ob in range(channels // 16):

                def eight_lines(block, carry):
                    first = pl.multiple_of(8 * block, 8)
                    mix_lines(first, 8, kc, ob, (2, 3), True, None, fixed)
                    return carry

                lax.fori_loop(0, lines // 8, eight_lines, 0)

    def mix_group(g):
        for kc in range(kept // 128):
            for ob in range(channels // 16):
                mix_lines(LINES * g, LINES, kc, ob, (0, 1), False, fixed, mixed)

    def layer(step):
        outer = half // PIECE - 1
        edges = [(g, outer) for g in range(groups)]
        ends = [(g, n) for g in sorted({0, groups - 1}) for n in range(outer)]
        inside = [(g, n) for g in range(1, groups - 1) for n in range(outer)]
        order = edges + ends + inside

        def multiply(g, n, slot):
            left = mixed[LINES * g : LINES * (g + 1)].reshape(LINES * channels, double + wide)
            piece = slice(PIECE * n, PIECE * (n + 1))
            before[slot, 0] = jnp.dot(
                left[:, : kept + wide], even_cols[g, :, piece], preferred_element_type=F32
            )
            before[slot, 1] = jnp.dot(
                left[:, kept:], odd_cols[g, :, piece], preferred_element_type=F32
            )

        def finish(g, n, slot):
            lines_of = slice(8 + LINES * g, 8 + LINES * (g + 1))
            even, odd = before[slot, 0], before[slot, 1]
            for side in range(2):
                active = scaled_gelu(even + odd if side else even - odd).astype(BF16)
                out = jnp.dot(project_map[...], active, preferred_element_type=F32)
                out = out * math.sqrt(0.5)
                if side:
                    first = 128 + half + PIECE * n
                else:
                    first = 128 + half - PIECE * (n + 1)
                    out = reversed_lanes(out)
                place = slice(first, first + PIECE)
                ext[step, 0, lines_of, place] = out[:LINES]
                ext[step, 1, lines_of, place] = out[LINES:]

        mix_group(0)
        for t in range(len(order) + 1):
            if t < len(order):
                g, n = order[t]
                multiply(g, n, t % 2)
                if t < len(edges) and g + 1 < groups:
                    mix_group(g + 1)
            if t > 0:
                finish(*order[t - 1], (t - 1) % 2)
            if t == groups // 2:
                for copy in halo_copies(step, (0, 1)):
                    copy.start()
            if t == len(edges):
                for copy in halo_copies(step, (2, 3, 4, 5, 6, 7)):
                    copy.start()
            if t == len(edges) + len(ends):
                for copy in halo_copies(step, (8, 9)):
                    copy.start()

    def halo_copies(step, wanted):
        tall, across_all = pl.ds(8, lines), pl.ds(128, columns)
        line_ends = {
            1: (pl.ds(7 + lines, 1), pl.ds(7, 1)),
            -1: (pl.ds(8, 1), pl.ds(8 + lines, 1)),
            0: (tall, tall),
        }
        col_ends = {
            1: (pl.ds(columns, 128), pl.ds(0, 128)),
            -1: (pl.ds(128, 128), pl.ds(128 + columns, 128)),
            0: (across_all, across_all),
        }
        copies = []
        moves = [(1, 0), (-1, 0), (1, 0), (-1, 0), (1, 1), (1, -1), (-1, 1), (-1, -1), (0, 1), (0, -1)]
        for i in wanted:
            dr, dc = moves[i]
            here_l, there_l = line_ends[dc]
            if i < 4:
                here_l = there_l = pl.ds(8 + (i // 2) * (lines // 2), lines // 2)
            here_c, there_c = col_ends[dr]
            copies.append(
                pltpu.make_async_remote_copy(
                    src_ref=ext.at[step, :, here_l, here_c],
                    dst_ref=ext.at[step, :, there_l, there_c],
                    send_sem=halo_send.at[step, i],
                    recv_sem=halo_recv.at[step, i],
                    device_id={
                        "row": lax.rem(row + dr + row_count, row_count),
                        "col": lax.rem(col + dc + col_count, col_count),
                    },
                    device_id_type=MESH,
                )
            )
        return copies

    def side_halos(step):
        for copy in halo_copies(step, range(8)):
            copy.wait()
        view = ext.at[step]

        @pl.when(row == 0)
        def _():
            view[:, :, 0:128] = jnp.zeros((2, lines + 16, 128), F32)

        @pl.when(row == row_count - 1)
        def _():
            view[:, :, 128 + columns :] = jnp.zeros((2, lines + 16, 128), F32)

    def line_halos(step):
        for copy in halo_copies(step, (8, 9)):
            copy.wait()
        view = ext.at[step]

        @pl.when(col == 0)
        def _():
            view[:, 0:8, :] = jnp.zeros((2, 8, columns + 256), F32)

        @pl.when(col == col_count - 1)
        def _():
            view[:, 8 + lines :, :] = jnp.zeros((2, 8, columns + 256), F32)

    def operated(step, each):
        side_halos(step)
        for g in range(1, groups - 1):
            each(g)
        line_halos(step)
        for g in sorted({0, groups - 1}):
            each(g)

    def operate(step, g):
        laps, fields = [], []
        for p in range(2):
            first = 8 + LINES * g
            beside = (
                ext[step, p, first - 1 : first - 1 + LINES, :]
                + ext[step, p, first + 1 : first + 1 + LINES, :]
            )
            centre = ext[step, p, first : first + LINES, :]
            both = 4.0 * centre + beside
            width = columns + 256
            around = pltpu.roll(both, 1, 1) + pltpu.roll(both, width - 1, 1)
            total = (4.0 * beside - 20.0 * centre + around) * (1.0 / 6.0)
            laps.append(total[:, 128 : 128 + columns])
            fields.append(centre[:, 128 : 128 + columns])
        wave, damping = wave_ref[rows_of(g), :], feature_ref[1, rows_of(g), :]
        real = -laps[0] - wave * (fields[0] + damping * fields[1])
        imag = -laps[1] - wave * (fields[1] - damping * fields[0])
        return real, imag

    def pair(first, second):
        return (
            folded(first[0] * second[0] + first[1] * second[1]),
            folded(first[0] * second[1] - first[1] * second[0]),
        )

    def add(a, b):
        return [x + y for x, y in zip(a, b)]

    for block in blocks[len(blocks) // 2 :]:
        fold(*block)
    wave_reduce(0)

    lift = jnp.concatenate(
        [lift_weight[...], lift_bias[...], jnp.zeros((3, channels), F32)], axis=0
    )
    lift_parts = three_way(lift)
    point = jnp.zeros((8, channels), F32)
    for part in lift_parts:
        point = point + jnp.dot(part, point_weight[...], preferred_element_type=F32)
    channel_row = lax.broadcasted_iota(jnp.int32, (8, channels), 0)
    point = (point + jnp.where(channel_row == 4, layer_bias[...], 0.0)) * math.sqrt(0.5)
    top, rest = split(point)
    from_row = lax.broadcasted_iota(jnp.int32, (8, wide), 0)
    slab_of = lax.broadcasted_iota(jnp.int32, (8, wide), 1) // LINES
    first_slab = 3 * from_row
    pick_top = ((slab_of == first_slab) | ((slab_of == first_slab + 1) & (from_row < 4))) & (from_row < 5)
    pick_rest = ((slab_of == first_slab + 2) & (from_row < 4)) | ((slab_of == 13) & (from_row == 4))
    over_rows = (((0,), (0,)), ((), ()))
    spread_out = lax.dot_general(
        top.astype(F32), jnp.where(pick_top, 1.0, 0.0), over_rows, preferred_element_type=F32
    ) + lax.dot_general(
        rest.astype(F32), jnp.where(pick_rest, 1.0, 0.0), over_rows, preferred_element_type=F32
    )
    line_of = lax.broadcasted_iota(jnp.int32, (channels, wide), 1) % LINES
    for i in range(LINES):
        masked = jnp.where(line_of == i, spread_out, 0.0).astype(BF16)
        for g in range(groups):
            mixed[LINES * g + i, :, kept : kept + wide] = masked
    all_rows = LINES * channels
    tiles = jnp.where(
        lax.broadcasted_iota(jnp.int32, (channels, all_rows), 0)
        == lax.broadcasted_iota(jnp.int32, (channels, all_rows), 1) % channels,
        1.0,
        0.0,
    )
    across = lax.dot_general(
        project_weight[...].astype(F32), tiles, (((1,), (0,)), ((), ())), preferred_element_type=F32
    )
    own_line = (
        lax.broadcasted_iota(jnp.int32, (LINES, all_rows), 0)
        == lax.broadcasted_iota(jnp.int32, (LINES, all_rows), 1) // channels
    )
    for p in range(2):
        project_map[LINES * p : LINES * (p + 1), :] = jnp.where(
            own_line, across[p : p + 1, :], 0.0
        ).astype(BF16)

    for g in range(groups):
        ones = jnp.ones((LINES, half), BF16)
        zeros = jnp.zeros_like(ones)
        slab(g, 12, ones, zeros)
        slab(g, 13, ones, zeros)
        slab(g, 14, zeros, zeros)
        slab(g, 15, zeros, zeros)
        for i in range(2):
            field_slabs(g, 6 + 3 * i, *halves(feature_ref[i, rows_of(g), :]))
    keep_halves(0, right_ref)

    arrived(all_feat, 1, row_count, recv_sems)
    re, im = unrotated(all_feat[...].reshape(2 * lines, double))
    for g in range(2):
        modes[2 + g, :, :kept] = re[g * lines : (g + 1) * lines]
        modes[2 + g, :, kept:] = im[g * lines : (g + 1) * lines]
    mix_fixed()
    for copy in back_copies:
        copy.wait()

    total_square = col_total(0)[0:1, :]
    beta = jnp.sqrt(total_square + norm_eps)
    inverse_beta = 1.0 / beta
    for g in range(groups):
        for p in range(2):
            even, odd = (
                half_ref[0, i, p, rows_of(g), :] * (grid_scale * inverse_beta) for i in range(2)
            )
            field_slabs(g, 3 * p, even, odd)
    arrived(all_wave.at[0], 3, row_count, recv_sems)
    re, im = unrotated(all_wave[0].reshape(2 * lines, double))
    for p in range(2):
        modes[p, :, :kept] = re[p * lines : (p + 1) * lines] * (grid_scale * inverse_beta)
        modes[p, :, kept:] = im[p * lines : (p + 1) * lines] * (grid_scale * inverse_beta)
    layer(0)
    sums = [jnp.zeros((8, 128), F32)] * 3

    def first_applied(g):
        lines_of = rows_of(g)
        result = operate(0, g)
        for p in range(2):
            applied[0, p, lines_of, :] = result[p]
            top, rest = split(result[p])
            high[1, p * lines + LINES * g : p * lines + LINES * (g + 1), :] = top
            low[1, p * lines + LINES * g : p * lines + LINES * (g + 1), :] = rest
        start = (right_ref[0, lines_of, :], right_ref[1, lines_of, :])
        square = folded(result[0] * result[0] + result[1] * result[1])
        sums[:] = add(sums, (*pair(start, result), square))

    operated(0, first_applied)
    send_modes(1, scalar_tile(sums))
    keep_halves(1, applied.at[0])
    wave_reduce(1)
    totals = col_total(1)
    unit_square = total_square * inverse_beta * inverse_beta
    a = (totals[0:1, :] * inverse_beta, totals[1:2, :] * inverse_beta)
    a_square = a[0] * a[0] + a[1] * a[1]
    rest_square = jnp.maximum(totals[2:3, :] - a_square * (2.0 - unit_square), 0.0)
    c = jnp.sqrt(rest_square + norm_eps)
    inverse_c = 1.0 / c
    a_over = (a[0] * inverse_beta, a[1] * inverse_beta)

    def next_vector(w, v):
        scaled = cmul(a_over, v)
        return (w[0] - scaled[0]) * inverse_c, (w[1] - scaled[1]) * inverse_c

    for g in range(groups):
        lines_of = rows_of(g)
        vector = next_vector(
            (applied[0, 0, lines_of, :], applied[0, 1, lines_of, :]),
            (right_ref[0, lines_of, :], right_ref[1, lines_of, :]),
        )
        for p in range(2):
            basis[p, lines_of, :] = vector[p]
        even, odd = (
            next_vector(
                [half_ref[1, i, p, lines_of, :] for p in range(2)],
                [half_ref[0, i, p, lines_of, :] for p in range(2)],
            )
            for i in range(2)
        )
        for p in range(2):
            field_slabs(g, 3 * p, even[p] * grid_scale, odd[p] * grid_scale)
    arrived(all_wave.at[1], 6, row_count, recv_sems)
    old, new = (all_wave[i].reshape(2 * lines, double) for i in range(2))
    planes = next_vector((new[:lines], new[lines:]), (old[:lines], old[lines:]))
    for p in range(2):
        re, im = unrotated(planes[p])
        modes[p, :, :kept] = re * grid_scale
        modes[p, :, kept:] = im * grid_scale
    layer(1)
    sums = [jnp.zeros((8, 128), F32)] * 5

    def second_applied(g):
        lines_of = rows_of(g)
        result = operate(1, g)
        for p in range(2):
            applied[1, p, lines_of, :] = result[p]
        start = (right_ref[0, lines_of, :], right_ref[1, lines_of, :])
        vector = (basis[0, lines_of, :], basis[1, lines_of, :])
        square = folded(result[0] * result[0] + result[1] * result[1])
        sums[:] = add(sums, (*pair(start, result), *pair(vector, result), square))

    operated(1, second_applied)
    got_scal[row] = scalar_tile(sums)
    spread(lambda there: got_scal.at[row], got_scal, 8, "row", row, row_count)
    arrived(got_scal, 8, row_count, recv_sems)
    total = got_scal[0]
    for r in range(1, row_count):
        total = total + got_scal[r]
    col_scal[2, col] = total
    spread(lambda there: col_scal.at[2, col], col_scal.at[2], 9, "col", col, col_count)
    arrived(col_scal.at[2], 9, col_count, recv_sems)
    total = col_scal[2, 0]
    for r in range(1, col_count):
        total = total + col_scal[2, r]
    totals = jnp.sum(total, axis=1, keepdims=True)
    b = (totals[0:1, :] * inverse_beta, totals[1:2, :] * inverse_beta)
    d = (totals[2:3, :], totals[3:4, :])
    b_square = b[0] * b[0] + b[1] * b[1]
    d_square = d[0] * d[0] + d[1] * d[1]
    second_square = rest_square * inverse_c * inverse_c
    overlap = (norm_eps * inverse_beta * inverse_beta) * inverse_c
    between = conj_cmul(b, d)
    between = between[0] * a[0] - between[1] * a[1]
    last_square = (
        totals[4:5, :]
        - b_square * (2.0 - unit_square)
        - d_square * (2.0 - second_square)
        + 2.0 * overlap * between
    )
    e = jnp.sqrt(jnp.maximum(last_square, 0.0) + norm_eps)
    y0, y1 = small_solve(beta, a, b, c, d, e)
    for g in range(groups):
        lines_of = rows_of(g)
        inner = slice(8 + LINES * g, 8 + LINES * (g + 1))
        z0, z1, w0, w1 = (
            [ext[0, p, inner, 128 : 128 + columns] for p in range(2)],
            [ext[1, p, inner, 128 : 128 + columns] for p in range(2)],
            [applied[0, p, lines_of, :] for p in range(2)],
            [applied[1, p, lines_of, :] for p in range(2)],
        )
        z0, z1, w0, w1 = cmul(y0, z0), cmul(y1, z1), cmul(y0, w0), cmul(y1, w1)
        for p in range(2):
            solution_ref[p, lines_of, :] = z0[p] + z1[p]
            residual_ref[p, lines_of, :] = right_ref[p, lines_of, :] - w0[p] - w1[p]

    arrived(got_feat, 0, row_count, send_sems)
    arrived(all_feat, 1, row_count, send_sems)
    for step in range(2):
        arrived(got_wave.at[step], 2 + 3 * step, row_count, send_sems)
        arrived(all_wave.at[step], 3 + 3 * step, row_count, send_sems)
        arrived(col_scal.at[step], 4 + 3 * step, col_count, send_sems)
    arrived(got_scal, 8, row_count, send_sems)
    arrived(col_scal.at[2], 9, col_count, send_sems)


def deliver(solution_in, residual_in, solution_out, residual_out, sems):
    copies = [
        pltpu.make_async_copy(solution_in, solution_out, sems.at[0]),
        pltpu.make_async_copy(residual_in, residual_out, sems.at[1]),
    ]
    for copy in copies:
        copy.start()
    for copy in copies:
        copy.wait()


def shards(
    row_count,
    col_count,
    kept,
    forcing,
    medium_index,
    absorbing_mask,
    source_rows,
    source_cols,
    refraction,
    lift_weight,
    lift_bias,
    spectral_weight,
    point_weight,
    layer_bias,
    project_weight,
):
    _, lines, columns = forcing.shape
    channels = point_weight.shape[0]
    grid_cols = columns * row_count
    groups = lines // LINES
    double = 2 * kept
    assert row_count * 8 == 2 * lines

    table_high, table_low = forward_tables(columns, kept, grid_cols)
    table_back = back_tables(columns, kept, grid_cols)
    phases = phase_table(row_count, columns, kept)

    field = jax.ShapeDtypeStruct((2, lines, columns), F32)
    vmem = pl.BlockSpec(memory_space=pltpu.VMEM)
    smem = pl.BlockSpec(memory_space=pltpu.SMEM)
    hbm = pl.BlockSpec(memory_space=pl.ANY)
    dma = pltpu.SemaphoreType.DMA
    results = pl.pallas_call(
        functools.partial(kernel, row_count, col_count, kept),
        out_shape=(pltpu.VMEM(field.shape, F32), pltpu.VMEM(field.shape, F32)),
        in_specs=[hbm] * 3 + [smem] * 5 + [vmem] * 2 + [hbm] + [vmem] * 3 + [hbm] * 4,
        out_specs=(vmem, vmem),
        scratch_shapes=[
            pltpu.VMEM((2, lines, columns), F32),
            pltpu.VMEM((lines, columns), jnp.int32),
            pltpu.VMEM((lines, columns), jnp.int32),
            pltpu.VMEM((columns, double), BF16),
            pltpu.VMEM((columns, double), BF16),
            pltpu.VMEM((8, 2 * double), F32),
            pltpu.VMEM((2, channels, channels, kept), BF16),
            pltpu.VMEM((3, 5, channels, kept), F32),
            pltpu.VMEM((2 * LINES, LINES * channels), BF16),
            pltpu.VMEM((lines, columns), F32),
            pltpu.VMEM((2, lines, columns), F32),
            pltpu.VMEM((2, lines, columns), F32),
            pltpu.VMEM((groups, kept + SLABS * LINES, columns // 2), BF16),
            pltpu.VMEM((groups, kept + SLABS * LINES, columns // 2), BF16),
            pltpu.VMEM((lines, channels, double + SLABS * LINES), BF16),
            pltpu.VMEM((lines, channels, double), F32),
            pltpu.VMEM((4, lines, double), F32),
            pltpu.VMEM((2, 2 * lines, columns), BF16),
            pltpu.VMEM((2, 2 * lines, columns), BF16),
            pltpu.VMEM((row_count, 8, double), F32),
            pltpu.VMEM((row_count, 8, double), F32),
            pltpu.VMEM((row_count, 8, double), F32),
            pltpu.VMEM((2, row_count, 8, double + 128), F32),
            pltpu.VMEM((2, row_count, 8, double + 128), F32),
            pltpu.VMEM((2, row_count, 8, double), F32),
            pltpu.VMEM((row_count, 8, 128), F32),
            pltpu.VMEM((3, col_count, 8, 128), F32),
            pltpu.VMEM((2, 2, LINES * channels, PIECE), F32),
            pltpu.VMEM((2, 2, lines + 16, columns + 256), F32),
            pltpu.VMEM((2, 2, lines, columns), F32),
            pltpu.VMEM((2, lines, columns), F32),
            pltpu.VMEM((2, 2, 2, lines, columns // 2), F32),
            dma((7 + 2 * groups,)),
            dma((2, 10)),
            dma((2, 10)),
            dma((10,)),
            dma((10,)),
        ],
        compiler_params=pltpu.CompilerParams(
            collective_id=0, has_side_effects=True, vmem_limit_bytes=56 * 2**20
        ),
        name="krylov",
    )(
        forcing,
        medium_index,
        absorbing_mask,
        source_rows,
        source_cols,
        refraction,
        lift_weight,
        lift_bias,
        lift_weight,
        lift_bias.reshape(1, -1),
        spectral_weight.transpose(0, 2, 3, 1),
        point_weight,
        layer_bias.reshape(1, -1),
        project_weight.T,
        table_high,
        table_low,
        table_back,
        phases,
    )
    return pl.pallas_call(
        deliver,
        out_shape=(field, field),
        in_specs=[vmem] * 2,
        out_specs=[hbm] * 2,
        scratch_shapes=[dma((2,))],
        name="deliver",
    )(*[pltpu.with_memory_space_constraint(x, pltpu.VMEM) for x in results])


def solution(mesh):
    return jax.shard_map(
        functools.partial(shards, mesh.shape["row"], mesh.shape["col"], K),
        mesh=mesh,
        in_specs=(
            P(None, "col", "row"),
            P("col", "row"),
            P("col", "row"),
            P(),
            P(),
            P(),
            P(),
            P(),
            P(),
            P(),
            P(),
            P(),
        ),
        out_specs=(P(None, "col", "row"), P(None, "col", "row")),
        check_vma=False,
    )
```
